32 devices in a mesh: row: 4 (over y, x), col: 8 (over z, core).
Axes of the slice: x: 2, y: 2, z: 4, core: 2. Of those that a mesh axis runs over, the one named last changes fastest.
Arguments:
- three_center: bfloat16 [4096, 6144], P(('row', 'col')), may hold values from -6 to 6
- density: bfloat16 [4096, 4096], P('row', 'col'), may hold values from -0.1875 to 0.1875
- block_mask: int32 [128, 48], P(('row', 'col')), may hold values 0 or 1
- density_mask: int32 [128, 128], P('row', 'col'), may hold values 0 or 1
- basis_count: int32 [128], replicated, may hold values from 8 to 32
- ri_count: int32 [48], replicated, may hold values from 16 to 128
Outputs:
- contracted: bfloat16 [4096, 6144], P('row', 'col')
The draws below stay inside these ranges and needn't reach their ends.
All inputs are finite; a program needn't handle non-finite values. No bound on the sum of `block_mask` or of `density_mask` on one device may be relied on, other than what follows from the above.
Results may differ from the reference program's by a relative error of at most 0.001.
Values may be sent and summed in bfloat16 or wider, within the bound.
No kernel may reach another device: no remote copies, remote signals or barrier semaphores. Data moves between devices by JAX's collectives and lax.ppermute only.
A program may use at most 64 MiB of HBM per device.

```python
import jax
import jax.numpy as jnp

BW = 32
RW = 128
NA = 128
NB = 4096
NC = 48
NCOLS = 6144


def with_ends(result, own_key, least, largest):
    place = [jax.random.randint(jax.random.fold_in(own_key, axis), (), 0, length) for axis, length in enumerate(result.shape)]
    widest = result.shape.index(max(result.shape))
    neighbour = place[:widest] + [(place[widest] + 1) % result.shape[widest]] + place[widest + 1:]
    return result.at[tuple(place)].set(least).at[tuple(neighbour)].set(largest)


def shard_levels(stream_key, extent, cuts, low, high):
    gain = 1.0
    for position, parts in cuts:
        steps = jax.random.uniform(jax.random.fold_in(jax.random.fold_in(stream_key, 6), position), (parts,), jnp.float32, low / len(cuts), high / len(cuts))
        gain = gain * jnp.repeat(jnp.exp(steps), extent[position] // parts).reshape((-1,) + (1,) * (len(extent) - 1 - position))
    return gain


def bell_draw(rng, extent, deviation, reach, pieces=(), held_as=jnp.bfloat16):
    result = jax.random.normal(rng, extent, jnp.float32) * deviation
    if len(pieces) > 0:
        result = shard_levels(rng, extent, pieces, -0.22, 0.18) * result
    return jnp.clip(result, min=-reach, max=reach).astype(held_as)


def setup_inputs(seed: int = 0) -> dict:
    seeds = jax.random.split(jax.random.key(seed), 7)
    three_center = bell_draw(seeds[0], (NB, NCOLS), 1.0, 6.0, ((0, 32),))
    density = bell_draw(seeds[1], (NB, NB), (NB // 4) ** -0.5, 0.1875, ((0, 4), (1, 8)))
    block_mask = with_ends((jax.random.randint(seeds[2], (NA, NC), 0, 4) < 3).astype(jnp.int32), jax.random.fold_in(seeds[2], 1), 0, 1)
    density_mask = with_ends((jax.random.randint(seeds[3], (NA, NA), 0, 2) < 1).astype(jnp.int32), jax.random.fold_in(seeds[3], 1), 0, 1)
    basis_count = with_ends(jax.random.randint(seeds[4], (NA,), 8, BW + 1), jax.random.fold_in(seeds[4], 1), 8, BW).astype(jnp.int32)
    ri_count = with_ends(jax.random.randint(seeds[5], (NC,), RW // 8, RW + 1), jax.random.fold_in(seeds[5], 1), RW // 8, RW).astype(jnp.int32)
    return dict(three_center=three_center, density=density, block_mask=block_mask, density_mask=density_mask, basis_count=basis_count, ri_count=ri_count)


def reference(three_center, density, block_mask, density_mask, basis_count, ri_count):
    row_ok = jnp.arange(BW)[None, :] < basis_count[:, None]
    col_ok = jnp.arange(RW)[None, :] < ri_count[:, None]
    keep = row_ok[:, :, None, None] & col_ok[None, None, :, :] & (block_mask[:, None, :, None] > 0)
    screened = (three_center.reshape(NA, BW, NC, RW) * keep.astype(jnp.bfloat16)).reshape(NB, NCOLS)
    dkeep = row_ok[:, :, None, None] & row_ok[None, None, :, :] & (density_mask[:, None, :, None] > 0)
    dens = (density.reshape(NA, BW, NA, BW) * dkeep.astype(jnp.bfloat16)).reshape(NB, NB)
    return jnp.dot(dens, screened, preferred_element_type=jnp.float32).astype(jnp.bfloat16)
```

```python
import functools

import jax
import jax.numpy as jnp
from jax import lax
from jax.experimental import pallas as pl
from jax.experimental.pallas import tpu as pltpu
from jax.sharding import PartitionSpec as P

BW = 32
RW = 128
VMEM = 48 * 1024 * 1024


def screen_integrals(tc, own_count, ri_count, block_mask, ncols):
    rows, cols = tc.shape
    atoms = rows // BW
    wide = cols // ncols
    blocks = wide // RW

    def body(count_ref, ri_ref, mask_ref, x_ref, o_ref):
        dest = pl.program_id(0)
        row = lax.broadcasted_iota(jnp.int32, (BW, RW), 0)
        col = lax.broadcasted_iota(jnp.int32, (BW, RW), 1)
        for b in range(blocks):
            block = dest * blocks + b
            inside = col < ri_ref[block]
            for a in range(atoms):
                limit = jnp.where(mask_ref[a, block] > 0, count_ref[a], 0)
                at = (pl.ds(a * BW, BW), pl.ds(b * RW, RW))
                x = x_ref[at].astype(jnp.float32)
                o_ref[(0,) + at] = jnp.where(inside & (row < limit), x, 0.0).astype(jnp.bfloat16)

    smem = pl.BlockSpec(memory_space=pltpu.SMEM)
    return pl.pallas_call(
        body,
        out_shape=jax.ShapeDtypeStruct((ncols, rows, wide), jnp.bfloat16),
        grid=(ncols,),
        in_specs=[smem, smem, smem, pl.BlockSpec((rows, wide), lambda i: (0, i))],
        out_specs=pl.BlockSpec((1, rows, wide), lambda i: (i, 0, 0)),
        compiler_params=pltpu.CompilerParams(vmem_limit_bytes=VMEM),
        name="screen_integrals",
    )(own_count, ri_count, block_mask, tc)


def spread(values, size, axis):
    shape = (values.shape[0], size) if axis == 1 else (size, values.shape[1])
    long = lax.broadcasted_iota(jnp.int32, shape, axis) // BW
    short = lax.broadcasted_iota(jnp.int32, shape, 1 - axis)
    return (long == short).astype(jnp.bfloat16)


def screen_density(dens, lam_count, sum_count, mask):
    rows, cols = dens.shape
    lam_atoms, sum_atoms = mask.shape

    def body(lam_ref, sum_ref, mask_ref, x_ref, o_ref):
        def member(atoms, size, count, slot_axis):
            shape = (size, atoms) if slot_axis == 0 else (atoms, size)
            place = lax.broadcasted_iota(jnp.int32, shape, slot_axis)
            atom = lax.broadcasted_iota(jnp.int32, shape, 1 - slot_axis)
            first = atom * BW
            return jnp.where((place >= first) & (place < first + count), 1.0, 0.0).astype(jnp.bfloat16)

        left = member(lam_atoms, rows, lam_ref[...], 0)
        right = member(sum_atoms, cols, sum_ref[...], 1)
        keep = jnp.where(mask_ref[...] > 0, 1.0, 0.0).astype(jnp.bfloat16)
        keep = jnp.dot(left, keep, preferred_element_type=jnp.float32).astype(jnp.bfloat16)
        keep = jnp.dot(keep, right, preferred_element_type=jnp.float32)
        o_ref[...] = jnp.where(keep > 0.5, x_ref[...].astype(jnp.float32), 0.0).astype(jnp.bfloat16)

    return pl.pallas_call(
        body,
        out_shape=jax.ShapeDtypeStruct((rows, cols), jnp.bfloat16),
        compiler_params=pltpu.CompilerParams(vmem_limit_bytes=VMEM),
        name="screen_density",
    )(lam_count.reshape(1, -1), sum_count.reshape(-1, 1), mask, dens)


def contract(dens, integrals):
    parts, rows, depth = dens.shape
    cols = integrals.shape[2]

    def body(d_ref, s_ref, o_ref, total):
        step = pl.program_id(0)
        part = jnp.dot(d_ref[0], s_ref[0], preferred_element_type=jnp.float32)

        @pl.when(step == 0)
        def _():
            total[...] = part

        @pl.when(step > 0)
        def _():
            total[...] += part

        @pl.when(step == parts - 1)
        def _():
            o_ref[...] = total[...].astype(jnp.bfloat16)

    return pl.pallas_call(
        body,
        out_shape=jax.ShapeDtypeStruct((rows, cols), jnp.bfloat16),
        grid=(parts,),
        in_specs=[
            pl.BlockSpec((1, rows, depth), lambda i: (i, 0, 0)),
            pl.BlockSpec((1, depth, cols), lambda i: (i, 0, 0)),
        ],
        out_specs=pl.BlockSpec((rows, cols), lambda i: (0, 0)),
        scratch_shapes=[pltpu.VMEM((rows, cols), jnp.float32)],
        compiler_params=pltpu.CompilerParams(vmem_limit_bytes=VMEM),
        cost_estimate=pl.CostEstimate(
            flops=2 * parts * rows * depth * cols,
            bytes_accessed=2 * parts * depth * (rows + cols) + 2 * rows * cols,
            transcendentals=0,
        ),
        name="contract",
    )(dens, integrals)


def shards(three_center, density, block_mask, density_mask, basis_count, ri_count):
    ncols = lax.axis_size("col")
    row = lax.axis_index("row")
    col = lax.axis_index("col")
    atoms = block_mask.shape[0]
    lam_atoms, sum_atoms = density_mask.shape
    own_count = lax.dynamic_slice_in_dim(basis_count, (row * ncols + col) * atoms, atoms)
    lam_count = lax.dynamic_slice_in_dim(basis_count, row * lam_atoms, lam_atoms)
    sum_count = lax.dynamic_slice_in_dim(basis_count, col * sum_atoms, sum_atoms)
    dens = screen_density(density, lam_count, sum_count, density_mask)
    screened = screen_integrals(three_center, own_count, ri_count, block_mask, ncols)
    dens_all = lax.all_gather(dens, "col")
    blocks = lax.all_to_all(screened, "col", split_axis=0, concat_axis=0, tiled=True)
    rows_all = lax.all_gather(blocks, "row")
    wide = blocks.shape[2]
    return contract(dens_all, rows_all.reshape(ncols, -1, wide))


def solution(mesh):
    in_specs = (
        P(("row", "col"), None),
        P("row", "col"),
        P(("row", "col"), None),
        P("row", "col"),
        P(),
        P(),
    )
    return jax.shard_map(
        shards, mesh=mesh, in_specs=in_specs, out_specs=P("row", "col"), check_vma=False
    )
```

```python
import jax
import jax.numpy as jnp
from jax import lax
from jax.experimental import pallas as pl
from jax.experimental.pallas import tpu as pltpu
from jax.sharding import PartitionSpec as P

BW = 32
RW = 128
CORES = 2
VMEM = 48 * 1024 * 1024
BF16 = jnp.bfloat16
F32 = jnp.float32
SMEM_SPEC = pl.BlockSpec(memory_space=pltpu.SMEM)
VMEM_SPEC = pl.BlockSpec(memory_space=pltpu.VMEM)
ANY_SPEC = pl.BlockSpec(memory_space=pl.ANY)


def params():
    return pltpu.CompilerParams(vmem_limit_bytes=VMEM)


def ones_where(cond):
    return jnp.where(cond, 1.0, 0.0).astype(BF16)


def iota(shape, axis):
    return lax.broadcasted_iota(jnp.int32, shape, axis)


def place_row(count_ref, base, atoms, width):
    lane = iota((1, atoms * width), 1)
    place = jnp.full(lane.shape, -1, jnp.int32)
    offset = jnp.int32(0)
    for a in range(atoms):
        count = count_ref[base + a]
        inside = (lane >= a * width) & (lane < a * width + count)
        place = jnp.where(inside, lane - a * width + offset, place)
        offset = offset + count
    return place


def pack_rows(count_ref, base, atoms, width, size):
    place = place_row(count_ref, base, atoms, width)
    return ones_where(iota((size, atoms * width), 0) == place)


def pack_cols(count_ref, base, atoms, width, size, out):
    gap = iota((width, size), 1) - iota((width, size), 0)
    slot = iota((width, size), 0)
    offset = jnp.int32(0)
    for a in range(atoms):
        count = count_ref[base + a]
        out[pl.ds(a * width, width), :] = ones_where((gap == offset) & (slot < count))
        offset = offset + count


def keep_mask(lam_count, sum_count, mask, rows, cols):
    def member(atoms, size, count, axis):
        shape = (size, atoms) if axis == 0 else (atoms, size)
        first = iota(shape, 1 - axis) * BW
        at = iota(shape, axis)
        return ones_where((at >= first) & (at < first + count))

    left = member(mask.shape[0], rows, lam_count, 0)
    right = member(mask.shape[1], cols, sum_count, 1)
    keep = jnp.dot(left, ones_where(mask > 0), preferred_element_type=F32).astype(BF16)
    return jnp.dot(keep, right, preferred_element_type=F32)


def screen_integrals(tc, own_count, ri_count, block_mask, ncols):
    rows, cols = tc.shape
    atoms = rows // BW
    wide = cols // ncols
    blocks = wide // RW

    def body(count_ref, ri_ref, mask_ref, x_ref, o_ref):
        dest = pl.program_id(0)
        row = iota((BW, RW), 0)
        col = iota((BW, RW), 1)
        for b in range(blocks):
            block = dest * blocks + b
            inside = col < ri_ref[block]
            for a in range(atoms):
                limit = jnp.where(mask_ref[a, block] > 0, count_ref[a], 0)
                at = (pl.ds(a * BW, BW), pl.ds(b * RW, RW))
                x = x_ref[at].astype(F32)
                o_ref[(0,) + at] = jnp.where(inside & (row < limit), x, 0.0).astype(BF16)

    return pl.pallas_call(
        body,
        out_shape=jax.ShapeDtypeStruct((ncols, rows, wide), BF16),
        grid=(ncols,),
        in_specs=[SMEM_SPEC, SMEM_SPEC, SMEM_SPEC, pl.BlockSpec((rows, wide), lambda i: (0, i))],
        out_specs=pl.BlockSpec((1, rows, wide), lambda i: (i, 0, 0)),
        compiler_params=params(),
        name="screen_integrals",
    )(own_count, ri_count, block_mask, tc)


def screen_density(dens, lam_count, sum_count, mask):
    rows, cols = dens.shape

    def body(lam_ref, sum_ref, mask_ref, x_ref, o_ref):
        keep = keep_mask(lam_ref[...], sum_ref[...], mask_ref[...], rows, cols)
        o_ref[...] = jnp.where(keep > 0.5, x_ref[...].astype(F32), 0.0).astype(BF16)

    return pl.pallas_call(
        body,
        out_shape=jax.ShapeDtypeStruct((rows, cols), BF16),
        compiler_params=params(),
        name="screen_density",
    )(lam_count.reshape(1, -1), sum_count.reshape(-1, 1), mask, dens)


def contract_dense(dens, integrals):
    parts, rows, depth = dens.shape
    cols = integrals.shape[2]

    def body(d_ref, s_ref, o_ref, total):
        step = pl.program_id(0)
        part = jnp.dot(d_ref[0], s_ref[0], preferred_element_type=F32)

        @pl.when(step == 0)
        def _():
            total[...] = part

        @pl.when(step > 0)
        def _():
            total[...] += part

        @pl.when(step == parts - 1)
        def _():
            o_ref[...] = total[...].astype(BF16)

    return pl.pallas_call(
        body,
        out_shape=jax.ShapeDtypeStruct((rows, cols), BF16),
        grid=(parts,),
        in_specs=[
            pl.BlockSpec((1, rows, depth), lambda i: (i, 0, 0)),
            pl.BlockSpec((1, depth, cols), lambda i: (i, 0, 0)),
        ],
        out_specs=pl.BlockSpec((rows, cols), lambda i: (0, 0)),
        scratch_shapes=[pltpu.VMEM((rows, cols), F32)],
        compiler_params=params(),
        name="contract_dense",
    )(dens, integrals)


def dense(three_center, density, block_mask, density_mask, basis_count, ri_count):
    ncols = lax.axis_size("col")
    row = lax.axis_index("row")
    col = lax.axis_index("col")
    atoms = block_mask.shape[0]
    lam_atoms, sum_atoms = density_mask.shape
    own_count = lax.dynamic_slice_in_dim(basis_count, (row * ncols + col) * atoms, atoms)
    lam_count = lax.dynamic_slice_in_dim(basis_count, row * lam_atoms, lam_atoms)
    sum_count = lax.dynamic_slice_in_dim(basis_count, col * sum_atoms, sum_atoms)
    dens = screen_density(density, lam_count, sum_count, density_mask)
    screened = screen_integrals(three_center, own_count, ri_count, block_mask, ncols)
    dens_all = lax.all_gather(dens, "col")
    blocks = lax.all_to_all(screened, "col", split_axis=0, concat_axis=0, tiled=True)
    rows_all = lax.all_gather(blocks, "row")
    wide = blocks.shape[2]
    return contract_dense(dens_all, rows_all.reshape(ncols, -1, wide))


def pack_integrals(tc, block_mask, basis_count, ri_count, ncols, packed):
    rows, cols = tc.shape
    atoms = rows // BW
    wide = cols // ncols
    blocks = wide // RW
    chips = ncols // CORES

    def body(count_ref, ri_ref, mask_ref, x_ref, *refs):
        outs, held, hot = refs[:ncols], refs[ncols], refs[ncols + 1]
        row, col = lax.axis_index("row"), lax.axis_index("col")
        base = (row * ncols + col) * atoms
        slot = iota((BW, RW), 0)
        for n in range(ncols):
            up, other = n // CORES, n % CORES
            chip = lax.rem(col // CORES + up, chips)
            core = lax.rem(col + other, CORES)
            dest = chip * CORES + core
            for b in range(blocks):
                for a in range(atoms):
                    limit = jnp.where(mask_ref[a, dest * blocks + b] > 0, count_ref[base + a], 0)
                    lanes = pl.multiple_of(dest * wide + b * RW, RW)
                    x = x_ref[pl.ds(a * BW, BW), pl.ds(lanes, RW)].astype(F32)
                    held[pl.ds(a * BW, BW), pl.ds(b * RW, RW)] = jnp.where(slot < limit, x, 0.0).astype(BF16)
            pack_cols(ri_ref, dest * blocks, blocks, RW, packed, hot)
            outs[n][...] = jnp.dot(held[...], hot[...], preferred_element_type=F32).astype(BF16)

    return pl.pallas_call(
        body,
        out_shape=[jax.ShapeDtypeStruct((rows, packed), BF16)] * ncols,
        in_specs=[SMEM_SPEC, SMEM_SPEC, SMEM_SPEC, VMEM_SPEC],
        out_specs=[VMEM_SPEC] * ncols,
        scratch_shapes=[pltpu.VMEM((rows, wide), BF16), pltpu.VMEM((wide, packed), BF16)],
        compiler_params=params(),
        name="pack_integrals",
    )(basis_count, ri_count, block_mask, tc)


def pack_density(dens, mask, basis_count, lam_size, sum_size):
    rows, cols = dens.shape
    lam_atoms, sum_atoms = mask.shape

    def body(count_ref, mask_ref, x_ref, o_ref, hot):
        row, col = lax.axis_index("row"), lax.axis_index("col")
        keep = keep_mask(BW, BW, mask_ref[...], rows, cols)
        x = jnp.where(keep > 0.5, x_ref[...].astype(F32), 0.0).astype(BF16)
        left = pack_rows(count_ref, col * sum_atoms, sum_atoms, BW, sum_size)
        x = lax.dot_general(left, x, (((1,), (1,)), ((), ())), preferred_element_type=F32).astype(BF16)
        pack_cols(count_ref, row * lam_atoms, lam_atoms, BW, lam_size, hot)
        o_ref[...] = jnp.dot(x, hot[...], preferred_element_type=F32).astype(BF16)

    return pl.pallas_call(
        body,
        out_shape=jax.ShapeDtypeStruct((sum_size, lam_size), BF16),
        in_specs=[SMEM_SPEC, VMEM_SPEC, VMEM_SPEC],
        out_specs=VMEM_SPEC,
        scratch_shapes=[pltpu.VMEM((rows, lam_size), BF16)],
        compiler_params=params(),
        name="pack_density",
    )(basis_count, mask, dens)


def exchange(pieces, ncols):
    chips = ncols // CORES

    def dest(col, n):
        return (col // CORES + n // CORES) % chips * CORES + (col + n) % CORES

    got = [pieces[0]]
    for n in range(1, ncols):
        got.append(lax.ppermute(pieces[n], "col", [(c, dest(c, n)) for c in range(ncols)]))
    return got


def double(own, bits):
    nrows = lax.axis_size("row")
    have = {0: own}
    for bit in bits:
        for far in sorted(have):
            have[far | bit] = lax.ppermute(have[far], "row", [(r, r ^ bit) for r in range(nrows)])
    return have


def pack_sums(groups, basis_count, ncols, rows, depth, size):
    nrows = len(groups[0])
    cols = groups[0][0].shape[1]
    per = ncols // len(groups)
    parts = nrows * ncols * rows // depth
    atoms = depth // BW
    order = [(far, g) for far in range(nrows) for g in range(len(groups))]

    def body(count_ref, *refs):
        blocks = refs[: len(order)]
        o_ref, full, sem = refs[len(order):]
        row, col = lax.axis_index("row"), lax.axis_index("col")
        copies = []
        for i, (far, g) in enumerate(order):
            for j in range(per):
                n = g * per + j
                chips = ncols // CORES
                chip = lax.rem(col // CORES - n // CORES + chips, chips)
                core = lax.rem(col + n, CORES)
                start = ((row ^ far) * ncols + chip * CORES + core) * rows
                copies.append(
                    pltpu.make_async_copy(
                        blocks[i].at[pl.ds(j * rows, rows), :],
                        full.at[pl.ds(pl.multiple_of(start, rows), rows), :],
                        sem.at[i * per + j],
                    )
                )
        for copy in copies:
            copy.start()
        for copy in copies:
            copy.wait()
        for part in range(parts):
            hot = pack_rows(count_ref, part * atoms, atoms, BW, size)
            x = full[pl.ds(part * depth, depth), :]
            o_ref[part] = jnp.dot(hot, x, preferred_element_type=F32).astype(BF16)

    return pl.pallas_call(
        body,
        out_shape=jax.ShapeDtypeStruct((parts, size, cols), BF16),
        in_specs=[SMEM_SPEC] + [ANY_SPEC] * len(order),
        out_specs=VMEM_SPEC,
        scratch_shapes=[
            pltpu.VMEM((parts * depth, cols), BF16),
            pltpu.SemaphoreType.DMA((len(order) * per,)),
        ],
        compiler_params=params(),
        name="pack_sums",
    )(basis_count, *[groups[g][far] for far, g in order])


def contract(dens, integrals, basis_count, ri_count, rows, wide):
    parts, depth, lam = dens.shape
    cols = integrals.shape[2]
    lam_atoms, blocks = rows // BW, wide // RW

    def body(count_ref, ri_ref, d_ref, s_ref, o_ref, total, lam_hot, col_hot):
        step = pl.program_id(0)
        part = lax.dot_general(d_ref[0], s_ref[0], (((0,), (0,)), ((), ())), preferred_element_type=F32)

        @pl.when(step == 0)
        def _():
            total[...] = part
            row, col = lax.axis_index("row"), lax.axis_index("col")
            pack_cols(count_ref, row * lam_atoms, lam_atoms, BW, lam, lam_hot)
            col_hot[...] = pack_rows(ri_ref, col * blocks, blocks, RW, cols)

        @pl.when(step > 0)
        def _():
            total[...] += part

        @pl.when(step == parts - 1)
        def _():
            x = jnp.dot(total[...].astype(BF16), col_hot[...], preferred_element_type=F32).astype(BF16)
            o_ref[...] = jnp.dot(lam_hot[...], x, preferred_element_type=F32).astype(BF16)

    return pl.pallas_call(
        body,
        out_shape=jax.ShapeDtypeStruct((rows, wide), BF16),
        grid=(parts,),
        in_specs=[
            SMEM_SPEC,
            SMEM_SPEC,
            pl.BlockSpec((1, depth, lam), lambda i: (i, 0, 0)),
            pl.BlockSpec((1, depth, cols), lambda i: (i, 0, 0)),
        ],
        out_specs=pl.BlockSpec((rows, wide), lambda i: (0, 0)),
        scratch_shapes=[
            pltpu.VMEM((lam, cols), F32),
            pltpu.VMEM((rows, lam), BF16),
            pltpu.VMEM((cols, wide), BF16),
        ],
        compiler_params=params(),
        name="contract",
    )(basis_count, ri_count, dens, integrals)


def sizes(density, three_center, ncols):
    rows, depth = density.shape
    wide = three_center.shape[1] // ncols
    return rows * 3 // 4, depth * 13 // 16, wide * 5 // 6


def compact(three_center, density, block_mask, density_mask, basis_count, ri_count):
    ncols = lax.axis_size("col")
    nrows = lax.axis_size("row")
    rows, depth = density.shape
    lam_size, sum_size, col_size = sizes(density, three_center, ncols)
    pieces = pack_integrals(three_center, block_mask, basis_count, ri_count, ncols, col_size)
    dens = pack_density(density, density_mask, basis_count, lam_size, sum_size)
    dens_all = lax.all_gather(dens, "col")
    got = exchange(pieces, ncols)
    half = ncols // 2
    bits = [1 << b for b in range(nrows.bit_length() - 1)]
    groups = [
        double(jnp.concatenate(got[:half], axis=0), bits),
        double(jnp.concatenate(got[half:], axis=0), bits[::-1]),
    ]
    packed = pack_sums(groups, basis_count, ncols, three_center.shape[0], depth, sum_size)
    return contract(dens_all, packed, basis_count, ri_count, rows, three_center.shape[1] // ncols)


def shards(three_center, density, block_mask, density_mask, basis_count, ri_count):
    ncols = lax.axis_size("col")
    nrows = lax.axis_size("row")
    lam_size, sum_size, col_size = sizes(density, three_center, ncols)
    fits = (
        (basis_count.reshape(nrows, -1).sum(axis=1).max() <= lam_size)
        & (basis_count.reshape(ncols, -1).sum(axis=1).max() <= sum_size)
        & (ri_count.reshape(ncols, -1).sum(axis=1).max() <= col_size)
    )
    args = (three_center, density, block_mask, density_mask, basis_count, ri_count)
    return lax.cond(fits, compact, dense, *args)


def solution(mesh):
    in_specs = (
        P(("row", "col"), None),
        P("row", "col"),
        P(("row", "col"), None),
        P("row", "col"),
        P(),
        P(),
    )
    return jax.shard_map(
        shards, mesh=mesh, in_specs=in_specs, out_specs=P("row", "col"), check_vma=False
    )
```

```python
import jax
import jax.numpy as jnp
from jax import lax
from jax.experimental import pallas as pl
from jax.experimental.pallas import tpu as pltpu
from jax.sharding import PartitionSpec as P

BW = 32
RW = 128
CORES = 2
VMEM = 48 * 1024 * 1024
BF16 = jnp.bfloat16
F32 = jnp.float32
SMEM_SPEC = pl.BlockSpec(memory_space=pltpu.SMEM)
VMEM_SPEC = pl.BlockSpec(memory_space=pltpu.VMEM)
ANY_SPEC = pl.BlockSpec(memory_space=pl.ANY)


def params():
    return pltpu.CompilerParams(vmem_limit_bytes=VMEM)


def cost(flops, bytes_accessed):
    return pl.CostEstimate(flops=flops, bytes_accessed=bytes_accessed, transcendentals=0)


def ones_where(cond):
    return jnp.where(cond, 1.0, 0.0).astype(BF16)


def iota(shape, axis):
    return lax.broadcasted_iota(jnp.int32, shape, axis)


def place_row(count_ref, base, atoms, width):
    lane = iota((1, atoms * width), 1)
    place = jnp.full(lane.shape, -1, jnp.int32)
    offset = jnp.int32(0)
    for a in range(atoms):
        count = count_ref[base + a]
        inside = (lane >= a * width) & (lane < a * width + count)
        place = jnp.where(inside, lane - a * width + offset, place)
        offset = offset + count
    return place


def pack_rows(count_ref, base, atoms, width, size):
    place = place_row(count_ref, base, atoms, width)
    return ones_where(iota((size, atoms * width), 0) == place)


def pack_cols(count_ref, base, atoms, width, size, out):
    gap = iota((width, size), 1) - iota((width, size), 0)
    slot = iota((width, size), 0)
    offset = jnp.int32(0)
    for a in range(atoms):
        count = count_ref[base + a]
        out[pl.ds(a * width, width), :] = ones_where((gap == offset) & (slot < count))
        offset = offset + count


def keep_mask(lam_count, sum_count, mask, rows, cols):
    def member(atoms, size, count, axis):
        shape = (size, atoms) if axis == 0 else (atoms, size)
        first = iota(shape, 1 - axis) * BW
        at = iota(shape, axis)
        return ones_where((at >= first) & (at < first + count))

    left = member(mask.shape[0], rows, lam_count, 0)
    right = member(mask.shape[1], cols, sum_count, 1)
    keep = jnp.dot(left, ones_where(mask > 0), preferred_element_type=F32).astype(BF16)
    return jnp.dot(keep, right, preferred_element_type=F32)


def pack_integrals(tc, block_mask, basis_count, ri_count, ncols, packed):
    rows, cols = tc.shape
    atoms = rows // BW
    wide = cols // ncols
    blocks = wide // RW

    def body(count_ref, ri_ref, mask_ref, x_ref, *refs):
        outs, held, hot = refs[:ncols], refs[ncols], refs[ncols + 1]
        row, col = lax.axis_index("row"), lax.axis_index("col")
        base = (row * ncols + col) * atoms
        slot = iota((BW, RW), 0)
        for n in range(ncols):
            dest = col ^ n
            for b in range(blocks):
                for a in range(atoms):
                    limit = jnp.where(mask_ref[a, dest * blocks + b] > 0, count_ref[base + a], 0)
                    lanes = pl.multiple_of(dest * wide + b * RW, RW)
                    x = x_ref[pl.ds(a * BW, BW), pl.ds(lanes, RW)].astype(F32)
                    held[pl.ds(a * BW, BW), pl.ds(b * RW, RW)] = jnp.where(slot < limit, x, 0.0).astype(BF16)
            pack_cols(ri_ref, dest * blocks, blocks, RW, packed, hot)
            outs[n][...] = jnp.dot(held[...], hot[...], preferred_element_type=F32).astype(BF16)

    return pl.pallas_call(
        body,
        out_shape=[jax.ShapeDtypeStruct((rows, packed), BF16)] * ncols,
        in_specs=[SMEM_SPEC, SMEM_SPEC, SMEM_SPEC, VMEM_SPEC],
        out_specs=[VMEM_SPEC] * ncols,
        scratch_shapes=[pltpu.VMEM((rows, wide), BF16), pltpu.VMEM((wide, packed), BF16)],
        compiler_params=params(),
        cost_estimate=cost(2 * rows * cols * packed, 2 * rows * (cols + ncols * packed)),
        name="pack_integrals",
    )(basis_count, ri_count, block_mask, tc)


def pack_density(dens, mask, basis_count, lam_size, sum_size):
    rows, cols = dens.shape
    lam_atoms, sum_atoms = mask.shape

    def body(count_ref, mask_ref, x_ref, o_ref, hot):
        row, col = lax.axis_index("row"), lax.axis_index("col")
        keep = keep_mask(BW, BW, mask_ref[...], rows, cols)
        x = jnp.where(keep > 0.5, x_ref[...].astype(F32), 0.0).astype(BF16)
        left = pack_rows(count_ref, col * sum_atoms, sum_atoms, BW, sum_size)
        x = lax.dot_general(left, x, (((1,), (1,)), ((), ())), preferred_element_type=F32).astype(BF16)
        pack_cols(count_ref, row * lam_atoms, lam_atoms, BW, lam_size, hot)
        o_ref[...] = jnp.dot(x, hot[...], preferred_element_type=F32).astype(BF16)

    return pl.pallas_call(
        body,
        out_shape=jax.ShapeDtypeStruct((sum_size, lam_size), BF16),
        in_specs=[SMEM_SPEC, VMEM_SPEC, VMEM_SPEC],
        out_specs=VMEM_SPEC,
        scratch_shapes=[pltpu.VMEM((rows, lam_size), BF16)],
        compiler_params=params(),
        cost_estimate=cost(2 * rows * sum_size * (cols + lam_size), 2 * rows * cols),
        name="pack_density",
    )(basis_count, mask, dens)


def pack_part(pieces, basis_count, first, ncols, size):
    rows, cols = pieces[0].shape
    per = len(pieces)
    depth = per * rows
    atoms = depth // BW

    def body(count_ref, *refs):
        blocks, o_ref, full = refs[:per], refs[per], refs[per + 1]
        row, col = lax.axis_index("row"), lax.axis_index("col")
        for i in range(per):
            at = lax.rem(col ^ (first + i), per) * rows
            full[pl.ds(pl.multiple_of(at, rows), rows), :] = blocks[i][...]
        part = (row * ncols + (col ^ first)) * rows // depth
        hot = pack_rows(count_ref, part * atoms, atoms, BW, size)
        o_ref[...] = jnp.dot(hot, full[...], preferred_element_type=F32).astype(BF16)

    return pl.pallas_call(
        body,
        out_shape=jax.ShapeDtypeStruct((size, cols), BF16),
        in_specs=[SMEM_SPEC] + [VMEM_SPEC] * per,
        out_specs=VMEM_SPEC,
        scratch_shapes=[pltpu.VMEM((depth, cols), BF16)],
        compiler_params=params(),
        cost_estimate=cost(2 * size * depth * cols, 2 * cols * (depth + size)),
        name="pack_part",
    )(basis_count, *pieces)


def exchange(pieces, ncols):
    return [pieces[0]] + [
        lax.ppermute(pieces[n], "col", [(c, c ^ n) for c in range(ncols)]) for n in range(1, ncols)
    ]


def double(own, bits):
    nrows = lax.axis_size("row")
    have = {0: own}
    for bit in bits:
        for far in sorted(have):
            have[far | bit] = lax.ppermute(have[far], "row", [(r, r ^ bit) for r in range(nrows)])
    return have


def swap_cores(x, ncols, chips):
    return lax.ppermute(x, "col", [(c, c ^ 1) for c in range(ncols) if c // CORES in chips])


def gather_line(own, ncols):
    chips = ncols // CORES
    have = {0: (own, swap_cores(own, ncols, range(chips)))}
    up = down = own
    for t in range(1, chips):
        up = lax.ppermute(up, "col", [(c, c + CORES) for c in range((t - 1) * CORES, ncols - CORES)])
        down = lax.ppermute(down, "col", [(c, c - CORES) for c in range(CORES, ncols - (t - 1) * CORES)])
        have[t] = (up, swap_cores(up, ncols, range(t, chips)))
        have[-t] = (down, swap_cores(down, ncols, range(chips - t)))
    return have


def contract(dens, integrals, basis_count, ri_count, ncols, rows, wide):
    depth, lam = dens[0][0].shape
    cols = integrals[0][0].shape[1]
    groups, nrows = len(integrals), len(integrals[0])
    parts = groups * nrows
    chips = ncols // CORES
    lam_atoms, blocks = rows // BW, wide // RW
    lines = [(t, other) for t in range(-(chips - 1), chips) for other in range(CORES)]
    halves = [(far, g) for far in range(nrows) for g in range(groups)]
    tile = 256

    def body(count_ref, ri_ref, *refs):
        d_refs, refs = refs[: len(lines)], refs[len(lines):]
        s_refs, refs = refs[: len(halves)], refs[len(halves):]
        o_ref, d_all, s_all, packed, lam_hot, col_hot, d_sem, s_sem = refs
        row, col = lax.axis_index("row"), lax.axis_index("col")
        chip = col // CORES

        def place(part):
            return pl.ds(pl.multiple_of(part * depth, 16), depth)

        for i, (far, g) in enumerate(halves):
            part = (row ^ far) * groups + (col // (ncols // groups) ^ g)
            pltpu.make_async_copy(s_refs[i], s_all.at[place(part), :], s_sem.at[part]).start()
        for i, (t, other) in enumerate(lines):

            @pl.when((chip >= t) & (chip - t < chips))
            def _():
                part = (chip - t) * CORES + (col % CORES ^ other)
                pltpu.make_async_copy(d_refs[i], d_all.at[place(part), :], d_sem.at[part]).start()

        pack_cols(count_ref, row * lam_atoms, lam_atoms, BW, lam, lam_hot)
        col_hot[...] = pack_rows(ri_ref, col * blocks, blocks, RW, cols)
        for part in range(parts):
            pltpu.make_async_copy(s_refs[0], s_all.at[place(part), :], s_sem.at[part]).wait()
            pltpu.make_async_copy(d_refs[0], d_all.at[place(part), :], d_sem.at[part]).wait()
        for at in range(0, lam, tile):
            x = lax.dot_general(
                d_all[:, pl.ds(at, tile)], s_all[...], (((0,), (0,)), ((), ())), preferred_element_type=F32
            ).astype(BF16)
            packed[pl.ds(at, tile), :] = jnp.dot(x, col_hot[...], preferred_element_type=F32).astype(BF16)
        for at in range(0, rows, tile):
            o_ref[pl.ds(at, tile), :] = jnp.dot(
                lam_hot[pl.ds(at, tile), :], packed[...], preferred_element_type=F32
            ).astype(BF16)

    return pl.pallas_call(
        body,
        out_shape=jax.ShapeDtypeStruct((rows, wide), BF16),
        in_specs=[SMEM_SPEC, SMEM_SPEC] + [ANY_SPEC] * (len(lines) + len(halves)),
        out_specs=VMEM_SPEC,
        scratch_shapes=[
            pltpu.VMEM((parts * depth, lam), BF16),
            pltpu.VMEM((parts * depth, cols), BF16),
            pltpu.VMEM((lam, wide), BF16),
            pltpu.VMEM((rows, lam), BF16),
            pltpu.VMEM((cols, wide), BF16),
            pltpu.SemaphoreType.DMA((parts,)),
            pltpu.SemaphoreType.DMA((parts,)),
        ],
        compiler_params=params(),
        cost_estimate=cost(2 * parts * depth * lam * cols, 2 * parts * depth * (lam + cols)),
        name="contract",
    )(basis_count, ri_count, *[dens[t][o] for t, o in lines], *[integrals[g][f] for f, g in halves])


def program(lam_size, sum_size, col_size):
    def run(three_center, density, block_mask, density_mask, basis_count, ri_count):
        ncols = lax.axis_size("col")
        nrows = lax.axis_size("row")
        rows, depth = density.shape
        pieces = pack_integrals(three_center, block_mask, basis_count, ri_count, ncols, col_size)
        dens = pack_density(density, density_mask, basis_count, lam_size, sum_size)
        got = exchange(pieces, ncols)
        line = gather_line(dens, ncols)
        per = depth // three_center.shape[0]
        bits = [1 << b for b in range(nrows.bit_length() - 1)]
        groups = []
        for g in range(ncols // per):
            own = pack_part(got[g * per : (g + 1) * per], basis_count, g * per, ncols, sum_size)
            groups.append(double(own, bits if g % 2 == 0 else bits[::-1]))
        wide = three_center.shape[1] // ncols
        return contract(line, groups, basis_count, ri_count, ncols, rows, wide)

    return run


def all_fit(basis_count, ri_count, limits):
    def body(count_ref, ri_ref, o_ref):
        fits = jnp.int32(1)
        for ref, groups, limit in ((count_ref, *limits[0]), (count_ref, *limits[1]), (ri_ref, *limits[2])):
            per = ref.shape[0] // groups
            for g in range(groups):
                total = jnp.int32(0)
                for i in range(per):
                    total = total + ref[g * per + i]
                fits = jnp.where(total > limit, 0, fits)
        o_ref[0] = fits

    return pl.pallas_call(
        body,
        out_shape=jax.ShapeDtypeStruct((1,), jnp.int32),
        in_specs=[SMEM_SPEC, SMEM_SPEC],
        out_specs=SMEM_SPEC,
        name="all_fit",
    )(basis_count, ri_count)


def shards(three_center, density, block_mask, density_mask, basis_count, ri_count):
    ncols = lax.axis_size("col")
    nrows = lax.axis_size("row")
    rows, depth = density.shape
    wide = three_center.shape[1] // ncols
    lam_size, sum_size, col_size = rows * 3 // 4, depth * 13 // 16, wide * 5 // 6
    fits = all_fit(basis_count, ri_count, ((nrows, lam_size), (ncols, sum_size), (ncols, col_size)))
    args = (three_center, density, block_mask, density_mask, basis_count, ri_count)
    return lax.cond(
        fits[0] > 0, program(lam_size, sum_size, col_size), program(rows, depth, wide), *args
    )


def solution(mesh):
    in_specs = (
        P(("row", "col"), None),
        P("row", "col"),
        P(("row", "col"), None),
        P("row", "col"),
        P(),
        P(),
    )
    return jax.shard_map(
        shards, mesh=mesh, in_specs=in_specs, out_specs=P("row", "col"), check_vma=False
    )
```

```python
import jax
import jax.numpy as jnp
from jax import lax
from jax.experimental import pallas as pl
from jax.experimental.pallas import tpu as pltpu
from jax.sharding import PartitionSpec as P

BW = 32
RW = 128
CORES = 2
VMEM = 48 * 1024 * 1024
BF16 = jnp.bfloat16
F32 = jnp.float32
SMEM_SPEC = pl.BlockSpec(memory_space=pltpu.SMEM)
VMEM_SPEC = pl.BlockSpec(memory_space=pltpu.VMEM)
ANY_SPEC = pl.BlockSpec(memory_space=pl.ANY)


def params():
    return pltpu.CompilerParams(vmem_limit_bytes=VMEM)


def cost(flops, bytes_accessed):
    return pl.CostEstimate(flops=flops, bytes_accessed=bytes_accessed, transcendentals=0)


def ones_where(cond):
    return jnp.where(cond, 1.0, 0.0).astype(BF16)


def iota(shape, axis):
    return lax.broadcasted_iota(jnp.int32, shape, axis)


def place_row(count_ref, base, atoms, width):
    lane = iota((1, atoms * width), 1)
    place = jnp.full(lane.shape, -1, jnp.int32)
    offset = jnp.int32(0)
    for a in range(atoms):
        count = count_ref[base + a]
        inside = (lane >= a * width) & (lane < a * width + count)
        place = jnp.where(inside, lane - a * width + offset, place)
        offset = offset + count
    return place


def pack_rows(count_ref, base, atoms, width, size):
    place = place_row(count_ref, base, atoms, width)
    return ones_where(iota((size, atoms * width), 0) == place)


def pack_cols(count_ref, base, atoms, width, size, out):
    gap = iota((width, size), 1) - iota((width, size), 0)
    slot = iota((width, size), 0)
    offset = jnp.int32(0)
    for a in range(atoms):
        count = count_ref[base + a]
        out[pl.ds(a * width, width), :] = ones_where((gap == offset) & (slot < count))
        offset = offset + count


def keep_mask(lam_count, sum_count, mask, rows, cols):
    def member(atoms, size, count, axis):
        shape = (size, atoms) if axis == 0 else (atoms, size)
        first = iota(shape, 1 - axis) * BW
        at = iota(shape, axis)
        return ones_where((at >= first) & (at < first + count))

    left = member(mask.shape[0], rows, lam_count, 0)
    right = member(mask.shape[1], cols, sum_count, 1)
    keep = jnp.dot(left, ones_where(mask > 0), preferred_element_type=F32).astype(BF16)
    return jnp.dot(keep, right, preferred_element_type=F32)


def pack_integrals(tc, block_mask, basis_count, ri_count, ncols, packed, arrived=None):
    rows, cols = tc.shape
    atoms = rows // BW
    wide = cols // ncols
    blocks = wide // RW
    chips = ncols // CORES
    first = arrived is None

    def body(count_ref, ri_ref, mask_ref, x_ref, *refs):
        held, hot = refs[-2:]
        row, col = lax.axis_index("row"), lax.axis_index("col")
        core = lax.rem(col, CORES)
        base = (row * ncols + col) * atoms
        slot = iota((BW, RW), 0)
        for t in range(chips):
            dest = col ^ (CORES * t + (1 if first else 0))
            for b in range(blocks):
                for a in range(atoms):
                    limit = jnp.where(mask_ref[a, dest * blocks + b] > 0, count_ref[base + a], 0)
                    lanes = pl.multiple_of(dest * wide + b * RW, RW)
                    x = x_ref[pl.ds(a * BW, BW), pl.ds(lanes, RW)].astype(F32)
                    held[pl.ds(a * BW, BW), pl.ds(b * RW, RW)] = jnp.where(slot < limit, x, 0.0).astype(BF16)
            pack_cols(ri_ref, dest * blocks, blocks, RW, packed, hot)
            x = jnp.dot(held[...], hot[...], preferred_element_type=F32).astype(BF16)
            if first:
                refs[0][t] = x
            else:
                refs[1 + t][pl.ds(pl.multiple_of(core * rows, rows), rows), :] = x
                refs[1 + t][pl.ds(pl.multiple_of((1 - core) * rows, rows), rows), :] = refs[0][t]

    shape = jax.ShapeDtypeStruct((chips, rows, packed), BF16)
    merged = jax.ShapeDtypeStruct((CORES * rows, packed), BF16)
    return pl.pallas_call(
        body,
        out_shape=shape if first else [merged] * chips,
        in_specs=[SMEM_SPEC, SMEM_SPEC, SMEM_SPEC] + [VMEM_SPEC] * (1 if first else 2),
        out_specs=VMEM_SPEC if first else [VMEM_SPEC] * chips,
        scratch_shapes=[pltpu.VMEM((rows, wide), BF16), pltpu.VMEM((wide, packed), BF16)],
        compiler_params=params(),
        cost_estimate=cost(rows * cols * packed, rows * cols + 3 * chips * rows * packed),
        name="pack_other_core" if first else "pack_own_core",
    )(basis_count, ri_count, block_mask, tc, *([] if first else [arrived]))


def pack_density(dens, mask, basis_count, lam_size, sum_size):
    rows, cols = dens.shape
    lam_atoms, sum_atoms = mask.shape

    def body(count_ref, mask_ref, x_ref, o_ref, hot):
        row, col = lax.axis_index("row"), lax.axis_index("col")
        keep = keep_mask(BW, BW, mask_ref[...], rows, cols)
        x = jnp.where(keep > 0.5, x_ref[...].astype(F32), 0.0).astype(BF16)
        left = pack_rows(count_ref, col * sum_atoms, sum_atoms, BW, sum_size)
        x = lax.dot_general(left, x, (((1,), (1,)), ((), ())), preferred_element_type=F32).astype(BF16)
        pack_cols(count_ref, row * lam_atoms, lam_atoms, BW, lam_size, hot)
        o_ref[...] = jnp.dot(x, hot[...], preferred_element_type=F32).astype(BF16)

    return pl.pallas_call(
        body,
        out_shape=jax.ShapeDtypeStruct((sum_size, lam_size), BF16),
        in_specs=[SMEM_SPEC, VMEM_SPEC, VMEM_SPEC],
        out_specs=VMEM_SPEC,
        scratch_shapes=[pltpu.VMEM((rows, lam_size), BF16)],
        compiler_params=params(),
        cost_estimate=cost(2 * rows * sum_size * (cols + lam_size), 2 * rows * cols),
        name="pack_density",
    )(basis_count, mask, dens)


def pack_part(pieces, basis_count, first, ncols, size):
    rows, cols = pieces[0].shape
    per = len(pieces)
    depth = per * rows
    atoms = depth // BW

    def body(count_ref, *refs):
        blocks, o_ref, full = refs[:per], refs[per], refs[per + 1]
        row, chip = lax.axis_index("row"), lax.axis_index("col") // CORES
        for i in range(per):
            at = lax.rem(chip ^ (first + i), per) * rows
            full[pl.ds(pl.multiple_of(at, rows), rows), :] = blocks[i][...]
        part = (row * (ncols // CORES) + (chip ^ first)) * rows // depth
        hot = pack_rows(count_ref, part * atoms, atoms, BW, size)
        o_ref[...] = jnp.dot(hot, full[...], preferred_element_type=F32).astype(BF16)

    return pl.pallas_call(
        body,
        out_shape=jax.ShapeDtypeStruct((size, cols), BF16),
        in_specs=[SMEM_SPEC] + [VMEM_SPEC] * per,
        out_specs=VMEM_SPEC,
        scratch_shapes=[pltpu.VMEM((depth, cols), BF16)],
        compiler_params=params(),
        cost_estimate=cost(2 * size * depth * cols, 2 * cols * (depth + size)),
        name="pack_part",
    )(basis_count, *pieces)


def exchange(x, axis, bit):
    peers = lax.axis_size(axis)
    return lax.ppermute(x, axis, [(i, i ^ bit) for i in range(peers)])


def double(own, axis, bits):
    have = {0: own}
    for bit in bits:
        for far in sorted(have):
            have[far | bit] = exchange(have[far], axis, bit)
    return have


def contract(dens, integrals, basis_count, ri_count, ncols, rows, wide, before=None):
    keys = sorted(dens)
    depth, lam = dens[keys[0]].shape
    cols = integrals[0][0].shape[1]
    groups, nrows = len(integrals), len(integrals[0])
    parts = groups * nrows
    lam_atoms, blocks = rows // BW, wide // RW
    halves = [(far, g) for far in range(nrows) for g in range(groups)]
    last = before is not None
    tile = 256

    def body(count_ref, ri_ref, *refs):
        d_refs, refs = refs[: len(keys)], refs[len(keys):]
        s_refs, refs = refs[: len(halves)], refs[len(halves):]
        if last:
            before_ref, o_ref, d_all, s_all, d_sem, s_sem, b_sem, total, packed, lam_hot, col_hot = refs
            pltpu.make_async_copy(before_ref, total, b_sem).start()
        else:
            o_ref, d_all, s_all, d_sem, s_sem = refs
        row, col = lax.axis_index("row"), lax.axis_index("col")

        def place(i):
            return pl.ds(i * depth, depth)

        for i, far in enumerate(keys):
            pltpu.make_async_copy(d_refs[i], d_all.at[place(i), :], d_sem.at[i]).start()
            part = col ^ far
            for j, (away, g) in enumerate(halves):

                @pl.when(part == (row ^ away) * groups + (col // (ncols // groups) ^ g))
                def _():
                    pltpu.make_async_copy(s_refs[j], s_all.at[place(i), :], s_sem.at[i]).start()

        if last:
            pack_cols(count_ref, row * lam_atoms, lam_atoms, BW, lam, lam_hot)
            col_hot[...] = pack_rows(ri_ref, col * blocks, blocks, RW, cols)
            pltpu.make_async_copy(before_ref, total, b_sem).wait()
        for i in range(len(keys)):
            pltpu.make_async_copy(d_refs[i], d_all.at[place(i), :], d_sem.at[i]).wait()
            pltpu.make_async_copy(s_refs[0], s_all.at[place(i), :], s_sem.at[i]).wait()
        for at in range(0, lam, tile):
            x = lax.dot_general(
                d_all[:, pl.ds(at, tile)], s_all[...], (((0,), (0,)), ((), ())), preferred_element_type=F32
            )
            if last:
                x = (x + total[pl.ds(at, tile), :]).astype(BF16)
                packed[pl.ds(at, tile), :] = jnp.dot(x, col_hot[...], preferred_element_type=F32).astype(BF16)
            else:
                o_ref[pl.ds(at, tile), :] = x
        if last:
            for at in range(0, rows, tile):
                o_ref[pl.ds(at, tile), :] = jnp.dot(
                    lam_hot[pl.ds(at, tile), :], packed[...], preferred_element_type=F32
                ).astype(BF16)

    n = len(keys)
    scratch = [
        pltpu.VMEM((n * depth, lam), BF16),
        pltpu.VMEM((n * depth, cols), BF16),
        pltpu.SemaphoreType.DMA((n,)),
        pltpu.SemaphoreType.DMA((n,)),
    ]
    if last:
        scratch += [
            pltpu.SemaphoreType.DMA(()),
            pltpu.VMEM((lam, cols), F32),
            pltpu.VMEM((lam, wide), BF16),
            pltpu.VMEM((rows, lam), BF16),
            pltpu.VMEM((cols, wide), BF16),
        ]
    out = jax.ShapeDtypeStruct((rows, wide), BF16) if last else jax.ShapeDtypeStruct((lam, cols), F32)
    return pl.pallas_call(
        body,
        out_shape=out,
        in_specs=[SMEM_SPEC, SMEM_SPEC] + [ANY_SPEC] * (n + parts + (1 if last else 0)),
        out_specs=VMEM_SPEC,
        scratch_shapes=scratch,
        compiler_params=params(),
        cost_estimate=cost(2 * n * depth * lam * cols, 2 * n * depth * (lam + cols)),
        name="contract_last" if last else "contract_first",
    )(
        basis_count,
        ri_count,
        *[dens[far] for far in keys],
        *[integrals[g][far] for far, g in halves],
        *([before] if last else []),
    )


def program(lam_size, sum_size, col_size):
    def run(three_center, density, block_mask, density_mask, basis_count, ri_count):
        ncols = lax.axis_size("col")
        nrows = lax.axis_size("row")
        chips = ncols // CORES
        rows, depth = density.shape
        wide = three_center.shape[1] // ncols
        row_bits = [1 << b for b in range(nrows.bit_length() - 1)]
        chip_bits = [CORES << b for b in range(chips.bit_length() - 1)][::-1]

        own = pack_density(density, density_mask, basis_count, lam_size, sum_size)
        counts = (block_mask, basis_count, ri_count, ncols, col_size)
        other = exchange(pack_integrals(three_center, *counts), "col", 1)
        line = {0: own, chip_bits[0]: exchange(own, "col", chip_bits[0])}
        other, _ = lax.optimization_barrier((other, own))
        pieces = pack_integrals(three_center, *counts, other)
        got = [pieces[0]] + [exchange(pieces[t], "col", CORES * t) for t in range(1, chips)]
        per = depth // pieces[0].shape[0]
        parts, groups = [], []
        for g in range(chips // per):
            parts.append(pack_part(got[g * per : (g + 1) * per], basis_count, g * per, ncols, sum_size))
            groups.append(double(parts[g], "row", row_bits if g % 2 == 0 else row_bits[::-1]))
        for far in list(line):
            line[far], _ = lax.optimization_barrier((line[far], parts[0] if far == 0 else parts[-1]))
        for bit in chip_bits[1:]:
            for far in sorted(line):
                line[far | bit] = exchange(line[far], "col", bit)
        blocks = {}
        for far, block in line.items():
            blocks[far] = block
            blocks[far | 1] = exchange(block, "col", 1)
        late = {far: blocks.pop(far) for far in (ncols - CORES, ncols - 1)}
        ends = (groups, basis_count, ri_count, ncols, rows, wide)
        return contract(late, *ends, contract(blocks, *ends))

    return run


def all_fit(basis_count, ri_count, limits):
    def body(count_ref, ri_ref, o_ref):
        fits = jnp.int32(1)
        for ref, groups, limit in ((count_ref, *limits[0]), (count_ref, *limits[1]), (ri_ref, *limits[2])):
            per = ref.shape[0] // groups
            for g in range(groups):
                total = jnp.int32(0)
                for i in range(per):
                    total = total + ref[g * per + i]
                fits = jnp.where(total > limit, 0, fits)
        o_ref[0] = fits

    return pl.pallas_call(
        body,
        out_shape=jax.ShapeDtypeStruct((1,), jnp.int32),
        in_specs=[SMEM_SPEC, SMEM_SPEC],
        out_specs=SMEM_SPEC,
        name="all_fit",
    )(basis_count, ri_count)


def shards(three_center, density, block_mask, density_mask, basis_count, ri_count):
    ncols = lax.axis_size("col")
    nrows = lax.axis_size("row")
    rows, depth = density.shape
    wide = three_center.shape[1] // ncols
    lam_size, sum_size, col_size = rows * 3 // 4, depth * 13 // 16, wide * 5 // 6
    fits = all_fit(basis_count, ri_count, ((nrows, lam_size), (ncols, sum_size), (ncols, col_size)))
    args = (three_center, density, block_mask, density_mask, basis_count, ri_count)
    return lax.cond(
        fits[0] > 0, program(lam_size, sum_size, col_size), program(rows, depth, wide), *args
    )


def solution(mesh):
    in_specs = (
        P(("row", "col"), None),
        P("row", "col"),
        P(("row", "col"), None),
        P("row", "col"),
        P(),
        P(),
    )
    return jax.shard_map(
        shards, mesh=mesh, in_specs=in_specs, out_specs=P("row", "col"), check_vma=False
    )
```

```python
import jax
import jax.numpy as jnp
from jax import lax
from jax.experimental import pallas as pl
from jax.experimental.pallas import tpu as pltpu
from jax.sharding import PartitionSpec as P

BW = 32
RW = 128
CORES = 2
VMEM = 48 * 1024 * 1024
BF16 = jnp.bfloat16
F32 = jnp.float32
SMEM_SPEC = pl.BlockSpec(memory_space=pltpu.SMEM)
VMEM_SPEC = pl.BlockSpec(memory_space=pltpu.VMEM)
ANY_SPEC = pl.BlockSpec(memory_space=pl.ANY)


def params():
    return pltpu.CompilerParams(vmem_limit_bytes=VMEM)


def cost(flops, bytes_accessed):
    return pl.CostEstimate(flops=flops, bytes_accessed=bytes_accessed, transcendentals=0)


def ones_where(cond):
    return jnp.where(cond, 1.0, 0.0).astype(BF16)


def iota(shape, axis):
    return lax.broadcasted_iota(jnp.int32, shape, axis)


def place_row(count_ref, base, atoms, width):
    lane = iota((1, atoms * width), 1)
    place = jnp.full(lane.shape, -1, jnp.int32)
    offset = jnp.int32(0)
    for a in range(atoms):
        count = count_ref[base + a]
        inside = (lane >= a * width) & (lane < a * width + count)
        place = jnp.where(inside, lane - a * width + offset, place)
        offset = offset + count
    return place


def pack_rows(count_ref, base, atoms, width, size):
    place = place_row(count_ref, base, atoms, width)
    return ones_where(iota((size, atoms * width), 0) == place)


def pack_cols(count_ref, base, atoms, width, size, out):
    gap = iota((width, size), 1) - iota((width, size), 0)
    slot = iota((width, size), 0)
    offset = jnp.int32(0)
    for a in range(atoms):
        count = count_ref[base + a]
        out[pl.ds(a * width, width), :] = ones_where((gap == offset) & (slot < count))
        offset = offset + count


def keep_mask(lam_count, sum_count, mask, rows, cols):
    def member(atoms, size, count, axis):
        shape = (size, atoms) if axis == 0 else (atoms, size)
        first = iota(shape, 1 - axis) * BW
        at = iota(shape, axis)
        return ones_where((at >= first) & (at < first + count))

    left = member(mask.shape[0], rows, lam_count, 0)
    right = member(mask.shape[1], cols, sum_count, 1)
    keep = jnp.dot(left, ones_where(mask > 0), preferred_element_type=F32).astype(BF16)
    return jnp.dot(keep, right, preferred_element_type=F32)


def pack_integrals(tc, block_mask, basis_count, ri_count, ncols, packed, arrived=None):
    rows, cols = tc.shape
    atoms = rows // BW
    wide = cols // ncols
    blocks = wide // RW
    chips = ncols // CORES
    first = arrived is None

    def body(count_ref, ri_ref, mask_ref, x_ref, *refs):
        held, hot = refs[-2:]
        row, col = lax.axis_index("row"), lax.axis_index("col")
        core = lax.rem(col, CORES)
        base = (row * ncols + col) * atoms
        slot = iota((BW, RW), 0)
        for t in range(chips):
            dest = col ^ (CORES * t + (1 if first else 0))
            for b in range(blocks):
                for a in range(atoms):
                    limit = jnp.where(mask_ref[a, dest * blocks + b] > 0, count_ref[base + a], 0)
                    lanes = pl.multiple_of(dest * wide + b * RW, RW)
                    x = x_ref[pl.ds(a * BW, BW), pl.ds(lanes, RW)].astype(F32)
                    held[pl.ds(a * BW, BW), pl.ds(b * RW, RW)] = jnp.where(slot < limit, x, 0.0).astype(BF16)
            pack_cols(ri_ref, dest * blocks, blocks, RW, packed, hot)
            x = jnp.dot(held[...], hot[...], preferred_element_type=F32).astype(BF16)
            if first:
                refs[0][t] = x
            else:
                refs[1 + t][pl.ds(pl.multiple_of(core * rows, rows), rows), :] = x
                refs[1 + t][pl.ds(pl.multiple_of((1 - core) * rows, rows), rows), :] = refs[0][t]

    shape = jax.ShapeDtypeStruct((chips, rows, packed), BF16)
    merged = jax.ShapeDtypeStruct((CORES * rows, packed), BF16)
    return pl.pallas_call(
        body,
        out_shape=shape if first else [merged] * chips,
        in_specs=[SMEM_SPEC, SMEM_SPEC, SMEM_SPEC] + [VMEM_SPEC] * (1 if first else 2),
        out_specs=VMEM_SPEC if first else [VMEM_SPEC] * chips,
        scratch_shapes=[pltpu.VMEM((rows, wide), BF16), pltpu.VMEM((wide, packed), BF16)],
        compiler_params=params(),
        cost_estimate=cost(rows * cols * packed, rows * cols + 3 * chips * rows * packed),
        name="pack_other_core" if first else "pack_own_core",
    )(basis_count, ri_count, block_mask, tc, *([] if first else [arrived]))


def pack_density(dens, mask, basis_count, lam_size, sum_size):
    rows, cols = dens.shape
    lam_atoms, sum_atoms = mask.shape

    def body(count_ref, mask_ref, x_ref, o_ref, hot):
        row, col = lax.axis_index("row"), lax.axis_index("col")
        keep = keep_mask(BW, BW, mask_ref[...], rows, cols)
        x = jnp.where(keep > 0.5, x_ref[...].astype(F32), 0.0).astype(BF16)
        pack_cols(count_ref, col * sum_atoms, sum_atoms, BW, sum_size, hot)
        x = jnp.dot(x, hot[...], preferred_element_type=F32).astype(BF16)
        left = pack_rows(count_ref, row * lam_atoms, lam_atoms, BW, lam_size)
        o_ref[...] = jnp.dot(left, x, preferred_element_type=F32).astype(BF16)

    return pl.pallas_call(
        body,
        out_shape=jax.ShapeDtypeStruct((lam_size, sum_size), BF16),
        in_specs=[SMEM_SPEC, VMEM_SPEC, VMEM_SPEC],
        out_specs=VMEM_SPEC,
        scratch_shapes=[pltpu.VMEM((cols, sum_size), BF16)],
        compiler_params=params(),
        cost_estimate=cost(2 * rows * sum_size * (cols + lam_size), 2 * rows * cols),
        name="pack_density",
    )(basis_count, mask, dens)


def pack_part(pieces, basis_count, first, ncols, size):
    rows, cols = pieces[0].shape
    per = len(pieces)
    depth = per * rows
    atoms = depth // BW

    def body(count_ref, *refs):
        blocks, o_ref, full = refs[:per], refs[per], refs[per + 1]
        row, chip = lax.axis_index("row"), lax.axis_index("col") // CORES
        for i in range(per):
            at = lax.rem(chip ^ (first + i), per) * rows
            full[pl.ds(pl.multiple_of(at, rows), rows), :] = blocks[i][...]
        part = (row * (ncols // CORES) + (chip ^ first)) * rows // depth
        hot = pack_rows(count_ref, part * atoms, atoms, BW, size)
        o_ref[...] = jnp.dot(hot, full[...], preferred_element_type=F32).astype(BF16)

    return pl.pallas_call(
        body,
        out_shape=jax.ShapeDtypeStruct((size, cols), BF16),
        in_specs=[SMEM_SPEC] + [VMEM_SPEC] * per,
        out_specs=VMEM_SPEC,
        scratch_shapes=[pltpu.VMEM((depth, cols), BF16)],
        compiler_params=params(),
        cost_estimate=cost((2 + 10 * first) * size * depth * cols, 2 * cols * (depth + size)),
        name="pack_part",
    )(basis_count, *pieces)


def exchange(x, axis, bit):
    peers = lax.axis_size(axis)
    return lax.ppermute(x, axis, [(i, i ^ bit) for i in range(peers)])


def after(x, *others):
    return lax.optimization_barrier((x, *others))[0]


def double(own, axis, bits):
    have = {0: own}
    for bit in bits:
        for far in sorted(have):
            have[far | bit] = exchange(have[far], axis, bit)
    return have


def contract(dens, integrals, basis_count, ri_count, ncols, rows, wide, before=None):
    keys = list(dens)
    lam, depth = dens[keys[0]].shape
    cols = integrals[0][0].shape[1]
    groups, nrows = len(integrals), len(integrals[0])
    parts = groups * nrows
    lam_atoms, blocks = rows // BW, wide // RW
    halves = [(far, g) for far in range(nrows) for g in range(groups)]
    last = before is not None
    tile = 256
    n = len(keys)

    def body(count_ref, ri_ref, *refs):
        d_refs, refs = refs[:n], refs[n:]
        s_refs, refs = refs[: len(halves)], refs[len(halves):]
        if last:
            before_ref, o_ref, d_all, s_all, d_sem, s_sem, b_sem, total, packed, lam_hot, col_hot = refs
            begin = pltpu.make_async_copy(before_ref, total, b_sem)
            begin.start()
        else:
            total, d_all, s_all, d_sem, s_sem = refs
        row, col = lax.axis_index("row"), lax.axis_index("col")
        for i, far in enumerate(keys):
            part = col ^ far
            for j, (away, g) in enumerate(halves):

                @pl.when(part == (row ^ away) * groups + (col // (ncols // groups) ^ g))
                def _():
                    pltpu.make_async_copy(s_refs[j], s_all.at[i], s_sem.at[i]).start()

            pltpu.make_async_copy(d_refs[i], d_all.at[i], d_sem.at[i]).start()

        if last:
            pack_cols(count_ref, row * lam_atoms, lam_atoms, BW, lam, lam_hot)
            col_hot[...] = pack_rows(ri_ref, col * blocks, blocks, RW, cols)
            begin.wait()
        for i in range(n):
            pltpu.make_async_copy(s_refs[0], s_all.at[i], s_sem.at[i]).wait()
            pltpu.make_async_copy(d_refs[i], d_all.at[i], d_sem.at[i]).wait()
            for at in range(0, lam, tile):
                x = jnp.dot(d_all[i, pl.ds(at, tile), :], s_all[i], preferred_element_type=F32)
                if i > 0 or last:
                    x = x + total[pl.ds(at, tile), :]
                if last and i == n - 1:
                    x = x.astype(BF16)
                    packed[pl.ds(at, tile), :] = jnp.dot(x, col_hot[...], preferred_element_type=F32).astype(BF16)
                else:
                    total[pl.ds(at, tile), :] = x
        if last:
            for at in range(0, rows, tile):
                o_ref[pl.ds(at, tile), :] = jnp.dot(
                    lam_hot[pl.ds(at, tile), :], packed[...], preferred_element_type=F32
                ).astype(BF16)

    scratch = [
        pltpu.VMEM((n, lam, depth), BF16),
        pltpu.VMEM((n, depth, cols), BF16),
        pltpu.SemaphoreType.DMA((n,)),
        pltpu.SemaphoreType.DMA((n,)),
    ]
    if last:
        scratch += [
            pltpu.SemaphoreType.DMA(()),
            pltpu.VMEM((lam, cols), F32),
            pltpu.VMEM((lam, wide), BF16),
            pltpu.VMEM((rows, lam), BF16),
            pltpu.VMEM((cols, wide), BF16),
        ]
    out = jax.ShapeDtypeStruct((rows, wide), BF16) if last else jax.ShapeDtypeStruct((lam, cols), F32)
    return pl.pallas_call(
        body,
        out_shape=out,
        in_specs=[SMEM_SPEC, SMEM_SPEC] + [ANY_SPEC] * (n + parts + (1 if last else 0)),
        out_specs=VMEM_SPEC,
        scratch_shapes=scratch,
        compiler_params=params(),
        cost_estimate=cost(2 * n * depth * lam * cols, 2 * n * depth * (lam + cols)),
        name="contract_last" if last else "contract_first",
    )(
        basis_count,
        ri_count,
        *[dens[far] for far in keys],
        *[integrals[g][far] for far, g in halves],
        *([before] if last else []),
    )


def program(lam_size, sum_size, col_size):
    def run(three_center, density, block_mask, density_mask, basis_count, ri_count):
        ncols = lax.axis_size("col")
        nrows = lax.axis_size("row")
        chips = ncols // CORES
        rows, depth = density.shape
        wide = three_center.shape[1] // ncols
        row_bits = [1 << b for b in range(nrows.bit_length() - 1)]
        chip_bits = [CORES << b for b in range(chips.bit_length() - 1)][::-1]

        counts = (block_mask, basis_count, ri_count, ncols, col_size)
        other = exchange(pack_integrals(three_center, *counts), "col", 1)
        own = pack_density(density, density_mask, basis_count, lam_size, sum_size)
        pieces = pack_integrals(three_center, *counts, after(other, own))
        got = [pieces[0]] + [exchange(pieces[t], "col", CORES * t) for t in range(1, chips)]
        per = depth // pieces[0].shape[0]
        parts, groups = [], []
        for g in range(chips // per):
            part = pack_part(got[g * per : (g + 1) * per], basis_count, g * per, ncols, sum_size)
            if g > 0:
                part = after(part, *[groups[0][bit] for bit in row_bits])
            parts.append(part)
            groups.append(double(part, "row", row_bits if g % 2 == 0 else row_bits[::-1]))
        own = after(own, parts[-1])
        line = {0: own, chip_bits[0]: exchange(own, "col", chip_bits[0])}
        for bit in chip_bits[1:]:
            for far in sorted(line):
                line[far | bit] = exchange(line[far], "col", bit)
        blocks = {}
        for far, block in line.items():
            blocks[far] = block
            blocks[far | 1] = exchange(block, "col", 1)
        late = {far: blocks.pop(far) for far in (ncols - CORES, ncols - 1)}
        ends = (groups, basis_count, ri_count, ncols, rows, wide)
        return contract(late, *ends, contract(blocks, *ends))

    return run


def first_fit(basis_count, ri_count, groups, levels):
    def body(count_ref, ri_ref, o_ref):
        level = jnp.int32(0)
        for axis, (ref, parts) in enumerate(zip((count_ref, count_ref, ri_ref), groups)):
            per = ref.shape[0] // parts
            most = jnp.int32(0)
            for g in range(parts):
                total = jnp.int32(0)
                for i in range(per):
                    total = total + ref[g * per + i]
                most = jnp.maximum(most, total)
            for n, sizes in enumerate(levels[:-1]):
                level = jnp.where(most > sizes[axis], jnp.maximum(level, n + 1), level)
        o_ref[0] = level

    return pl.pallas_call(
        body,
        out_shape=jax.ShapeDtypeStruct((1,), jnp.int32),
        in_specs=[SMEM_SPEC, SMEM_SPEC],
        out_specs=SMEM_SPEC,
        name="first_fit",
    )(basis_count, ri_count)


def shards(three_center, density, block_mask, density_mask, basis_count, ri_count):
    ncols = lax.axis_size("col")
    nrows = lax.axis_size("row")
    rows, depth = density.shape
    wide = three_center.shape[1] // ncols
    levels = (
        (rows * 3 // 4, depth * 3 // 4, wide * 5 // 6),
        (rows * 3 // 4, depth, wide),
        (rows, depth, wide),
    )
    level = first_fit(basis_count, ri_count, (nrows, ncols, ncols), levels)
    args = (three_center, density, block_mask, density_mask, basis_count, ri_count)
    return lax.switch(level[0], [program(*sizes) for sizes in levels], *args)


def solution(mesh):
    in_specs = (
        P(("row", "col"), None),
        P("row", "col"),
        P(("row", "col"), None),
        P("row", "col"),
        P(),
        P(),
    )
    return jax.shard_map(
        shards, mesh=mesh, in_specs=in_specs, out_specs=P("row", "col"), check_vma=False
    )
```

```python
import jax
import jax.numpy as jnp
from jax import lax
from jax.experimental import pallas as pl
from jax.experimental.pallas import tpu as pltpu
from jax.sharding import PartitionSpec as P

BW = 32
RW = 128
CORES = 2
VMEM = 48 * 1024 * 1024
BF16 = jnp.bfloat16
F32 = jnp.float32
SMEM_SPEC = pl.BlockSpec(memory_space=pltpu.SMEM)
VMEM_SPEC = pl.BlockSpec(memory_space=pltpu.VMEM)
ANY_SPEC = pl.BlockSpec(memory_space=pl.ANY)


def params(limit=VMEM):
    return pltpu.CompilerParams(vmem_limit_bytes=limit)


def cost(flops, bytes_accessed):
    return pl.CostEstimate(flops=flops, bytes_accessed=bytes_accessed, transcendentals=0)


def ones_where(cond):
    return jnp.where(cond, 1.0, 0.0).astype(BF16)


def iota(shape, axis):
    return lax.broadcasted_iota(jnp.int32, shape, axis)


def place_row(count_ref, base, atoms, width):
    lane = iota((1, atoms * width), 1)
    place = jnp.full(lane.shape, -1, jnp.int32)
    offset = jnp.int32(0)
    for a in range(atoms):
        count = count_ref[base + a]
        inside = (lane >= a * width) & (lane < a * width + count)
        place = jnp.where(inside, lane - a * width + offset, place)
        offset = offset + count
    return place


def pack_rows(count_ref, base, atoms, width, size):
    place = place_row(count_ref, base, atoms, width)
    return ones_where(iota((size, atoms * width), 0) == place)


def pack_cols(count_ref, base, atoms, width, size, out):
    gap = iota((width, size), 1) - iota((width, size), 0)
    slot = iota((width, size), 0)
    offset = jnp.int32(0)
    for a in range(atoms):
        count = count_ref[base + a]
        out[pl.ds(a * width, width), :] = ones_where((gap == offset) & (slot < count))
        offset = offset + count


def keep_mask(lam_count, sum_count, mask, rows, cols):
    def member(atoms, size, count, axis):
        shape = (size, atoms) if axis == 0 else (atoms, size)
        first = iota(shape, 1 - axis) * BW
        at = iota(shape, axis)
        return ones_where((at >= first) & (at < first + count))

    left = member(mask.shape[0], rows, lam_count, 0)
    right = member(mask.shape[1], cols, sum_count, 1)
    keep = jnp.dot(left, ones_where(mask > 0), preferred_element_type=F32).astype(BF16)
    return jnp.dot(keep, right, preferred_element_type=F32)


def pack_integrals(tc, block_mask, basis_count, ri_count, ncols, packed, arrived=None):
    rows, cols = tc.shape
    atoms = rows // BW
    wide = cols // ncols
    blocks = wide // RW
    chips = ncols // CORES
    first = arrived is None

    def body(count_ref, ri_ref, mask_ref, x_ref, *refs):
        held, hot = refs[-2:]
        row, col = lax.axis_index("row"), lax.axis_index("col")
        core = lax.rem(col, CORES)
        base = (row * ncols + col) * atoms
        slot = iota((BW, RW), 0)
        for t in range(chips):
            dest = col ^ (CORES * t + (1 if first else 0))
            for b in range(blocks):
                for a in range(atoms):
                    limit = jnp.where(mask_ref[a, dest * blocks + b] > 0, count_ref[base + a], 0)
                    lanes = pl.multiple_of(dest * wide + b * RW, RW)
                    x = x_ref[pl.ds(a * BW, BW), pl.ds(lanes, RW)].astype(F32)
                    held[pl.ds(a * BW, BW), pl.ds(b * RW, RW)] = jnp.where(slot < limit, x, 0.0).astype(BF16)
            pack_cols(ri_ref, dest * blocks, blocks, RW, packed, hot)
            x = jnp.dot(held[...], hot[...], preferred_element_type=F32).astype(BF16)
            if first:
                refs[0][t] = x
            else:
                refs[1 + t][pl.ds(pl.multiple_of(core * rows, rows), rows), :] = x
                refs[1 + t][pl.ds(pl.multiple_of((1 - core) * rows, rows), rows), :] = refs[0][t]

    shape = jax.ShapeDtypeStruct((chips, rows, packed), BF16)
    merged = jax.ShapeDtypeStruct((CORES * rows, packed), BF16)
    return pl.pallas_call(
        body,
        out_shape=shape if first else [merged] * chips,
        in_specs=[SMEM_SPEC, SMEM_SPEC, SMEM_SPEC] + [VMEM_SPEC] * (1 if first else 2),
        out_specs=VMEM_SPEC if first else [VMEM_SPEC] * chips,
        scratch_shapes=[pltpu.VMEM((rows, wide), BF16), pltpu.VMEM((wide, packed), BF16)],
        compiler_params=params(),
        cost_estimate=cost(rows * cols * packed, rows * cols + 3 * chips * rows * packed),
        name="pack_other_core" if first else "pack_own_core",
    )(basis_count, ri_count, block_mask, tc, *([] if first else [arrived]))


def pack_density(dens, mask, basis_count, lam_size, sum_size):
    rows, cols = dens.shape
    lam_atoms, sum_atoms = mask.shape
    half = lam_size // 2

    def body(count_ref, mask_ref, x_ref, o_ref, upper_ref, lower_ref, hot):
        row, col = lax.axis_index("row"), lax.axis_index("col")
        keep = keep_mask(BW, BW, mask_ref[...], rows, cols)
        x = jnp.where(keep > 0.5, x_ref[...].astype(F32), 0.0).astype(BF16)
        pack_cols(count_ref, col * sum_atoms, sum_atoms, BW, sum_size, hot)
        x = jnp.dot(x, hot[...], preferred_element_type=F32).astype(BF16)
        left = pack_rows(count_ref, row * lam_atoms, lam_atoms, BW, lam_size)
        x = jnp.dot(left, x, preferred_element_type=F32).astype(BF16)
        o_ref[...] = x
        upper_ref[...] = x[:half]
        lower_ref[...] = x[half:]

    whole = jax.ShapeDtypeStruct((lam_size, sum_size), BF16)
    part = jax.ShapeDtypeStruct((half, sum_size), BF16)
    return pl.pallas_call(
        body,
        out_shape=[whole, part, part],
        in_specs=[SMEM_SPEC, VMEM_SPEC, VMEM_SPEC],
        out_specs=[VMEM_SPEC] * 3,
        scratch_shapes=[pltpu.VMEM((cols, sum_size), BF16)],
        compiler_params=params(),
        cost_estimate=cost(2 * rows * sum_size * (cols + lam_size), 2 * rows * cols),
        name="pack_density",
    )(basis_count, mask, dens)


def pack_part(pieces, basis_count, first, ncols, size):
    rows, cols = pieces[0].shape
    per = len(pieces)
    depth = per * rows
    atoms = depth // BW

    def body(count_ref, *refs):
        blocks, o_ref, full = refs[:per], refs[per], refs[per + 1]
        row, chip = lax.axis_index("row"), lax.axis_index("col") // CORES
        for i in range(per):
            at = lax.rem(chip ^ (first + i), per) * rows
            full[pl.ds(pl.multiple_of(at, rows), rows), :] = blocks[i][...]
        part = (row * (ncols // CORES) + (chip ^ first)) * rows // depth
        hot = pack_rows(count_ref, part * atoms, atoms, BW, size)
        o_ref[...] = jnp.dot(hot, full[...], preferred_element_type=F32).astype(BF16)

    return pl.pallas_call(
        body,
        out_shape=jax.ShapeDtypeStruct((size, cols), BF16),
        in_specs=[SMEM_SPEC] + [VMEM_SPEC] * per,
        out_specs=VMEM_SPEC,
        scratch_shapes=[pltpu.VMEM((depth, cols), BF16)],
        compiler_params=params(),
        cost_estimate=cost((2 + 10 * first) * size * depth * cols, 2 * cols * (depth + size)),
        name="pack_part",
    )(basis_count, *pieces)


def exchange(x, axis, bit):
    peers = lax.axis_size(axis)
    return lax.ppermute(x, axis, [(i, i ^ bit) for i in range(peers)])


def after(x, *others):
    return lax.optimization_barrier((x, *others))[0]


def double(own, axis, bits):
    have = {0: own}
    for bit in bits:
        for far in sorted(have):
            have[far | bit] = exchange(have[far], axis, bit)
    return have


def gather_sums(keys, s_refs, s_all, s_sem, groups, ncols):
    row, col = lax.axis_index("row"), lax.axis_index("col")
    for i, far in enumerate(keys):
        part = col ^ far
        for j, ref in enumerate(s_refs):

            @pl.when(part == (row ^ (j // groups)) * groups + (col // (ncols // groups) ^ (j % groups)))
            def _():
                pltpu.make_async_copy(ref, s_all.at[i], s_sem.at[i]).start()


def contract_first(dens, integrals, basis_count, ri_count, ncols, rows, wide):
    keys = list(dens)
    chunks = [chunk for far in keys for chunk in dens[far]]
    lam, depth = sum(x.shape[0] for x in dens[keys[0]]), chunks[0].shape[1]
    sums = [integrals[g][far] for far in range(len(integrals[0])) for g in range(len(integrals))]
    cols = sums[0].shape[1]
    lam_atoms, blocks = rows // BW, wide // RW
    n = len(keys)

    def body(count_ref, ri_ref, *refs):
        d_refs, refs = refs[: len(chunks)], refs[len(chunks):]
        s_refs, refs = refs[: len(sums)], refs[len(sums):]
        total, lam_hot, col_hot, s_all, s_sem = refs
        gather_sums(keys, s_refs, s_all, s_sem, len(integrals), ncols)
        row, col = lax.axis_index("row"), lax.axis_index("col")
        pack_cols(count_ref, row * lam_atoms, lam_atoms, BW, lam, lam_hot)
        col_hot[...] = pack_rows(ri_ref, col * blocks, blocks, RW, cols)
        at = 0
        for i in range(n):
            pltpu.make_async_copy(s_refs[0], s_all.at[i], s_sem.at[i]).wait()
            for _ in dens[keys[i]]:
                d_ref = d_refs[at]
                at += 1
                size = d_ref.shape[0]
                first = 0 if size == lam else size * ((at - 1 - d_at[i]))
                for tile in range(0, size, half):
                    x = jnp.dot(d_ref[pl.ds(tile, half), :], s_all[i], preferred_element_type=F32)
                    out = pl.ds(first + tile, half)
                    total[out, :] = x if i == 0 else total[out, :] + x

    half = lam // 2
    d_at = [sum(len(dens[k]) for k in keys[:i]) for i in range(n)]
    need = 2 * (n * depth * (lam + cols) + 2 * lam * cols + rows * lam + cols * wide)
    return pl.pallas_call(
        body,
        out_shape=[
            jax.ShapeDtypeStruct((lam, cols), F32),
            jax.ShapeDtypeStruct((rows, lam), BF16),
            jax.ShapeDtypeStruct((cols, wide), BF16),
        ],
        in_specs=[SMEM_SPEC, SMEM_SPEC] + [VMEM_SPEC] * len(chunks) + [ANY_SPEC] * len(sums),
        out_specs=[VMEM_SPEC] * 3,
        scratch_shapes=[pltpu.VMEM((n, depth, cols), BF16), pltpu.SemaphoreType.DMA((n,))],
        compiler_params=params(need + 8 * 1024 * 1024),
        cost_estimate=cost(2 * n * depth * lam * cols, 2 * n * depth * (lam + cols)),
        name="contract_first",
    )(basis_count, ri_count, *chunks, *sums)


def contract_last(dens, integrals, before, ncols):
    keys = list(dens)
    chunks = [chunk for far in keys for chunk in dens[far]]
    sums = [integrals[g][far] for far in range(len(integrals[0])) for g in range(len(integrals))]
    total, lam_hot, col_hot = before
    (rows, lam), (cols, wide) = lam_hot.shape, col_hot.shape
    half, depth = chunks[0].shape
    n = len(keys)

    def body(total, lam_hot, col_hot, *refs):
        d_refs, refs = refs[: len(chunks)], refs[len(chunks):]
        s_refs, refs = refs[: len(sums)], refs[len(sums):]
        o_ref, s_all, s_sem, packed = refs
        gather_sums(keys, s_refs, s_all, s_sem, len(integrals), ncols)
        for i in range(n):
            pltpu.make_async_copy(s_refs[0], s_all.at[i], s_sem.at[i]).wait()
        for h in range(2):
            out = pl.ds(h * half, half)
            x = total[out, :]
            for i in range(n):
                x = x + jnp.dot(d_refs[2 * i + h][...], s_all[i], preferred_element_type=F32)
            packed[out, :] = jnp.dot(x.astype(BF16), col_hot[...], preferred_element_type=F32).astype(BF16)
        tile = rows // 4
        for at in range(0, rows, tile):
            o_ref[pl.ds(at, tile), :] = jnp.dot(
                lam_hot[pl.ds(at, tile), :], packed[...], preferred_element_type=F32
            ).astype(BF16)

    need = 2 * (n * depth * (lam + cols) + 2 * lam * cols + rows * lam + cols * wide + (lam + rows) * wide)
    return pl.pallas_call(
        body,
        out_shape=jax.ShapeDtypeStruct((rows, wide), BF16),
        in_specs=[VMEM_SPEC] * (3 + len(chunks)) + [ANY_SPEC] * len(sums),
        out_specs=VMEM_SPEC,
        scratch_shapes=[
            pltpu.VMEM((n, depth, cols), BF16),
            pltpu.SemaphoreType.DMA((n,)),
            pltpu.VMEM((lam, wide), BF16),
        ],
        compiler_params=params(need + 8 * 1024 * 1024),
        cost_estimate=cost(2 * n * depth * lam * cols, 2 * n * depth * (lam + cols)),
        name="contract_last",
    )(total, lam_hot, col_hot, *chunks, *sums)


def program(lam_size, sum_size, col_size):
    def run(three_center, density, block_mask, density_mask, basis_count, ri_count):
        ncols = lax.axis_size("col")
        nrows = lax.axis_size("row")
        chips = ncols // CORES
        rows, depth = density.shape
        wide = three_center.shape[1] // ncols
        row_bits = [1 << b for b in range(nrows.bit_length() - 1)]
        chip_bits = [CORES << b for b in range(chips.bit_length() - 1)][::-1]

        counts = (block_mask, basis_count, ri_count, ncols, col_size)
        other = exchange(pack_integrals(three_center, *counts), "col", 1)
        own, *halves = pack_density(density, density_mask, basis_count, lam_size, sum_size)
        pieces = pack_integrals(three_center, *counts, after(other, own))
        got = [pieces[0]] + [exchange(pieces[t], "col", CORES * t) for t in range(1, chips)]
        per = depth // pieces[0].shape[0]
        parts, groups = [], []
        for g in range(chips // per):
            part = pack_part(got[g * per : (g + 1) * per], basis_count, g * per, ncols, sum_size)
            if g > 0:
                part = after(part, *[groups[0][bit] for bit in row_bits])
            parts.append(part)
            groups.append(double(part, "row", row_bits if g % 2 == 0 else row_bits[::-1]))
        own = after(own, parts[-1])
        step = groups[-1][row_bits[-1]]
        lines = []
        for half, hold in zip(halves, (parts[-1], step)):
            half = after(half, hold)
            lines.append({0: half, chip_bits[0]: exchange(half, "col", chip_bits[0])})
        near = double(own, "col", chip_bits[1:])
        ready = [have[far] for have in groups for far in have]
        hold = [step]
        for line in lines:
            far = after(line[chip_bits[0]], *hold)
            for away, block in double(far, "col", chip_bits[1:]).items():
                line[chip_bits[0] | away] = block
            hold = [*ready, line[ncols - CORES]]
        early = {}
        for far, block in near.items():
            early[far] = [block]
            early[far | 1] = [exchange(block, "col", 1)]
        late = {}
        for far in range(chip_bits[0], ncols, CORES):
            blocks = [line[far] for line in lines]
            if far < ncols - CORES:
                early[far] = blocks
                early[far | 1] = [exchange(x, "col", 1) for x in blocks]
            else:
                late[far] = blocks
        before = contract_first(early, groups, basis_count, ri_count, ncols, rows, wide)
        for far in list(late):
            upper, lower = late[far]
            late[far | 1] = [exchange(upper, "col", 1), exchange(after(lower, before[0]), "col", 1)]
        return contract_last(late, groups, before, ncols)

    return run


def first_fit(basis_count, ri_count, groups, levels):
    def body(count_ref, ri_ref, o_ref):
        level = jnp.int32(0)
        for axis, (ref, parts) in enumerate(zip((count_ref, count_ref, ri_ref), groups)):
            per = ref.shape[0] // parts
            most = jnp.int32(0)
            for g in range(parts):
                total = jnp.int32(0)
                for i in range(per):
                    total = total + ref[g * per + i]
                most = jnp.maximum(most, total)
            for n, sizes in enumerate(levels[:-1]):
                level = jnp.where(most > sizes[axis], jnp.maximum(level, n + 1), level)
        o_ref[0] = level

    return pl.pallas_call(
        body,
        out_shape=jax.ShapeDtypeStruct((1,), jnp.int32),
        in_specs=[SMEM_SPEC, SMEM_SPEC],
        out_specs=SMEM_SPEC,
        name="first_fit",
    )(basis_count, ri_count)


def shards(three_center, density, block_mask, density_mask, basis_count, ri_count):
    ncols = lax.axis_size("col")
    nrows = lax.axis_size("row")
    rows, depth = density.shape
    wide = three_center.shape[1] // ncols
    levels = (
        (rows * 3 // 4, depth * 3 // 4, wide * 5 // 6),
        (rows * 3 // 4, depth, wide * 5 // 6),
        (rows * 3 // 4, depth, wide),
        (rows, depth, wide),
    )
    level = first_fit(basis_count, ri_count, (nrows, ncols, ncols), levels)
    args = (three_center, density, block_mask, density_mask, basis_count, ri_count)
    return lax.switch(level[0], [program(*sizes) for sizes in levels], *args)


def solution(mesh):
    in_specs = (
        P(("row", "col"), None),
        P("row", "col"),
        P(("row", "col"), None),
        P("row", "col"),
        P(),
        P(),
    )
    return jax.shard_map(
        shards, mesh=mesh, in_specs=in_specs, out_specs=P("row", "col"), check_vma=False
    )
```

```python
import jax
import jax.numpy as jnp
from jax import lax
from jax.experimental import pallas as pl
from jax.experimental.pallas import tpu as pltpu
from jax.sharding import PartitionSpec as P

BW = 32
RW = 128
CORES = 2
VMEM = 48 * 1024 * 1024
BF16 = jnp.bfloat16
F32 = jnp.float32
SMEM_SPEC = pl.BlockSpec(memory_space=pltpu.SMEM)
VMEM_SPEC = pl.BlockSpec(memory_space=pltpu.VMEM)
ANY_SPEC = pl.BlockSpec(memory_space=pl.ANY)


def params(limit=VMEM):
    return pltpu.CompilerParams(vmem_limit_bytes=limit)


def cost(flops, bytes_accessed):
    return pl.CostEstimate(flops=flops, bytes_accessed=bytes_accessed, transcendentals=0)


def ones_where(cond):
    return jnp.where(cond, 1.0, 0.0).astype(BF16)


def iota(shape, axis):
    return lax.broadcasted_iota(jnp.int32, shape, axis)


def place_row(count_ref, base, atoms, width):
    lane = iota((1, atoms * width), 1)

    def atom(a, carry):
        place, offset = carry
        count = count_ref[base + a]
        inside = (lane >= a * width) & (lane < a * width + count)
        return jnp.where(inside, lane - a * width + offset, place), offset + count

    return lax.fori_loop(0, atoms, atom, (jnp.full(lane.shape, -1, jnp.int32), jnp.int32(0)))[0]


def pack_rows(count_ref, base, atoms, width, size):
    place = place_row(count_ref, base, atoms, width)
    return ones_where(iota((size, atoms * width), 0) == place)


def pack_cols(count_ref, base, atoms, width, size, out):
    def atom(a, offset):
        count = count_ref[base + a]
        slot = iota((width, size), 0)
        gap = iota((width, size), 1) - slot
        out[pl.ds(pl.multiple_of(a * width, width), width), :] = ones_where((gap == offset) & (slot < count))
        return offset + count

    lax.fori_loop(0, atoms, atom, jnp.int32(0))


def pack_integrals(tc, block_mask, basis_count, ri_count, ncols, packed, arrived=None):
    rows, cols = tc.shape
    atoms = rows // BW
    wide = cols // ncols
    blocks = wide // RW
    chips = ncols // CORES
    first = arrived is None

    def body(count_ref, ri_ref, mask_ref, x_ref, *refs):
        outs = refs[:1] if first else refs[1 : 1 + chips]
        held, hot = refs[-2:] if first else refs[-3:-1]
        made = outs[0] if first else refs[-1]
        row, col = lax.axis_index("row"), lax.axis_index("col")
        base = (row * ncols + col) * atoms

        @pl.loop(0, chips)
        def _(t):
            dest = col ^ (CORES * t + (1 if first else 0))

            @pl.loop(0, blocks)
            def _(b):
                lanes = pl.ds(pl.multiple_of(dest * wide + b * RW, RW), RW)
                slot = iota((BW, RW), 0)
                for a in range(atoms):
                    limit = jnp.where(mask_ref[a, dest * blocks + b] > 0, count_ref[base + a], 0)
                    x = x_ref[pl.ds(a * BW, BW), lanes].astype(F32)
                    at = (pl.ds(a * BW, BW), pl.ds(pl.multiple_of(b * RW, RW), RW))
                    held[at] = jnp.where(slot < limit, x, 0.0).astype(BF16)

            pack_cols(ri_ref, dest * blocks, blocks, RW, packed, hot)
            made[t] = jnp.dot(held[...], hot[...], preferred_element_type=F32).astype(BF16)

        if not first:
            core = lax.rem(col, CORES)
            for t in range(chips):
                outs[t][pl.ds(pl.multiple_of(core * rows, rows), rows), :] = made[t]
                outs[t][pl.ds(pl.multiple_of((1 - core) * rows, rows), rows), :] = refs[0][t]

    shape = (chips, rows, packed)
    merged = jax.ShapeDtypeStruct((CORES * rows, packed), BF16)
    return pl.pallas_call(
        body,
        out_shape=jax.ShapeDtypeStruct(shape, BF16) if first else [merged] * chips,
        in_specs=[SMEM_SPEC, SMEM_SPEC, SMEM_SPEC] + [VMEM_SPEC] * (1 if first else 2),
        out_specs=VMEM_SPEC if first else [VMEM_SPEC] * chips,
        scratch_shapes=[pltpu.VMEM((rows, wide), BF16), pltpu.VMEM((wide, packed), BF16)]
        + ([] if first else [pltpu.VMEM(shape, BF16)]),
        compiler_params=params(),
        cost_estimate=cost(rows * cols * packed, rows * cols + 3 * chips * rows * packed),
        name="pack_other_core" if first else "pack_own_core",
    )(basis_count, ri_count, block_mask, tc, *([] if first else [arrived]))


def pack_density(dens, mask, basis_count, lam_size, sum_size):
    rows, cols = dens.shape
    lam_atoms, sum_atoms = mask.shape
    half = lam_size // 2
    tile = rows // 4
    out_tile = lam_size // 4

    def body(count_ref, mask_ref, x_ref, o_ref, upper_ref, lower_ref, hot, keep, mid):
        row, col = lax.axis_index("row"), lax.axis_index("col")
        of_atom = ones_where(iota((sum_atoms, cols), 1) // BW == iota((sum_atoms, cols), 0))
        keep[...] = jnp.dot(ones_where(mask_ref[...] > 0), of_atom, preferred_element_type=F32).astype(BF16)
        pack_cols(count_ref, col * sum_atoms, sum_atoms, BW, sum_size, hot)

        @pl.loop(0, 4)
        def _(i):
            at = pl.ds(pl.multiple_of(i * tile, tile), tile)
            shape = (tile, lam_atoms)
            atom = ones_where((iota(shape, 0) + i * tile) // BW == iota(shape, 1))
            kept = jnp.dot(atom, keep[...], preferred_element_type=F32)
            x = jnp.where(kept > 0.5, x_ref[at, :].astype(F32), 0.0).astype(BF16)
            mid[at, :] = jnp.dot(x, hot[...], preferred_element_type=F32).astype(BF16)

        place = place_row(count_ref, row * lam_atoms, lam_atoms, BW)

        @pl.loop(0, 4)
        def _(i):
            at = pl.ds(pl.multiple_of(i * out_tile, out_tile), out_tile)
            left = ones_where(iota((out_tile, rows), 0) + i * out_tile == place)
            o_ref[at, :] = jnp.dot(left, mid[...], preferred_element_type=F32).astype(BF16)

        upper_ref[...] = o_ref[pl.ds(0, half), :]
        lower_ref[...] = o_ref[pl.ds(half, half), :]

    whole = jax.ShapeDtypeStruct((lam_size, sum_size), BF16)
    part = jax.ShapeDtypeStruct((half, sum_size), BF16)
    return pl.pallas_call(
        body,
        out_shape=[whole, part, part],
        in_specs=[SMEM_SPEC, VMEM_SPEC, VMEM_SPEC],
        out_specs=[VMEM_SPEC] * 3,
        scratch_shapes=[
            pltpu.VMEM((cols, sum_size), BF16),
            pltpu.VMEM((lam_atoms, cols), BF16),
            pltpu.VMEM((rows, sum_size), BF16),
        ],
        compiler_params=params(),
        cost_estimate=cost(2 * rows * sum_size * (cols + lam_size), 2 * rows * cols),
        name="pack_density",
    )(basis_count, mask, dens)


def pack_part(pieces, basis_count, first, ncols, size):
    rows, cols = pieces[0].shape
    per = len(pieces)
    depth = per * rows
    atoms = depth // BW

    def body(count_ref, *refs):
        blocks, o_ref, full = refs[:per], refs[per], refs[per + 1]
        row, chip = lax.axis_index("row"), lax.axis_index("col") // CORES
        for i in range(per):
            at = lax.rem(chip ^ (first + i), per) * rows
            full[pl.ds(pl.multiple_of(at, rows), rows), :] = blocks[i][...]
        part = (row * (ncols // CORES) + (chip ^ first)) * rows // depth
        hot = pack_rows(count_ref, part * atoms, atoms, BW, size)
        o_ref[...] = jnp.dot(hot, full[...], preferred_element_type=F32).astype(BF16)

    return pl.pallas_call(
        body,
        out_shape=jax.ShapeDtypeStruct((size, cols), BF16),
        in_specs=[SMEM_SPEC] + [VMEM_SPEC] * per,
        out_specs=VMEM_SPEC,
        scratch_shapes=[pltpu.VMEM((depth, cols), BF16)],
        compiler_params=params(),
        cost_estimate=cost((2 + 10 * first) * size * depth * cols, 2 * cols * (depth + size)),
        name="pack_part",
    )(basis_count, *pieces)


def exchange(x, axis, bit):
    peers = lax.axis_size(axis)
    return lax.ppermute(x, axis, [(i, i ^ bit) for i in range(peers)])


def after(x, *others):
    return lax.optimization_barrier((x, *others))[0]


def double(own, axis, bits):
    have = {0: own}
    for bit in bits:
        for far in sorted(have):
            have[far | bit] = exchange(have[far], axis, bit)
    return have


def contract_first(dens, late, integrals, basis_count, ri_count, ncols, rows, wide):
    keys = list(dens)
    chunks = [chunk for far in keys for chunk in dens[far]]
    lam, depth = sum(x.shape[0] for x in dens[keys[0]]), chunks[0].shape[1]
    groups, nrows = len(integrals), len(integrals[0])
    sums = [integrals[g][far] for far in range(nrows) for g in range(groups)]
    cols = sums[0].shape[1]
    lam_atoms, blocks = rows // BW, wide // RW
    n = len(keys)
    tile = 256

    def body(count_ref, ri_ref, *refs):
        d_refs, refs = refs[: len(chunks)], refs[len(chunks):]
        s_refs, refs = refs[: len(sums)], refs[len(sums):]
        total, lam_hot, col_hot, s_late, d_all, s_all, d_sem, s_sem, l_sem = refs
        row, col = lax.axis_index("row"), lax.axis_index("col")
        for j, ref in enumerate(s_refs):
            part = (row ^ (j // groups)) * groups + (col // (ncols // groups) ^ (j % groups))
            pltpu.make_async_copy(ref, s_all.at[part], s_sem.at[part]).start()
        copies = []
        for i, far in enumerate(keys):
            for h, chunk in enumerate(dens[far]):
                at = pl.ds(h * chunk.shape[0], chunk.shape[0])
                copies.append(
                    pltpu.make_async_copy(d_refs[len(copies)], d_all.at[i, at, :], d_sem.at[len(copies)])
                )
                copies[-1].start()
        pack_cols(count_ref, row * lam_atoms, lam_atoms, BW, lam, lam_hot)
        place = place_row(ri_ref, col * blocks, blocks, RW)

        @pl.loop(0, cols // RW)
        def _(i):
            at = pl.multiple_of(i * RW, RW)
            col_hot[pl.ds(at, RW), :] = ones_where(iota((RW, wide), 0) + at == place)

        @pl.loop(0, lam // tile)
        def _(j):
            total[pl.ds(pl.multiple_of(j * tile, tile), tile), :] = jnp.zeros((tile, cols), F32)

        @pl.loop(0, len(sums))
        def _(i):
            pltpu.make_async_copy(s_all.at[i], s_all.at[i], s_sem.at[i]).wait()

        outs = [pltpu.make_async_copy(s_all.at[col ^ far], s_late.at[i], l_sem.at[i]) for i, far in enumerate(late)]
        for copy in outs:
            copy.start()
        for copy in copies:
            copy.wait()

        @pl.loop(0, n)
        def _(far):
            @pl.loop(0, lam // tile)
            def _(j):
                out = pl.ds(pl.multiple_of(j * tile, tile), tile)
                total[out, :] += jnp.dot(d_all[far, out, :], s_all[col ^ far], preferred_element_type=F32)

        for copy in outs:
            copy.wait()

    need = 2 * (n * depth * lam + 2 * len(sums) * depth * cols + 2 * lam * cols + rows * lam + cols * wide)
    return pl.pallas_call(
        body,
        out_shape=[
            jax.ShapeDtypeStruct((lam, cols), F32),
            jax.ShapeDtypeStruct((rows, lam), BF16),
            jax.ShapeDtypeStruct((cols, wide), BF16),
            jax.ShapeDtypeStruct((len(late), depth, cols), BF16),
        ],
        in_specs=[SMEM_SPEC, SMEM_SPEC] + [ANY_SPEC] * (len(chunks) + len(sums)),
        out_specs=[VMEM_SPEC] * 4,
        scratch_shapes=[
            pltpu.VMEM((n, lam, depth), BF16),
            pltpu.VMEM((len(sums), depth, cols), BF16),
            pltpu.SemaphoreType.DMA((len(chunks),)),
            pltpu.SemaphoreType.DMA((len(sums),)),
            pltpu.SemaphoreType.DMA((len(late),)),
        ],
        compiler_params=params(need + 4 * 1024 * 1024),
        cost_estimate=cost(2 * n * depth * lam * cols, 2 * n * depth * (lam + cols)),
        name="contract_first",
    )(basis_count, ri_count, *chunks, *sums)


def contract_last(dens, before):
    chunks = [chunk for far in dens for chunk in dens[far]]
    total, lam_hot, col_hot, s_late = before
    (rows, lam), (cols, wide) = lam_hot.shape, col_hot.shape
    half, depth = chunks[0].shape
    n = len(dens)
    tile = 256

    def body(total, lam_hot, col_hot, s_late, *refs):
        d_refs = refs[: len(chunks)]
        o_ref, d_all, acc, packed, sem = refs[len(chunks):]
        copies = [
            pltpu.make_async_copy(ref, d_all.at[i // 2, pl.ds(i % 2 * half, half), :], sem.at[i])
            for i, ref in enumerate(d_refs)
        ]
        for copy in copies:
            copy.start()
        for copy in copies:
            copy.wait()

        @pl.loop(0, lam // tile)
        def _(j):
            out = pl.ds(pl.multiple_of(j * tile, tile), tile)

            acc[...] = total[out, :]

            @pl.loop(0, n)
            def _(i):
                acc[...] += jnp.dot(d_all[i, out, :], s_late[i], preferred_element_type=F32)

            x = acc[...].astype(BF16)
            packed[out, :] = jnp.dot(x, col_hot[...], preferred_element_type=F32).astype(BF16)

        @pl.loop(0, rows // tile)
        def _(j):
            out = pl.ds(pl.multiple_of(j * tile, tile), tile)
            o_ref[out, :] = jnp.dot(lam_hot[out, :], packed[...], preferred_element_type=F32).astype(BF16)

    need = 2 * (2 * n * depth * (lam + cols) + 2 * lam * cols + rows * lam + cols * wide + (lam + rows) * wide)
    return pl.pallas_call(
        body,
        out_shape=jax.ShapeDtypeStruct((rows, wide), BF16),
        in_specs=[VMEM_SPEC] * 4 + [ANY_SPEC] * len(chunks),
        out_specs=VMEM_SPEC,
        scratch_shapes=[
            pltpu.VMEM((n, lam, depth), BF16),
            pltpu.VMEM((tile, cols), F32),
            pltpu.VMEM((lam, wide), BF16),
            pltpu.SemaphoreType.DMA((len(chunks),)),
        ],
        compiler_params=params(need + 4 * 1024 * 1024),
        cost_estimate=cost(2 * n * depth * lam * cols, 2 * n * depth * (lam + cols)),
        name="contract_last",
    )(total, lam_hot, col_hot, s_late, *chunks)


def program(lam_size, sum_size, col_size):
    def run(three_center, density, block_mask, density_mask, basis_count, ri_count):
        ncols = lax.axis_size("col")
        nrows = lax.axis_size("row")
        chips = ncols // CORES
        rows, depth = density.shape
        wide = three_center.shape[1] // ncols
        row_bits = [1 << b for b in range(nrows.bit_length() - 1)]
        chip_bits = [CORES << b for b in range(chips.bit_length() - 1)][::-1]

        counts = (block_mask, basis_count, ri_count, ncols, col_size)
        other = exchange(pack_integrals(three_center, *counts), "col", 1)
        own, *halves = pack_density(density, density_mask, basis_count, lam_size, sum_size)
        pieces = pack_integrals(three_center, *counts, after(other, own))
        got = [pieces[0]] + [exchange(pieces[t], "col", CORES * t) for t in range(1, chips)]
        per = depth // pieces[0].shape[0]
        parts, groups = [], []
        for g in range(chips // per):
            part = pack_part(got[g * per : (g + 1) * per], basis_count, g * per, ncols, sum_size)
            if g > 0:
                part = after(part, *[groups[0][bit] for bit in row_bits])
            parts.append(part)
            groups.append(double(part, "row", row_bits if g % 2 == 0 else row_bits[::-1]))
        own = after(own, parts[-1])
        step = groups[-1][row_bits[-1]]
        lines = []
        for half, hold in zip(halves, (parts[-1], step)):
            half = after(half, hold)
            lines.append({0: half, chip_bits[0]: exchange(half, "col", chip_bits[0])})
        near = double(own, "col", chip_bits[1:])
        ready = [have[far] for have in groups for far in have]
        hold = [step]
        for line in lines:
            far = after(line[chip_bits[0]], *hold)
            for away, block in double(far, "col", chip_bits[1:]).items():
                line[chip_bits[0] | away] = block
            hold = [*ready, line[ncols - CORES]]
        early = {}
        for far, block in near.items():
            early[far] = [block]
            early[far | 1] = [exchange(block, "col", 1)]
        late = {}
        for far in range(chip_bits[0], ncols, CORES):
            blocks = [line[far] for line in lines]
            if far < ncols - CORES:
                early[far] = blocks
                early[far | 1] = [exchange(x, "col", 1) for x in blocks]
            else:
                late[far] = blocks
        early = {far: early[far] for far in sorted(early)}
        before = contract_first(
            early, [ncols - CORES, ncols - 1], groups, basis_count, ri_count, ncols, rows, wide
        )
        for far in list(late):
            upper, lower = late[far]
            late[far | 1] = [exchange(upper, "col", 1), exchange(after(lower, before[0]), "col", 1)]
        return contract_last(late, before)

    return run


def first_fit(basis_count, ri_count, groups, levels):
    def body(count_ref, ri_ref, o_ref):
        level = jnp.int32(0)
        for axis, (ref, parts) in enumerate(zip((count_ref, count_ref, ri_ref), groups)):
            per = ref.shape[0] // parts
            most = jnp.int32(0)
            for g in range(parts):
                total = jnp.int32(0)
                for i in range(per):
                    total = total + ref[g * per + i]
                most = jnp.maximum(most, total)
            for n, sizes in enumerate(levels[:-1]):
                level = jnp.where(most > sizes[axis], jnp.maximum(level, n + 1), level)
        o_ref[0] = level

    return pl.pallas_call(
        body,
        out_shape=jax.ShapeDtypeStruct((1,), jnp.int32),
        in_specs=[SMEM_SPEC, SMEM_SPEC],
        out_specs=SMEM_SPEC,
        name="first_fit",
    )(basis_count, ri_count)


def shards(three_center, density, block_mask, density_mask, basis_count, ri_count):
    ncols = lax.axis_size("col")
    nrows = lax.axis_size("row")
    rows, depth = density.shape
    wide = three_center.shape[1] // ncols
    levels = (
        (rows * 3 // 4, depth * 3 // 4, wide * 5 // 6),
        (rows * 3 // 4, depth, wide * 5 // 6),
        (rows * 3 // 4, depth, wide),
        (rows, depth, wide),
    )
    level = first_fit(basis_count, ri_count, (nrows, ncols, ncols), levels)
    args = (three_center, density, block_mask, density_mask, basis_count, ri_count)
    return lax.switch(level[0], [program(*sizes) for sizes in levels], *args)


def solution(mesh):
    in_specs = (
        P(("row", "col"), None),
        P("row", "col"),
        P(("row", "col"), None),
        P("row", "col"),
        P(),
        P(),
    )
    return jax.shard_map(
        shards, mesh=mesh, in_specs=in_specs, out_specs=P("row", "col"), check_vma=False
    )
```

```python
import jax
import jax.numpy as jnp
from jax import lax
from jax.experimental import pallas as pl
from jax.experimental.pallas import tpu as pltpu
from jax.sharding import PartitionSpec as P

BW = 32
RW = 128
CORES = 2
VMEM = 48 * 1024 * 1024
BF16 = jnp.bfloat16
F32 = jnp.float32
SMEM_SPEC = pl.BlockSpec(memory_space=pltpu.SMEM)
VMEM_SPEC = pl.BlockSpec(memory_space=pltpu.VMEM)
ANY_SPEC = pl.BlockSpec(memory_space=pl.ANY)


def params(limit=VMEM):
    return pltpu.CompilerParams(vmem_limit_bytes=limit)


def cost(flops, bytes_accessed):
    return pl.CostEstimate(flops=flops, bytes_accessed=bytes_accessed, transcendentals=0)


def ones_where(cond):
    return jnp.where(cond, 1.0, 0.0).astype(BF16)


def iota(shape, axis):
    return lax.broadcasted_iota(jnp.int32, shape, axis)


def loop(n, unroll):
    def run(f):
        if unroll:
            for i in range(n):
                f(i)
        else:
            pl.loop(0, n)(f)

    return run


def span(i, size):
    return pl.ds(i * size if isinstance(i, int) else pl.multiple_of(i * size, size), size)


def place_row(count_ref, base, atoms, width):
    lane = iota((1, atoms * width), 1)

    def atom(a, carry):
        place, offset = carry
        count = count_ref[base + a]
        inside = (lane >= a * width) & (lane < a * width + count)
        return jnp.where(inside, lane - a * width + offset, place), offset + count

    return lax.fori_loop(0, atoms, atom, (jnp.full(lane.shape, -1, jnp.int32), jnp.int32(0)))[0]


def pack_rows(count_ref, base, atoms, width, size):
    place = place_row(count_ref, base, atoms, width)
    return ones_where(iota((size, atoms * width), 0) == place)


def pack_cols(count_ref, base, atoms, width, size, out, unroll):
    def atom(a, offset):
        count = count_ref[base + a]
        slot = iota((width, size), 0)
        gap = iota((width, size), 1) - slot
        out[span(a, width), :] = ones_where((gap == offset) & (slot < count))
        return offset + count

    if unroll:
        offset = jnp.int32(0)
        for a in range(atoms):
            offset = atom(a, offset)
    else:
        lax.fori_loop(0, atoms, atom, jnp.int32(0))


def pack_integrals(tc, block_mask, basis_count, ri_count, ncols, packed, unroll, arrived=None):
    rows, cols = tc.shape
    atoms = rows // BW
    wide = cols // ncols
    blocks = wide // RW
    chips = ncols // CORES
    first = arrived is None

    def body(count_ref, ri_ref, mask_ref, x_ref, *refs):
        outs = refs[:1] if first else refs[1 : 1 + chips]
        held, hot = refs[-2:] if first else refs[-3:-1]
        made = outs[0] if first else refs[-1]
        row, col = lax.axis_index("row"), lax.axis_index("col")
        base = (row * ncols + col) * atoms

        @loop(chips, unroll)
        def _(t):
            dest = col ^ (CORES * t + (1 if first else 0))

            @loop(blocks, unroll)
            def _(b):
                lanes = pl.ds(pl.multiple_of(dest * wide + b * RW, RW), RW)
                slot = iota((BW, RW), 0)
                for a in range(atoms):
                    limit = jnp.where(mask_ref[a, dest * blocks + b] > 0, count_ref[base + a], 0)
                    x = x_ref[pl.ds(a * BW, BW), lanes].astype(F32)
                    held[pl.ds(a * BW, BW), span(b, RW)] = jnp.where(slot < limit, x, 0.0).astype(BF16)

            pack_cols(ri_ref, dest * blocks, blocks, RW, packed, hot, unroll)
            made[t] = jnp.dot(held[...], hot[...], preferred_element_type=F32).astype(BF16)

        if not first:
            core = lax.rem(col, CORES)
            for t in range(chips):
                outs[t][pl.ds(pl.multiple_of(core * rows, rows), rows), :] = made[t]
                outs[t][pl.ds(pl.multiple_of((1 - core) * rows, rows), rows), :] = refs[0][t]

    shape = (chips, rows, packed)
    merged = jax.ShapeDtypeStruct((CORES * rows, packed), BF16)
    return pl.pallas_call(
        body,
        out_shape=jax.ShapeDtypeStruct(shape, BF16) if first else [merged] * chips,
        in_specs=[SMEM_SPEC, SMEM_SPEC, SMEM_SPEC] + [VMEM_SPEC] * (1 if first else 2),
        out_specs=VMEM_SPEC if first else [VMEM_SPEC] * chips,
        scratch_shapes=[pltpu.VMEM((rows, wide), BF16), pltpu.VMEM((wide, packed), BF16)]
        + ([] if first else [pltpu.VMEM(shape, BF16)]),
        compiler_params=params(),
        cost_estimate=cost(rows * cols * packed, rows * cols + 3 * chips * rows * packed),
        name="pack_other_core" if first else "pack_own_core",
    )(basis_count, ri_count, block_mask, tc, *([] if first else [arrived]))


def pack_density(dens, mask, basis_count, lam_size, sum_size, unroll):
    rows, cols = dens.shape
    lam_atoms, sum_atoms = mask.shape
    half = lam_size // 2
    tile = rows // 4
    out_tile = lam_size // 4

    def body(count_ref, mask_ref, x_ref, o_ref, upper_ref, lower_ref, hot, keep, mid):
        row, col = lax.axis_index("row"), lax.axis_index("col")
        of_atom = ones_where(iota((sum_atoms, cols), 1) // BW == iota((sum_atoms, cols), 0))
        keep[...] = jnp.dot(ones_where(mask_ref[...] > 0), of_atom, preferred_element_type=F32).astype(BF16)
        pack_cols(count_ref, col * sum_atoms, sum_atoms, BW, sum_size, hot, unroll)

        @loop(4, unroll)
        def _(i):
            at = span(i, tile)
            shape = (tile, lam_atoms)
            atom = ones_where((iota(shape, 0) + i * tile) // BW == iota(shape, 1))
            kept = jnp.dot(atom, keep[...], preferred_element_type=F32)
            x = jnp.where(kept > 0.5, x_ref[at, :].astype(F32), 0.0).astype(BF16)
            mid[at, :] = jnp.dot(x, hot[...], preferred_element_type=F32).astype(BF16)

        place = place_row(count_ref, row * lam_atoms, lam_atoms, BW)

        @loop(4, unroll)
        def _(i):
            at = span(i, out_tile)
            left = ones_where(iota((out_tile, rows), 0) + i * out_tile == place)
            o_ref[at, :] = jnp.dot(left, mid[...], preferred_element_type=F32).astype(BF16)

        upper_ref[...] = o_ref[pl.ds(0, half), :]
        lower_ref[...] = o_ref[pl.ds(half, half), :]

    whole = jax.ShapeDtypeStruct((lam_size, sum_size), BF16)
    part = jax.ShapeDtypeStruct((half, sum_size), BF16)
    return pl.pallas_call(
        body,
        out_shape=[whole, part, part],
        in_specs=[SMEM_SPEC, VMEM_SPEC, VMEM_SPEC],
        out_specs=[VMEM_SPEC] * 3,
        scratch_shapes=[
            pltpu.VMEM((cols, sum_size), BF16),
            pltpu.VMEM((lam_atoms, cols), BF16),
            pltpu.VMEM((rows, sum_size), BF16),
        ],
        compiler_params=params(),
        cost_estimate=cost(2 * rows * sum_size * (cols + lam_size), 2 * rows * cols),
        name="pack_density",
    )(basis_count, mask, dens)


def pack_part(pieces, basis_count, first, ncols, size):
    rows, cols = pieces[0].shape
    per = len(pieces)
    depth = per * rows
    atoms = depth // BW

    def body(count_ref, *refs):
        blocks, o_ref, full = refs[:per], refs[per], refs[per + 1]
        row, chip = lax.axis_index("row"), lax.axis_index("col") // CORES
        for i in range(per):
            at = lax.rem(chip ^ (first + i), per) * rows
            full[pl.ds(pl.multiple_of(at, rows), rows), :] = blocks[i][...]
        part = (row * (ncols // CORES) + (chip ^ first)) * rows // depth
        hot = pack_rows(count_ref, part * atoms, atoms, BW, size)
        o_ref[...] = jnp.dot(hot, full[...], preferred_element_type=F32).astype(BF16)

    return pl.pallas_call(
        body,
        out_shape=jax.ShapeDtypeStruct((size, cols), BF16),
        in_specs=[SMEM_SPEC] + [VMEM_SPEC] * per,
        out_specs=VMEM_SPEC,
        scratch_shapes=[pltpu.VMEM((depth, cols), BF16)],
        compiler_params=params(),
        cost_estimate=cost((2 + 10 * first) * size * depth * cols, 2 * cols * (depth + size)),
        name="pack_part",
    )(basis_count, *pieces)


def exchange(x, axis, bit):
    peers = lax.axis_size(axis)
    return lax.ppermute(x, axis, [(i, i ^ bit) for i in range(peers)])


def after(x, *others):
    return lax.optimization_barrier((x, *others))[0]


def double(own, axis, bits):
    have = {0: own}
    for bit in bits:
        for far in sorted(have):
            have[far | bit] = exchange(have[far], axis, bit)
    return have


def add_parts(total, tile, unroll, d_refs, sums, before=None):
    lam, cols = total.shape

    @loop(lam // tile, unroll)
    def _(j):
        out = span(j, tile)
        x = None if before is None else before[out, :]
        for chunks, part in zip(d_refs, sums):
            if len(chunks) == 1:
                d = chunks[0][out, :]
            elif isinstance(j, int):
                size = chunks[0].shape[0]
                d = chunks[j * tile // size][pl.ds(j * tile % size, tile), :]
            else:
                per = chunks[0].shape[0] // tile
                inner = span(lax.rem(j, per), tile)
                d = jnp.where(j < per, chunks[0][inner, :].astype(F32), chunks[1][inner, :].astype(F32)).astype(BF16)
            y = jnp.dot(d, part(), preferred_element_type=F32)
            x = y if x is None else x + y
        total[out, :] = x


def split_refs(dens, refs):
    lists, at = [], 0
    for chunks in dens.values():
        lists.append(refs[at : at + len(chunks)])
        at += len(chunks)
    return lists, refs[at:]


def flat(dens):
    return [chunk for chunks in dens.values() for chunk in chunks]


def contract_near(dens, integrals, basis_count, ri_count, ncols, rows, wide, unroll):
    lam, depth = dens[0][0].shape
    groups, nrows = len(integrals), len(integrals[0])
    sums = [integrals[g][far] for far in range(nrows) for g in range(groups)]
    cols = sums[0].shape[1]
    lam_atoms, blocks = rows // BW, wide // RW
    n, parts = len(dens), len(sums)

    def body(count_ref, ri_ref, *refs):
        d_refs, refs = split_refs(dens, refs)
        s_refs, refs = refs[:parts], refs[parts:]
        total, lam_hot, col_hot, s_rest, s_all, s_sem, r_sem = refs
        row, col = lax.axis_index("row"), lax.axis_index("col")
        for j, ref in enumerate(s_refs):
            part = (row ^ (j // groups)) * groups + (col // (ncols // groups) ^ (j % groups))
            pltpu.make_async_copy(ref, s_all.at[part], s_sem.at[part]).start()
        pack_cols(count_ref, row * lam_atoms, lam_atoms, BW, lam, lam_hot, unroll)
        place = place_row(ri_ref, col * blocks, blocks, RW)

        @loop(cols // RW, unroll)
        def _(i):
            col_hot[span(i, RW), :] = ones_where(iota((RW, wide), 0) + i * RW == place)

        @pl.loop(0, parts)
        def _(i):
            pltpu.make_async_copy(s_all.at[i], s_all.at[i], s_sem.at[i]).wait()

        rest = [pltpu.make_async_copy(s_all.at[col ^ far], s_rest.at[far - n], r_sem.at[far - n]) for far in range(n, parts)]
        for copy in rest:
            copy.start()
        add_parts(total, lam // 2, unroll, d_refs, [lambda far=far: s_all[col ^ far] for far in range(n)])
        for copy in rest:
            copy.wait()

    need = 2 * (n * depth * lam + 2 * parts * depth * cols + 4 * lam * cols + rows * lam + cols * wide)
    return pl.pallas_call(
        body,
        out_shape=[
            jax.ShapeDtypeStruct((lam, cols), F32),
            jax.ShapeDtypeStruct((rows, lam), BF16),
            jax.ShapeDtypeStruct((cols, wide), BF16),
            jax.ShapeDtypeStruct((parts - n, depth, cols), BF16),
        ],
        in_specs=[SMEM_SPEC, SMEM_SPEC] + [VMEM_SPEC] * n + [ANY_SPEC] * parts,
        out_specs=[VMEM_SPEC] * 4,
        scratch_shapes=[
            pltpu.VMEM((parts, depth, cols), BF16),
            pltpu.SemaphoreType.DMA((parts,)),
            pltpu.SemaphoreType.DMA((parts - n,)),
        ],
        compiler_params=params(need + 4 * 1024 * 1024),
        cost_estimate=cost(2 * n * depth * lam * cols, 2 * n * depth * (lam + cols)),
        name="contract_near",
    )(basis_count, ri_count, *flat(dens), *sums)


def contract_far(dens, first, total, sums, unroll):
    (lam, cols), depth = total.shape, sums.shape[1]
    n = len(dens)

    def body(before, s_ref, *refs):
        d_refs, (o_ref,) = split_refs(dens, refs)
        add_parts(o_ref, lam // 2, unroll, d_refs, [lambda i=i: s_ref[first + i] for i in range(n)], before)

    need = 2 * (n * depth * lam + sums.size + 4 * lam * cols)
    return pl.pallas_call(
        body,
        out_shape=jax.ShapeDtypeStruct((lam, cols), F32),
        in_specs=[VMEM_SPEC] * (2 + len(flat(dens))),
        out_specs=VMEM_SPEC,
        compiler_params=params(need + 4 * 1024 * 1024),
        cost_estimate=cost(2 * n * depth * lam * cols, 2 * n * depth * (lam + cols)),
        name="contract_far",
    )(total, sums, *flat(dens))


def contract_last(dens, first, total, sums, lam_hot, col_hot, unroll):
    (rows, lam), (cols, wide) = lam_hot.shape, col_hot.shape
    depth = sums.shape[1]
    n = len(dens)
    half = lam // 2

    def body(before, s_ref, lam_hot, col_hot, *refs):
        d_refs, (o_ref, total, packed) = split_refs(dens, refs)
        add_parts(total, half, unroll, d_refs, [lambda i=i: s_ref[first + i] for i in range(n)], before)

        @loop(2, unroll)
        def _(j):
            x = total[span(j, half), :].astype(BF16)
            packed[span(j, half), :] = jnp.dot(x, col_hot[...], preferred_element_type=F32).astype(BF16)

        @loop(4, unroll)
        def _(j):
            out = span(j, rows // 4)
            o_ref[out, :] = jnp.dot(lam_hot[out, :], packed[...], preferred_element_type=F32).astype(BF16)

    need = 2 * (n * depth * lam + sums.size + 4 * lam * cols + rows * lam + cols * wide + (lam + rows) * wide)
    return pl.pallas_call(
        body,
        out_shape=jax.ShapeDtypeStruct((rows, wide), BF16),
        in_specs=[VMEM_SPEC] * (4 + len(flat(dens))),
        out_specs=VMEM_SPEC,
        scratch_shapes=[pltpu.VMEM((lam, cols), F32), pltpu.VMEM((lam, wide), BF16)],
        compiler_params=params(need + 4 * 1024 * 1024),
        cost_estimate=cost(2 * n * depth * lam * cols, 2 * n * depth * (lam + cols)),
        name="contract_last",
    )(total, sums, lam_hot, col_hot, *flat(dens))


def program(lam_size, sum_size, col_size, unroll):
    def run(three_center, density, block_mask, density_mask, basis_count, ri_count):
        ncols = lax.axis_size("col")
        nrows = lax.axis_size("row")
        chips = ncols // CORES
        rows, depth = density.shape
        wide = three_center.shape[1] // ncols
        row_bits = [1 << b for b in range(nrows.bit_length() - 1)]
        chip_bits = [CORES << b for b in range(chips.bit_length() - 1)][::-1]
        far_bit, near_bits = chip_bits[0], chip_bits[1:]

        counts = (block_mask, basis_count, ri_count, ncols, col_size, unroll)
        other = exchange(pack_integrals(three_center, *counts), "col", 1)
        own, *halves = pack_density(density, density_mask, basis_count, lam_size, sum_size, unroll)
        near = double(own, "col", near_bits)
        near[1] = exchange(own, "col", 1)
        pieces = pack_integrals(three_center, *counts, after(other, own))
        got = [pieces[0]] + [exchange(pieces[t], "col", CORES * t) for t in range(1, chips)]
        per = depth // pieces[0].shape[0]
        parts, groups = [], []
        for g in range(chips // per):
            arrived = got[g * per : (g + 1) * per]
            if g == 0:
                arrived = [after(arrived[0], *near.values())] + arrived[1:]
            part = pack_part(arrived, basis_count, g * per, ncols, sum_size)
            if g > 0:
                part = after(part, *[groups[0][bit] for bit in row_bits])
            parts.append(part)
            groups.append({0: part})
            bits = row_bits if g % 2 == 0 else row_bits[::-1]
            for bit in bits:
                groups[g][bit] = exchange(part, "row", bit)
        step = groups[-1][row_bits[-1]]
        for g, have in enumerate(groups):
            bits = row_bits if g % 2 == 0 else row_bits[::-1]
            done = [0, bits[0]]
            for bit in bits[1:]:
                for far in done[1:]:
                    block = have[far] if g == len(groups) - 1 else after(have[far], step)
                    have[far | bit] = exchange(block, "row", bit)
                done += [far | bit for far in done]
        for far in [far for far in near if far > 1]:
            near[far | 1] = exchange(after(near[far], parts[-1]), "col", 1)
        lines = []
        for half, hold in zip(halves, ([parts[-1]], [step, *near.values()])):
            half = after(half, *hold)
            lines.append({0: half, far_bit: exchange(half, "col", far_bit)})
        ready = [have[far] for have in groups for far in have]
        hold = [step]
        for line in lines:
            far = after(line[far_bit], *hold)
            for away, block in double(far, "col", near_bits).items():
                line[far_bit | away] = block
            hold = [*ready, line[ncols - CORES]]

        first = {far: [near[far]] for far in sorted(near)}
        total, lam_hot, col_hot, sums = contract_near(
            first, groups, basis_count, ri_count, ncols, rows, wide, unroll
        )
        middle, last = {}, {}
        for far in range(far_bit, ncols, CORES):
            blocks = [line[far] for line in lines]
            if far < ncols - CORES:
                middle[far] = blocks
                middle[far | 1] = [exchange(x, "col", 1) for x in blocks]
            else:
                last[far] = blocks
        total = contract_far(middle, 0, total, sums, unroll)
        upper, lower = last[ncols - CORES]
        last[ncols - 1] = [exchange(upper, "col", 1), exchange(after(lower, total), "col", 1)]
        return contract_last(last, len(middle), total, sums, lam_hot, col_hot, unroll)

    return run


def first_fit(basis_count, ri_count, groups, levels):
    def body(count_ref, ri_ref, o_ref):
        level = jnp.int32(0)
        for axis, (ref, parts) in enumerate(zip((count_ref, count_ref, ri_ref), groups)):
            per = ref.shape[0] // parts
            most = jnp.int32(0)
            for g in range(parts):
                total = jnp.int32(0)
                for i in range(per):
                    total = total + ref[g * per + i]
                most = jnp.maximum(most, total)
            for n, sizes in enumerate(levels[:-1]):
                level = jnp.where(most > sizes[axis], jnp.maximum(level, n + 1), level)
        o_ref[0] = level

    return pl.pallas_call(
        body,
        out_shape=jax.ShapeDtypeStruct((1,), jnp.int32),
        in_specs=[SMEM_SPEC, SMEM_SPEC],
        out_specs=SMEM_SPEC,
        name="first_fit",
    )(basis_count, ri_count)


def shards(three_center, density, block_mask, density_mask, basis_count, ri_count):
    ncols = lax.axis_size("col")
    nrows = lax.axis_size("row")
    rows, depth = density.shape
    wide = three_center.shape[1] // ncols
    levels = (
        (rows * 3 // 4, depth * 3 // 4, wide * 5 // 6),
        (rows * 3 // 4, depth, wide * 5 // 6),
        (rows * 3 // 4, depth, wide),
        (rows, depth, wide),
    )
    level = first_fit(basis_count, ri_count, (nrows, ncols, ncols), levels)
    args = (three_center, density, block_mask, density_mask, basis_count, ri_count)
    return lax.switch(level[0], [program(*sizes, sizes == levels[0]) for sizes in levels], *args)


def solution(mesh):
    in_specs = (
        P(("row", "col"), None),
        P("row", "col"),
        P(("row", "col"), None),
        P("row", "col"),
        P(),
        P(),
    )
    return jax.shard_map(
        shards, mesh=mesh, in_specs=in_specs, out_specs=P("row", "col"), check_vma=False
    )
```

```python
import jax
import jax.numpy as jnp
from jax import lax
from jax.experimental import pallas as pl
from jax.experimental.pallas import tpu as pltpu
from jax.sharding import PartitionSpec as P

BW = 32
RW = 128
CORES = 2
VMEM = 48 * 1024 * 1024
BF16 = jnp.bfloat16
F32 = jnp.float32
SMEM_SPEC = pl.BlockSpec(memory_space=pltpu.SMEM)
VMEM_SPEC = pl.BlockSpec(memory_space=pltpu.VMEM)
ANY_SPEC = pl.BlockSpec(memory_space=pl.ANY)


def params(limit=VMEM):
    return pltpu.CompilerParams(vmem_limit_bytes=limit)


def cost(flops, bytes_accessed):
    return pl.CostEstimate(flops=flops, bytes_accessed=bytes_accessed, transcendentals=0)


def ones_where(cond):
    return jnp.where(cond, 1.0, 0.0).astype(BF16)


def iota(shape, axis):
    return lax.broadcasted_iota(jnp.int32, shape, axis)


def loop(n, unroll):
    def run(f):
        if unroll:
            for i in range(n):
                f(i)
        else:
            pl.loop(0, n)(f)

    return run


def span(i, size):
    return pl.ds(i * size if isinstance(i, int) else pl.multiple_of(i * size, size), size)


def place_row(count_ref, base, atoms, width):
    lane = iota((1, atoms * width), 1)

    def atom(a, carry):
        place, offset = carry
        count = count_ref[base + a]
        inside = (lane >= a * width) & (lane < a * width + count)
        return jnp.where(inside, lane - a * width + offset, place), offset + count

    return lax.fori_loop(0, atoms, atom, (jnp.full(lane.shape, -1, jnp.int32), jnp.int32(0)))[0]


def pack_rows(count_ref, base, atoms, width, size):
    place = place_row(count_ref, base, atoms, width)
    return ones_where(iota((size, atoms * width), 0) == place)


def pack_cols(count_ref, base, atoms, width, size, out, unroll):
    def atom(a, offset):
        count = count_ref[base + a]
        slot = iota((width, size), 0)
        gap = iota((width, size), 1) - slot
        out[span(a, width), :] = ones_where((gap == offset) & (slot < count))
        return offset + count

    if unroll:
        offset = jnp.int32(0)
        for a in range(atoms):
            offset = atom(a, offset)
    else:
        lax.fori_loop(0, atoms, atom, jnp.int32(0))


def pack_integrals(tc, block_mask, basis_count, ri_count, ncols, packed, unroll, arrived=None):
    rows, cols = tc.shape
    atoms = rows // BW
    wide = cols // ncols
    blocks = wide // RW
    chips = ncols // CORES
    first = arrived is None

    def body(count_ref, ri_ref, mask_ref, x_ref, *refs):
        outs = refs[:1] if first else refs[1 : 1 + chips]
        held, hot = refs[-2:] if first else refs[-3:-1]
        made = outs[0] if first else refs[-1]
        row, col = lax.axis_index("row"), lax.axis_index("col")
        base = (row * ncols + col) * atoms

        @loop(chips, unroll)
        def _(t):
            dest = col ^ (CORES * t + (1 if first else 0))

            @loop(blocks, unroll)
            def _(b):
                lanes = pl.ds(pl.multiple_of(dest * wide + b * RW, RW), RW)
                slot = iota((BW, RW), 0)
                for a in range(atoms):
                    limit = jnp.where(mask_ref[a, dest * blocks + b] > 0, count_ref[base + a], 0)
                    x = x_ref[pl.ds(a * BW, BW), lanes].astype(F32)
                    held[pl.ds(a * BW, BW), span(b, RW)] = jnp.where(slot < limit, x, 0.0).astype(BF16)

            pack_cols(ri_ref, dest * blocks, blocks, RW, packed, hot, unroll)
            made[t] = jnp.dot(held[...], hot[...], preferred_element_type=F32).astype(BF16)

        if not first:
            core = lax.rem(col, CORES)
            for t in range(chips):
                outs[t][pl.ds(pl.multiple_of(core * rows, rows), rows), :] = made[t]
                outs[t][pl.ds(pl.multiple_of((1 - core) * rows, rows), rows), :] = refs[0][t]

    shape = (chips, rows, packed)
    merged = jax.ShapeDtypeStruct((CORES * rows, packed), BF16)
    return pl.pallas_call(
        body,
        out_shape=jax.ShapeDtypeStruct(shape, BF16) if first else [merged] * chips,
        in_specs=[SMEM_SPEC, SMEM_SPEC, SMEM_SPEC] + [VMEM_SPEC] * (1 if first else 2),
        out_specs=VMEM_SPEC if first else [VMEM_SPEC] * chips,
        scratch_shapes=[pltpu.VMEM((rows, wide), BF16), pltpu.VMEM((wide, packed), BF16)]
        + ([] if first else [pltpu.VMEM(shape, BF16)]),
        compiler_params=params(),
        cost_estimate=cost(rows * cols * packed, rows * cols + 3 * chips * rows * packed),
        name="pack_other_core" if first else "pack_own_core",
    )(basis_count, ri_count, block_mask, tc, *([] if first else [arrived]))


def pack_density(dens, mask, basis_count, lam_size, sum_size, unroll):
    rows, cols = dens.shape
    lam_atoms, sum_atoms = mask.shape
    half = lam_size // 2
    tile = rows // 4
    out_tile = lam_size // 4

    def body(count_ref, mask_ref, x_ref, o_ref, upper_ref, lower_ref, hot, keep, mid):
        row, col = lax.axis_index("row"), lax.axis_index("col")
        of_atom = ones_where(iota((sum_atoms, cols), 1) // BW == iota((sum_atoms, cols), 0))
        keep[...] = jnp.dot(ones_where(mask_ref[...] > 0), of_atom, preferred_element_type=F32).astype(BF16)
        pack_cols(count_ref, col * sum_atoms, sum_atoms, BW, sum_size, hot, unroll)

        @loop(4, unroll)
        def _(i):
            at = span(i, tile)
            shape = (tile, lam_atoms)
            atom = ones_where((iota(shape, 0) + i * tile) // BW == iota(shape, 1))
            kept = jnp.dot(atom, keep[...], preferred_element_type=F32)
            x = jnp.where(kept > 0.5, x_ref[at, :].astype(F32), 0.0).astype(BF16)
            mid[at, :] = jnp.dot(x, hot[...], preferred_element_type=F32).astype(BF16)

        place = place_row(count_ref, row * lam_atoms, lam_atoms, BW)

        @loop(4, unroll)
        def _(i):
            at = span(i, out_tile)
            left = ones_where(iota((out_tile, rows), 0) + i * out_tile == place)
            o_ref[at, :] = jnp.dot(left, mid[...], preferred_element_type=F32).astype(BF16)

        upper_ref[...] = o_ref[pl.ds(0, half), :]
        lower_ref[...] = o_ref[pl.ds(half, half), :]

    whole = jax.ShapeDtypeStruct((lam_size, sum_size), BF16)
    part = jax.ShapeDtypeStruct((half, sum_size), BF16)
    return pl.pallas_call(
        body,
        out_shape=[whole, part, part],
        in_specs=[SMEM_SPEC, VMEM_SPEC, VMEM_SPEC],
        out_specs=[VMEM_SPEC] * 3,
        scratch_shapes=[
            pltpu.VMEM((cols, sum_size), BF16),
            pltpu.VMEM((lam_atoms, cols), BF16),
            pltpu.VMEM((rows, sum_size), BF16),
        ],
        compiler_params=params(),
        cost_estimate=cost(2 * rows * sum_size * (cols + lam_size), 2 * rows * cols),
        name="pack_density",
    )(basis_count, mask, dens)


def pack_part(pieces, basis_count, first, ncols, size):
    rows, cols = pieces[0].shape
    per = len(pieces)
    depth = per * rows
    atoms = depth // BW

    def body(count_ref, *refs):
        blocks, o_ref, full = refs[:per], refs[per], refs[per + 1]
        row, chip = lax.axis_index("row"), lax.axis_index("col") // CORES
        for i in range(per):
            at = lax.rem(chip ^ (first + i), per) * rows
            full[pl.ds(pl.multiple_of(at, rows), rows), :] = blocks[i][...]
        part = (row * (ncols // CORES) + (chip ^ first)) * rows // depth
        hot = pack_rows(count_ref, part * atoms, atoms, BW, size)
        o_ref[...] = jnp.dot(hot, full[...], preferred_element_type=F32).astype(BF16)

    return pl.pallas_call(
        body,
        out_shape=jax.ShapeDtypeStruct((size, cols), BF16),
        in_specs=[SMEM_SPEC] + [VMEM_SPEC] * per,
        out_specs=VMEM_SPEC,
        scratch_shapes=[pltpu.VMEM((depth, cols), BF16)],
        compiler_params=params(),
        cost_estimate=cost((2 + 10 * first) * size * depth * cols, 2 * cols * (depth + size)),
        name="pack_part",
    )(basis_count, *pieces)


def exchange(x, axis, bit):
    peers = lax.axis_size(axis)
    return lax.ppermute(x, axis, [(i, i ^ bit) for i in range(peers)])


def after(x, *others):
    return lax.optimization_barrier((x, *others))[0]


def double(own, axis, bits):
    have = {0: own}
    for bit in bits:
        for far in sorted(have):
            have[far | bit] = exchange(have[far], axis, bit)
    return have


def add_parts(total, tile, unroll, d_refs, sums, before=None):
    lam, cols = total.shape

    @loop(lam // tile, unroll)
    def _(j):
        out = span(j, tile)
        x = None if before is None else before[out, :]
        for chunks, part in zip(d_refs, sums):
            if len(chunks) == 1:
                d = chunks[0][out, :]
            elif isinstance(j, int):
                size = chunks[0].shape[0]
                d = chunks[j * tile // size][pl.ds(j * tile % size, tile), :]
            else:
                per = chunks[0].shape[0] // tile
                inner = span(lax.rem(j, per), tile)
                d = jnp.where(j < per, chunks[0][inner, :].astype(F32), chunks[1][inner, :].astype(F32)).astype(BF16)
            y = jnp.dot(d, part(), preferred_element_type=F32)
            x = y if x is None else x + y
        total[out, :] = x


def split_refs(dens, refs):
    lists, at = [], 0
    for chunks in dens.values():
        lists.append(refs[at : at + len(chunks)])
        at += len(chunks)
    return lists, refs[at:]


def flat(dens):
    return [chunk for chunks in dens.values() for chunk in chunks]


def contract_near(dens, integrals, basis_count, ri_count, ncols, rows, wide, unroll):
    lam, depth = dens[0][0].shape
    groups, nrows = len(integrals), len(integrals[0])
    sums = [integrals[g][far] for far in range(nrows) for g in range(groups)]
    cols = sums[0].shape[1]
    lam_atoms, blocks = rows // BW, wide // RW
    n, parts = len(dens), len(sums)

    def body(count_ref, ri_ref, *refs):
        d_refs, refs = split_refs(dens, refs)
        s_refs, refs = refs[:parts], refs[parts:]
        total, lam_hot, col_hot, s_rest, s_all, s_sem, r_sem = refs
        row, col = lax.axis_index("row"), lax.axis_index("col")
        for j, ref in enumerate(s_refs):
            part = (row ^ (j // groups)) * groups + (col // (ncols // groups) ^ (j % groups))
            pltpu.make_async_copy(ref, s_all.at[part], s_sem.at[part]).start()
        pack_cols(count_ref, row * lam_atoms, lam_atoms, BW, lam, lam_hot, unroll)
        place = place_row(ri_ref, col * blocks, blocks, RW)

        @loop(cols // RW, unroll)
        def _(i):
            col_hot[span(i, RW), :] = ones_where(iota((RW, wide), 0) + i * RW == place)

        @pl.loop(0, parts)
        def _(i):
            pltpu.make_async_copy(s_all.at[i], s_all.at[i], s_sem.at[i]).wait()

        rest = [pltpu.make_async_copy(s_all.at[col ^ far], s_rest.at[far - n], r_sem.at[far - n]) for far in range(n, parts)]
        for copy in rest:
            copy.start()
        add_parts(total, lam // 2, unroll, d_refs, [lambda far=far: s_all[col ^ far] for far in range(n)])
        for copy in rest:
            copy.wait()

    need = 2 * (n * depth * lam + 2 * parts * depth * cols + 4 * lam * cols + rows * lam + cols * wide)
    return pl.pallas_call(
        body,
        out_shape=[
            jax.ShapeDtypeStruct((lam, cols), F32),
            jax.ShapeDtypeStruct((rows, lam), BF16),
            jax.ShapeDtypeStruct((cols, wide), BF16),
            jax.ShapeDtypeStruct((parts - n, depth, cols), BF16),
        ],
        in_specs=[SMEM_SPEC, SMEM_SPEC] + [VMEM_SPEC] * n + [ANY_SPEC] * parts,
        out_specs=[VMEM_SPEC] * 4,
        scratch_shapes=[
            pltpu.VMEM((parts, depth, cols), BF16),
            pltpu.SemaphoreType.DMA((parts,)),
            pltpu.SemaphoreType.DMA((parts - n,)),
        ],
        compiler_params=params(need + 4 * 1024 * 1024),
        cost_estimate=cost(2 * n * depth * lam * cols, 2 * n * depth * (lam + cols)),
        name="contract_near",
    )(basis_count, ri_count, *flat(dens), *sums)


def contract_far(dens, first, total, sums, unroll):
    (lam, cols), depth = total.shape, sums.shape[1]
    n = len(dens)

    def body(before, s_ref, *refs):
        d_refs, (o_ref,) = split_refs(dens, refs)
        add_parts(o_ref, lam // 2, unroll, d_refs, [lambda i=i: s_ref[first + i] for i in range(n)], before)

    need = 2 * (n * depth * lam + sums.size + 4 * lam * cols)
    return pl.pallas_call(
        body,
        out_shape=jax.ShapeDtypeStruct((lam, cols), F32),
        in_specs=[VMEM_SPEC] * (2 + len(flat(dens))),
        out_specs=VMEM_SPEC,
        compiler_params=params(need + 4 * 1024 * 1024),
        cost_estimate=cost(2 * n * depth * lam * cols, 2 * n * depth * (lam + cols)),
        name="contract_far",
    )(total, sums, *flat(dens))


def contract_last(dens, first, total, sums, lam_hot, col_hot, unroll):
    (rows, lam), (cols, wide) = lam_hot.shape, col_hot.shape
    depth = sums.shape[1]
    n = len(dens)
    half = lam // 2

    def body(before, s_ref, lam_hot, col_hot, *refs):
        d_refs, (o_ref, total, packed) = split_refs(dens, refs)
        add_parts(total, half, unroll, d_refs, [lambda i=i: s_ref[first + i] for i in range(n)], before)

        @loop(2, unroll)
        def _(j):
            x = total[span(j, half), :].astype(BF16)
            packed[span(j, half), :] = jnp.dot(x, col_hot[...], preferred_element_type=F32).astype(BF16)

        @loop(4, unroll)
        def _(j):
            out = span(j, rows // 4)
            o_ref[out, :] = jnp.dot(lam_hot[out, :], packed[...], preferred_element_type=F32).astype(BF16)

    need = 2 * (n * depth * lam + sums.size + 4 * lam * cols + rows * lam + cols * wide + (lam + rows) * wide)
    return pl.pallas_call(
        body,
        out_shape=jax.ShapeDtypeStruct((rows, wide), BF16),
        in_specs=[VMEM_SPEC] * (4 + len(flat(dens))),
        out_specs=VMEM_SPEC,
        scratch_shapes=[pltpu.VMEM((lam, cols), F32), pltpu.VMEM((lam, wide), BF16)],
        compiler_params=params(need + 4 * 1024 * 1024),
        cost_estimate=cost(2 * n * depth * lam * cols, 2 * n * depth * (lam + cols)),
        name="contract_last",
    )(total, sums, lam_hot, col_hot, *flat(dens))


def program(lam_size, sum_size, col_size, unroll):
    def run(three_center, density, block_mask, density_mask, basis_count, ri_count):
        ncols = lax.axis_size("col")
        nrows = lax.axis_size("row")
        chips = ncols // CORES
        rows, depth = density.shape
        wide = three_center.shape[1] // ncols
        row_bits = [1 << b for b in range(nrows.bit_length() - 1)]
        chip_bits = [CORES << b for b in range(chips.bit_length() - 1)][::-1]
        far_bit, near_bits = chip_bits[0], chip_bits[1:]

        counts = (block_mask, basis_count, ri_count, ncols, col_size, unroll)
        other = exchange(pack_integrals(three_center, *counts), "col", 1)
        own, *halves = pack_density(density, density_mask, basis_count, lam_size, sum_size, unroll)
        near = {0: own, 1: exchange(own, "col", 1)}
        pieces = pack_integrals(three_center, *counts, after(other, own))
        got = [pieces[0]] + [exchange(pieces[t], "col", CORES * t) for t in range(1, chips)]
        per = depth // pieces[0].shape[0]
        parts, groups = [], []
        for g in range(chips // per):
            arrived = got[g * per : (g + 1) * per]
            if g == 0:
                arrived = [after(arrived[0], near[1])] + arrived[1:]
            part = pack_part(arrived, basis_count, g * per, ncols, sum_size)
            if g == 0:
                near.update(double(after(own, part), "col", near_bits))
            if g > 0:
                part = after(part, *[groups[0][bit] for bit in row_bits])
            parts.append(part)
            groups.append({0: part})
            bits = row_bits if g % 2 == 0 else row_bits[::-1]
            for bit in bits:
                groups[g][bit] = exchange(part, "row", bit)
        step = groups[-1][row_bits[-1]]
        for g, have in enumerate(groups):
            bits = row_bits if g % 2 == 0 else row_bits[::-1]
            done = [0, bits[0]]
            for bit in bits[1:]:
                for far in done[1:]:
                    block = have[far] if g == len(groups) - 1 else after(have[far], step)
                    have[far | bit] = exchange(block, "row", bit)
                done += [far | bit for far in done]
        steps = [near[far] for far in near if far > 1]
        for far in [far for far in near if far > 1]:
            near[far | 1] = exchange(after(near[far], parts[-1]), "col", 1)
        lines = []
        for half, hold in zip(halves, ([parts[-1], *steps], [step, *near.values()])):
            half = after(half, *hold)
            lines.append({0: half, far_bit: exchange(half, "col", far_bit)})
        ready = [have[far] for have in groups for far in have]
        hold = [step]
        for line in lines:
            far = after(line[far_bit], *hold)
            for away, block in double(far, "col", near_bits).items():
                line[far_bit | away] = block
            hold = [*ready, line[ncols - CORES]]

        first = {far: [near[far]] for far in sorted(near)}
        total, lam_hot, col_hot, sums = contract_near(
            first, groups, basis_count, ri_count, ncols, rows, wide, unroll
        )
        middle, last = {}, {}
        for far in range(far_bit, ncols, CORES):
            blocks = [line[far] for line in lines]
            if far < ncols - CORES:
                middle[far] = blocks
                middle[far | 1] = [exchange(x, "col", 1) for x in blocks]
            else:
                last[far] = blocks
        total = contract_far(middle, 0, total, sums, unroll)
        upper, lower = last[ncols - CORES]
        last[ncols - 1] = [exchange(upper, "col", 1), exchange(after(lower, total), "col", 1)]
        return contract_last(last, len(middle), total, sums, lam_hot, col_hot, unroll)

    return run


def first_fit(basis_count, ri_count, groups, levels):
    def body(count_ref, ri_ref, o_ref):
        level = jnp.int32(0)
        for axis, (ref, parts) in enumerate(zip((count_ref, count_ref, ri_ref), groups)):
            per = ref.shape[0] // parts
            most = jnp.int32(0)
            for g in range(parts):
                total = jnp.int32(0)
                for i in range(per):
                    total = total + ref[g * per + i]
                most = jnp.maximum(most, total)
            for n, sizes in enumerate(levels[:-1]):
                level = jnp.where(most > sizes[axis], jnp.maximum(level, n + 1), level)
        o_ref[0] = level

    return pl.pallas_call(
        body,
        out_shape=jax.ShapeDtypeStruct((1,), jnp.int32),
        in_specs=[SMEM_SPEC, SMEM_SPEC],
        out_specs=SMEM_SPEC,
        name="first_fit",
    )(basis_count, ri_count)


def choose(here, yes, no):
    return lambda *args: lax.cond(here, yes, no, *args)


def shards(three_center, density, block_mask, density_mask, basis_count, ri_count):
    ncols = lax.axis_size("col")
    nrows = lax.axis_size("row")
    rows, depth = density.shape
    wide = three_center.shape[1] // ncols
    levels = (
        (rows * 3 // 4, depth * 3 // 4, wide * 5 // 6),
        (rows * 3 // 4, depth, wide * 5 // 6),
        (rows * 3 // 4, depth, wide),
        (rows, depth, wide),
    )
    level = first_fit(basis_count, ri_count, (nrows, ncols, ncols), levels)
    args = (three_center, density, block_mask, density_mask, basis_count, ri_count)
    run = program(*levels[-1], False)
    for n in reversed(range(len(levels) - 1)):
        run = choose(level[0] == n, program(*levels[n], n == 0), run)
    return run(*args)


def solution(mesh):
    in_specs = (
        P(("row", "col"), None),
        P("row", "col"),
        P(("row", "col"), None),
        P("row", "col"),
        P(),
        P(),
    )
    return jax.shard_map(
        shards, mesh=mesh, in_specs=in_specs, out_specs=P("row", "col"), check_vma=False
    )
```

```python
import jax
import jax.numpy as jnp
from jax import lax
from jax.experimental import pallas as pl
from jax.experimental.pallas import tpu as pltpu
from jax.sharding import PartitionSpec as P

BW = 32
RW = 128
CORES = 2
VMEM = 48 * 1024 * 1024
BF16 = jnp.bfloat16
F32 = jnp.float32
SMEM_SPEC = pl.BlockSpec(memory_space=pltpu.SMEM)
VMEM_SPEC = pl.BlockSpec(memory_space=pltpu.VMEM)
ANY_SPEC = pl.BlockSpec(memory_space=pl.ANY)


def params(limit=VMEM):
    return pltpu.CompilerParams(vmem_limit_bytes=limit)


def cost(flops, bytes_accessed):
    return pl.CostEstimate(flops=flops, bytes_accessed=bytes_accessed, transcendentals=0)


def ones_where(cond):
    return jnp.where(cond, 1.0, 0.0).astype(BF16)


def iota(shape, axis):
    return lax.broadcasted_iota(jnp.int32, shape, axis)


def loop(n, unroll):
    def run(f):
        if unroll:
            for i in range(n):
                f(i)
        else:
            pl.loop(0, n)(f)

    return run


def span(i, size):
    return pl.ds(i * size if isinstance(i, int) else pl.multiple_of(i * size, size), size)


def place_row(count_ref, base, atoms, width):
    lane = iota((1, atoms * width), 1)

    def atom(a, carry):
        place, offset = carry
        count = count_ref[base + a]
        inside = (lane >= a * width) & (lane < a * width + count)
        return jnp.where(inside, lane - a * width + offset, place), offset + count

    return lax.fori_loop(0, atoms, atom, (jnp.full(lane.shape, -1, jnp.int32), jnp.int32(0)))[0]


def pack_rows(count_ref, base, atoms, width, size):
    place = place_row(count_ref, base, atoms, width)
    return ones_where(iota((size, atoms * width), 0) == place)


def pack_cols(count_ref, base, atoms, width, size, out, unroll):
    def atom(a, offset):
        count = count_ref[base + a]
        slot = iota((width, size), 0)
        gap = iota((width, size), 1) - slot
        out[span(a, width), :] = ones_where((gap == offset) & (slot < count))
        return offset + count

    if unroll:
        offset = jnp.int32(0)
        for a in range(atoms):
            offset = atom(a, offset)
    else:
        lax.fori_loop(0, atoms, atom, jnp.int32(0))


def first_fit(count_ref, ri_ref, groups, levels):
    level = jnp.int32(0)
    for axis, (ref, parts) in enumerate(zip((count_ref, count_ref, ri_ref), groups)):
        per = ref.shape[0] // parts
        most = jnp.int32(0)
        for g in range(parts):
            total = jnp.int32(0)
            for i in range(per):
                total = total + ref[g * per + i]
            most = jnp.maximum(most, total)
        for n, sizes in enumerate(levels[:-1]):
            level = jnp.where(most > sizes[axis], jnp.maximum(level, n + 1), level)
    return level


def pack_integrals(tc, block_mask, basis_count, ri_count, ncols, packed, unroll, arrived=None, levels=None):
    rows, cols = tc.shape
    atoms = rows // BW
    wide = cols // ncols
    blocks = wide // RW
    chips = ncols // CORES
    first = arrived is None

    def body(count_ref, ri_ref, mask_ref, x_ref, *refs):
        if levels is not None:
            refs[1][0] = first_fit(count_ref, ri_ref, *levels)
        outs = refs[:1] if first else refs[1 : 1 + chips]
        held, hot = refs[-2:] if first else refs[-3:-1]
        made = outs[0] if first else refs[-1]
        row, col = lax.axis_index("row"), lax.axis_index("col")
        base = (row * ncols + col) * atoms

        @loop(chips, unroll)
        def _(t):
            dest = col ^ (CORES * t + (1 if first else 0))

            @loop(blocks, unroll)
            def _(b):
                lanes = pl.ds(pl.multiple_of(dest * wide + b * RW, RW), RW)
                slot = iota((BW, RW), 0)
                for a in range(atoms):
                    limit = jnp.where(mask_ref[a, dest * blocks + b] > 0, count_ref[base + a], 0)
                    x = x_ref[pl.ds(a * BW, BW), lanes].astype(F32)
                    held[pl.ds(a * BW, BW), span(b, RW)] = jnp.where(slot < limit, x, 0.0).astype(BF16)

            pack_cols(ri_ref, dest * blocks, blocks, RW, packed, hot, unroll)
            made[t] = jnp.dot(held[...], hot[...], preferred_element_type=F32).astype(BF16)

        if not first:
            core = lax.rem(col, CORES)
            for t in range(chips):
                outs[t][pl.ds(pl.multiple_of(core * rows, rows), rows), :] = made[t]
                outs[t][pl.ds(pl.multiple_of((1 - core) * rows, rows), rows), :] = refs[0][t]

    shape = (chips, rows, packed)
    merged = jax.ShapeDtypeStruct((CORES * rows, packed), BF16)
    out_shape = [jax.ShapeDtypeStruct(shape, BF16)] if first else [merged] * chips
    out_specs = [VMEM_SPEC] * len(out_shape)
    if levels is not None:
        out_shape.append(jax.ShapeDtypeStruct((1,), jnp.int32))
        out_specs.append(SMEM_SPEC)
    return pl.pallas_call(
        body,
        out_shape=out_shape,
        in_specs=[SMEM_SPEC, SMEM_SPEC, SMEM_SPEC] + [VMEM_SPEC] * (1 if first else 2),
        out_specs=out_specs,
        scratch_shapes=[pltpu.VMEM((rows, wide), BF16), pltpu.VMEM((wide, packed), BF16)]
        + ([] if first else [pltpu.VMEM(shape, BF16)]),
        compiler_params=params(),
        cost_estimate=cost(rows * cols * packed, rows * cols + 3 * chips * rows * packed),
        name="pack_other_core" if first else "pack_own_core",
    )(basis_count, ri_count, block_mask, tc, *([] if first else [arrived]))


def pack_density(dens, mask, basis_count, lam_size, sum_size, unroll):
    rows, cols = dens.shape
    lam_atoms, sum_atoms = mask.shape
    steps = 1 if unroll else 4
    tile = rows // steps
    out_tile = lam_size // steps

    def body(count_ref, mask_ref, x_ref, o_ref, hot, keep, mid):
        row, col = lax.axis_index("row"), lax.axis_index("col")
        of_atom = ones_where(iota((sum_atoms, cols), 1) // BW == iota((sum_atoms, cols), 0))
        keep[...] = jnp.dot(ones_where(mask_ref[...] > 0), of_atom, preferred_element_type=F32).astype(BF16)
        pack_cols(count_ref, col * sum_atoms, sum_atoms, BW, sum_size, hot, unroll)

        @loop(steps, unroll)
        def _(i):
            at = span(i, tile)
            shape = (tile, lam_atoms)
            atom = ones_where((iota(shape, 0) + i * tile) // BW == iota(shape, 1))
            kept = jnp.dot(atom, keep[...], preferred_element_type=F32)
            x = jnp.where(kept > 0.5, x_ref[at, :].astype(F32), 0.0).astype(BF16)
            mid[at, :] = jnp.dot(x, hot[...], preferred_element_type=F32).astype(BF16)

        place = place_row(count_ref, row * lam_atoms, lam_atoms, BW)

        @loop(steps, unroll)
        def _(i):
            at = span(i, out_tile)
            left = ones_where(iota((out_tile, rows), 0) + i * out_tile == place)
            o_ref[at, :] = jnp.dot(left, mid[...], preferred_element_type=F32).astype(BF16)

    return pl.pallas_call(
        body,
        out_shape=jax.ShapeDtypeStruct((lam_size, sum_size), BF16),
        in_specs=[SMEM_SPEC, VMEM_SPEC, VMEM_SPEC],
        out_specs=VMEM_SPEC,
        scratch_shapes=[
            pltpu.VMEM((cols, sum_size), BF16),
            pltpu.VMEM((lam_atoms, cols), BF16),
            pltpu.VMEM((rows, sum_size), BF16),
        ],
        compiler_params=params(),
        cost_estimate=cost(2 * rows * sum_size * (cols + lam_size), 2 * rows * cols),
        name="pack_density",
    )(basis_count, mask, dens)


def pack_part(pieces, basis_count, first, ncols, size):
    rows, cols = pieces[0].shape
    per = len(pieces)
    depth = per * rows
    atoms = depth // BW

    def body(count_ref, *refs):
        blocks, o_ref, full = refs[:per], refs[per], refs[per + 1]
        row, chip = lax.axis_index("row"), lax.axis_index("col") // CORES
        for i in range(per):
            at = lax.rem(chip ^ (first + i), per) * rows
            full[pl.ds(pl.multiple_of(at, rows), rows), :] = blocks[i][...]
        part = (row * (ncols // CORES) + (chip ^ first)) * rows // depth
        hot = pack_rows(count_ref, part * atoms, atoms, BW, size)
        o_ref[...] = jnp.dot(hot, full[...], preferred_element_type=F32).astype(BF16)

    return pl.pallas_call(
        body,
        out_shape=jax.ShapeDtypeStruct((size, cols), BF16),
        in_specs=[SMEM_SPEC] + [VMEM_SPEC] * per,
        out_specs=VMEM_SPEC,
        scratch_shapes=[pltpu.VMEM((depth, cols), BF16)],
        compiler_params=params(),
        cost_estimate=cost((2 + 10 * first) * size * depth * cols, 2 * cols * (depth + size)),
        name="pack_part",
    )(basis_count, *pieces)


def exchange(x, axis, bit):
    peers = lax.axis_size(axis)
    return lax.ppermute(x, axis, [(i, i ^ bit) for i in range(peers)])


def after(x, *others):
    return lax.optimization_barrier((x, *others))[0]


def double(own, axis, bits):
    have = {0: own}
    for bit in bits:
        for far in sorted(have):
            have[far | bit] = exchange(have[far], axis, bit)
    return have


def add_parts(total, tile, unroll, d_refs, sums, before=None):
    lam, cols = total.shape

    @loop(lam // tile, unroll)
    def _(j):
        out = span(j, tile)
        x = None if before is None else before[out, :]
        for chunks, part in zip(d_refs, sums):
            if len(chunks) == 1:
                d = chunks[0][out, :]
            elif isinstance(j, int):
                size = chunks[0].shape[0]
                d = chunks[j * tile // size][pl.ds(j * tile % size, tile), :]
            else:
                per = chunks[0].shape[0] // tile
                inner = span(lax.rem(j, per), tile)
                d = jnp.where(j < per, chunks[0][inner, :].astype(F32), chunks[1][inner, :].astype(F32)).astype(BF16)
            y = jnp.dot(d, part(), preferred_element_type=F32)
            x = y if x is None else x + y
        total[out, :] = x


def split_refs(dens, refs):
    lists, at = [], 0
    for chunks in dens.values():
        lists.append(refs[at : at + len(chunks)])
        at += len(chunks)
    return lists, refs[at:]


def flat(dens):
    return [chunk for chunks in dens.values() for chunk in chunks]


def contract_near(dens, integrals, basis_count, ri_count, ncols, rows, wide, unroll):
    lam, depth = dens[0][0].shape
    groups, nrows = len(integrals), len(integrals[0])
    sums = [integrals[g][far] for far in range(nrows) for g in range(groups)]
    cols = sums[0].shape[1]
    lam_atoms, blocks = rows // BW, wide // RW
    n, parts = len(dens), len(sums)

    def body(count_ref, ri_ref, *refs):
        d_refs, refs = split_refs(dens, refs)
        s_refs, refs = refs[:parts], refs[parts:]
        total, lam_hot, col_hot, s_rest, s_all, s_sem, r_sem = refs
        row, col = lax.axis_index("row"), lax.axis_index("col")
        for j, ref in enumerate(s_refs):
            part = (row ^ (j // groups)) * groups + (col // (ncols // groups) ^ (j % groups))
            pltpu.make_async_copy(ref, s_all.at[part], s_sem.at[part]).start()
        pack_cols(count_ref, row * lam_atoms, lam_atoms, BW, lam, lam_hot, unroll)
        place = place_row(ri_ref, col * blocks, blocks, RW)

        @loop(cols // RW, unroll)
        def _(i):
            col_hot[span(i, RW), :] = ones_where(iota((RW, wide), 0) + i * RW == place)

        @pl.loop(0, parts)
        def _(i):
            pltpu.make_async_copy(s_all.at[i], s_all.at[i], s_sem.at[i]).wait()

        rest = [pltpu.make_async_copy(s_all.at[col ^ far], s_rest.at[far - n], r_sem.at[far - n]) for far in range(n, parts)]
        for copy in rest:
            copy.start()
        add_parts(total, lam // 2, unroll, d_refs, [lambda far=far: s_all[col ^ far] for far in range(n)])
        for copy in rest:
            copy.wait()

    need = 2 * (n * depth * lam + 2 * parts * depth * cols + 4 * lam * cols + rows * lam + cols * wide)
    return pl.pallas_call(
        body,
        out_shape=[
            jax.ShapeDtypeStruct((lam, cols), F32),
            jax.ShapeDtypeStruct((rows, lam), BF16),
            jax.ShapeDtypeStruct((cols, wide), BF16),
            jax.ShapeDtypeStruct((parts - n, depth, cols), BF16),
        ],
        in_specs=[SMEM_SPEC, SMEM_SPEC] + [VMEM_SPEC] * n + [ANY_SPEC] * parts,
        out_specs=[VMEM_SPEC] * 4,
        scratch_shapes=[
            pltpu.VMEM((parts, depth, cols), BF16),
            pltpu.SemaphoreType.DMA((parts,)),
            pltpu.SemaphoreType.DMA((parts - n,)),
        ],
        compiler_params=params(need + 4 * 1024 * 1024),
        cost_estimate=cost(2 * n * depth * lam * cols, 2 * n * depth * (lam + cols)),
        name="contract_near",
    )(basis_count, ri_count, *flat(dens), *sums)


def contract_far(dens, first, total, sums, unroll):
    (lam, cols), depth = total.shape, sums.shape[1]
    n = len(dens)

    def body(before, s_ref, *refs):
        d_refs, (o_ref,) = split_refs(dens, refs)
        add_parts(o_ref, lam // 2, unroll, d_refs, [lambda i=i: s_ref[first + i] for i in range(n)], before)

    need = 2 * (n * depth * lam + sums.size + 4 * lam * cols)
    return pl.pallas_call(
        body,
        out_shape=jax.ShapeDtypeStruct((lam, cols), F32),
        in_specs=[VMEM_SPEC] * (2 + len(flat(dens))),
        out_specs=VMEM_SPEC,
        compiler_params=params(need + 4 * 1024 * 1024),
        cost_estimate=cost(2 * n * depth * lam * cols, 2 * n * depth * (lam + cols)),
        name="contract_far",
    )(total, sums, *flat(dens))


def contract_last(dens, first, total, sums, lam_hot, col_hot, unroll):
    (rows, lam), (cols, wide) = lam_hot.shape, col_hot.shape
    depth = sums.shape[1]
    n = len(dens)
    half = lam // 2

    def body(before, s_ref, lam_hot, col_hot, *refs):
        d_refs, (o_ref, total, packed, made, sem) = split_refs(dens, refs)
        add_parts(total, half, unroll, d_refs, [lambda i=i: s_ref[first + i] for i in range(n)], before)

        @loop(2, unroll)
        def _(j):
            x = total[span(j, half), :].astype(BF16)
            packed[span(j, half), :] = jnp.dot(x, col_hot[...], preferred_element_type=F32).astype(BF16)

        copies = []
        for j in range(4):
            out = span(j, rows // 4)
            made[out, :] = jnp.dot(lam_hot[out, :], packed[...], preferred_element_type=F32).astype(BF16)
            copies.append(pltpu.make_async_copy(made.at[out, :], o_ref.at[out, :], sem.at[j]))
            copies[-1].start()
        for copy in copies:
            copy.wait()

    need = 2 * (n * depth * lam + sums.size + 4 * lam * cols + rows * lam + cols * wide + (lam + rows) * wide)
    return pl.pallas_call(
        body,
        out_shape=jax.ShapeDtypeStruct((rows, wide), BF16),
        in_specs=[VMEM_SPEC] * (4 + len(flat(dens))),
        out_specs=ANY_SPEC,
        scratch_shapes=[
            pltpu.VMEM((lam, cols), F32),
            pltpu.VMEM((lam, wide), BF16),
            pltpu.VMEM((rows, wide), BF16),
            pltpu.SemaphoreType.DMA((4,)),
        ],
        compiler_params=params(need + 4 * 1024 * 1024),
        cost_estimate=cost(2 * n * depth * lam * cols, 2 * n * depth * (lam + cols)),
        name="contract_last",
    )(total, sums, lam_hot, col_hot, *flat(dens))


def program(lam_size, sum_size, col_size, common):
    unroll = common

    def run(three_center, density, block_mask, density_mask, basis_count, ri_count, other):
        ncols = lax.axis_size("col")
        nrows = lax.axis_size("row")
        chips = ncols // CORES
        rows, depth = density.shape
        wide = three_center.shape[1] // ncols
        row_bits = [1 << b for b in range(nrows.bit_length() - 1)]
        chip_bits = [CORES << b for b in range(chips.bit_length() - 1)][::-1]
        far_bit, near_bits = chip_bits[0], chip_bits[1:]

        counts = (block_mask, basis_count, ri_count, ncols, col_size, unroll)
        if not common:
            other = pack_integrals(three_center, *counts)[0]
        other = exchange(other, "col", 1)
        own = pack_density(density, density_mask, basis_count, lam_size, sum_size, unroll)
        near = {0: own, 1: exchange(own, "col", 1)}
        pieces = pack_integrals(three_center, *counts, after(other, own))
        got = [pieces[0]] + [exchange(pieces[t], "col", CORES * t) for t in range(1, chips)]
        per = depth // pieces[0].shape[0]
        parts, groups, orders = [], [], []
        for g in range(chips // per):
            arrived = got[g * per : (g + 1) * per]
            if g == 0:
                arrived = [after(arrived[0], near[1])] + arrived[1:]
            part = pack_part(arrived, basis_count, g * per, ncols, sum_size)
            if g == 0:
                near.update(double(after(own, part), "col", near_bits))
                steps = [near[far] for far in near if far > 1]
            else:
                part = after(part, *[groups[0][bit] for bit in row_bits])
            parts.append(part)
            orders.append(row_bits if g % 2 == 0 else row_bits[::-1])
            groups.append({0: part})
            for i, bit in enumerate(orders[g]):
                groups[g][bit] = exchange(after(part, *steps) if g > 0 and i > 0 else part, "row", bit)
        step = groups[-1][orders[-1][0]]
        line = {0: own, far_bit: exchange(after(own, parts[-1]), "col", far_bit)}
        for g, have in enumerate(groups):
            done = [0, orders[g][0]]
            for bit in orders[g][1:]:
                for far in done[1:]:
                    have[far | bit] = exchange(have[far] if g == len(groups) - 1 else after(have[far], step), "row", bit)
                done += [far | bit for far in done]
        for far in [far for far in near if far > 1]:
            near[far | 1] = exchange(near[far], "col", 1)
        first = {far: [near[far]] for far in sorted(near)}
        total, lam_hot, col_hot, sums = contract_near(
            first, groups, basis_count, ri_count, ncols, rows, wide, unroll
        )
        for away, block in double(line[far_bit], "col", near_bits).items():
            line[far_bit | away] = block
        middle = {}
        for far in range(far_bit, ncols - CORES, CORES):
            middle[far] = [line[far]]
            middle[far | 1] = [exchange(line[far], "col", 1)]
        total = contract_far(middle, 0, total, sums, unroll)
        end = line[ncols - CORES]
        last = {ncols - CORES: [end], ncols - 1: [exchange(after(end, total), "col", 1)]}
        return contract_last(last, len(middle), total, sums, lam_hot, col_hot, unroll)

    return run


def choose(here, yes, no):
    return lambda *args: lax.cond(here, yes, no, *args)


def shards(three_center, density, block_mask, density_mask, basis_count, ri_count):
    ncols = lax.axis_size("col")
    nrows = lax.axis_size("row")
    rows, depth = density.shape
    wide = three_center.shape[1] // ncols
    levels = (
        (rows * 3 // 4, depth * 3 // 4, wide * 5 // 6),
        (rows * 3 // 4, depth, wide * 5 // 6),
        (rows * 3 // 4, depth, wide),
        (rows, depth, wide),
    )
    other, level = pack_integrals(
        three_center,
        block_mask,
        basis_count,
        ri_count,
        ncols,
        levels[0][2],
        True,
        levels=((nrows, ncols, ncols), levels),
    )
    args = (three_center, density, block_mask, density_mask, basis_count, ri_count, other)
    run = program(*levels[-1], False)
    for n in reversed(range(len(levels) - 1)):
        run = choose(level[0] == n, program(*levels[n], n == 0), run)
    return run(*args)


def solution(mesh):
    in_specs = (
        P(("row", "col"), None),
        P("row", "col"),
        P(("row", "col"), None),
        P("row", "col"),
        P(),
        P(),
    )
    return jax.shard_map(
        shards, mesh=mesh, in_specs=in_specs, out_specs=P("row", "col"), check_vma=False
    )
```

```python
import jax
import jax.numpy as jnp
from jax import lax
from jax.experimental import pallas as pl
from jax.experimental.pallas import tpu as pltpu
from jax.sharding import PartitionSpec as P

BW = 32
RW = 128
CORES = 2
VMEM = 48 * 1024 * 1024
TILE = 256
BF16 = jnp.bfloat16
F32 = jnp.float32
SMEM_SPEC = pl.BlockSpec(memory_space=pltpu.SMEM)
VMEM_SPEC = pl.BlockSpec(memory_space=pltpu.VMEM)
ANY_SPEC = pl.BlockSpec(memory_space=pl.ANY)


def params(limit=VMEM):
    return pltpu.CompilerParams(vmem_limit_bytes=limit)


def cost(flops, bytes_accessed):
    return pl.CostEstimate(flops=flops, bytes_accessed=bytes_accessed, transcendentals=0)


def ones_where(cond):
    return jnp.where(cond, 1.0, 0.0).astype(BF16)


def iota(shape, axis):
    return lax.broadcasted_iota(jnp.int32, shape, axis)


def loop(n, unroll):
    def run(f):
        if unroll:
            for i in range(n):
                f(i)
        else:
            pl.loop(0, n)(f)

    return run


def span(i, size):
    return pl.ds(i * size if isinstance(i, int) else pl.multiple_of(i * size, size), size)


def place_row(count_ref, base, atoms, width):
    lane = iota((1, atoms * width), 1)

    def atom(a, carry):
        place, offset = carry
        count = count_ref[base + a]
        inside = (lane >= a * width) & (lane < a * width + count)
        return jnp.where(inside, lane - a * width + offset, place), offset + count

    return lax.fori_loop(0, atoms, atom, (jnp.full(lane.shape, -1, jnp.int32), jnp.int32(0)))[0]


def pack_rows(count_ref, base, atoms, width, size):
    place = place_row(count_ref, base, atoms, width)
    return ones_where(iota((size, atoms * width), 0) == place)


def pack_cols(count_ref, base, atoms, width, size, out, unroll):
    def atom(a, offset):
        count = count_ref[base + a]
        slot = iota((width, size), 0)
        gap = iota((width, size), 1) - slot
        out[span(a, width), :] = ones_where((gap == offset) & (slot < count))
        return offset + count

    if unroll:
        offset = jnp.int32(0)
        for a in range(atoms):
            offset = atom(a, offset)
    else:
        lax.fori_loop(0, atoms, atom, jnp.int32(0))


def first_fit(basis_count, ri_count, groups, levels):
    def body(count_ref, ri_ref, o_ref):
        level = jnp.int32(0)
        for axis, (ref, parts) in enumerate(zip((count_ref, count_ref, ri_ref), groups)):
            per = ref.shape[0] // parts
            most = jnp.int32(0)
            for g in range(parts):
                total = jnp.int32(0)
                for i in range(per):
                    total = total + ref[g * per + i]
                most = jnp.maximum(most, total)
            for n, sizes in enumerate(levels[:-1]):
                level = jnp.where(most > sizes[axis], jnp.maximum(level, n + 1), level)
        o_ref[0] = level

    return pl.pallas_call(
        body,
        out_shape=jax.ShapeDtypeStruct((1,), jnp.int32),
        in_specs=[SMEM_SPEC, SMEM_SPEC],
        out_specs=SMEM_SPEC,
        name="first_fit",
    )(basis_count, ri_count)


def pack_integrals(tc, block_mask, basis_count, ri_count, ncols, packed, unroll, arrived=None):
    rows, cols = tc.shape
    atoms = rows // BW
    wide = cols // ncols
    blocks = wide // RW
    chips = ncols // CORES
    first = arrived is None

    def body(count_ref, ri_ref, mask_ref, x_ref, *refs):
        outs = refs[:1] if first else refs[1 : 1 + chips]
        held, hot = refs[-2:] if first else refs[-3:-1]
        made = outs[0] if first else refs[-1]
        row, col = lax.axis_index("row"), lax.axis_index("col")
        base = (row * ncols + col) * atoms

        @loop(chips, unroll)
        def _(t):
            dest = col ^ (CORES * t + (1 if first else 0))

            @loop(blocks, unroll)
            def _(b):
                lanes = pl.ds(pl.multiple_of(dest * wide + b * RW, RW), RW)
                slot = iota((BW, RW), 0)
                for a in range(atoms):
                    limit = jnp.where(mask_ref[a, dest * blocks + b] > 0, count_ref[base + a], 0)
                    x = x_ref[pl.ds(a * BW, BW), lanes].astype(F32)
                    held[pl.ds(a * BW, BW), span(b, RW)] = jnp.where(slot < limit, x, 0.0).astype(BF16)

            pack_cols(ri_ref, dest * blocks, blocks, RW, packed, hot, unroll)
            made[t] = jnp.dot(held[...], hot[...], preferred_element_type=F32).astype(BF16)

        if not first:
            core = lax.rem(col, CORES)
            for t in range(chips):
                outs[t][pl.ds(pl.multiple_of(core * rows, rows), rows), :] = made[t]
                outs[t][pl.ds(pl.multiple_of((1 - core) * rows, rows), rows), :] = refs[0][t]

    shape = (chips, rows, packed)
    merged = jax.ShapeDtypeStruct((CORES * rows, packed), BF16)
    out_shape = [jax.ShapeDtypeStruct(shape, BF16)] if first else [merged] * chips
    out_specs = [VMEM_SPEC] * len(out_shape)
    return pl.pallas_call(
        body,
        out_shape=out_shape,
        in_specs=[SMEM_SPEC, SMEM_SPEC, SMEM_SPEC] + [VMEM_SPEC] * (1 if first else 2),
        out_specs=out_specs,
        scratch_shapes=[pltpu.VMEM((rows, wide), BF16), pltpu.VMEM((wide, packed), BF16)]
        + ([] if first else [pltpu.VMEM(shape, BF16)]),
        compiler_params=params(),
        cost_estimate=cost(rows * cols * packed, rows * cols + 3 * chips * rows * packed),
        name="pack_other_core" if first else "pack_own_core",
    )(basis_count, ri_count, block_mask, tc, *([] if first else [arrived]))


def pack_density(dens, mask, basis_count, lam_size, sum_size, unroll):
    rows, cols = dens.shape
    lam_atoms, sum_atoms = mask.shape
    steps = 1 if unroll else 4
    tile = rows // steps
    out_tile = lam_size // steps

    def body(count_ref, mask_ref, x_ref, o_ref, upper_ref, lower_ref, hot, keep, mid):
        row, col = lax.axis_index("row"), lax.axis_index("col")
        first = iota((sum_atoms, cols), 0) * BW
        lane = iota((sum_atoms, cols), 1)
        of_atom = ones_where((lane >= first) & (lane < first + BW))
        keep[...] = jnp.dot(ones_where(mask_ref[...] > 0), of_atom, preferred_element_type=F32).astype(BF16)
        pack_cols(count_ref, col * sum_atoms, sum_atoms, BW, sum_size, hot, unroll)

        @loop(steps, unroll)
        def _(i):
            at = span(i, tile)
            shape = (tile, lam_atoms)
            first = iota(shape, 1) * BW - i * tile
            atom = ones_where((iota(shape, 0) >= first) & (iota(shape, 0) < first + BW))
            kept = jnp.dot(atom, keep[...], preferred_element_type=F32)
            x = jnp.where(kept > 0.5, x_ref[at, :].astype(F32), 0.0).astype(BF16)
            mid[at, :] = jnp.dot(x, hot[...], preferred_element_type=F32).astype(BF16)

        place = place_row(count_ref, row * lam_atoms, lam_atoms, BW)

        @loop(steps, unroll)
        def _(i):
            at = span(i, out_tile)
            left = ones_where(iota((out_tile, rows), 0) + i * out_tile == place)
            o_ref[at, :] = jnp.dot(left, mid[...], preferred_element_type=F32).astype(BF16)

        upper_ref[...] = o_ref[pl.ds(0, TILE), :]
        lower_ref[...] = o_ref[pl.ds(TILE, lam_size - TILE), :]

    return pl.pallas_call(
        body,
        out_shape=[jax.ShapeDtypeStruct((n, sum_size), BF16) for n in (lam_size, TILE, lam_size - TILE)],
        in_specs=[SMEM_SPEC, VMEM_SPEC, VMEM_SPEC],
        out_specs=[VMEM_SPEC] * 3,
        scratch_shapes=[
            pltpu.VMEM((cols, sum_size), BF16),
            pltpu.VMEM((lam_atoms, cols), BF16),
            pltpu.VMEM((rows, sum_size), BF16),
        ],
        compiler_params=params(),
        cost_estimate=cost(2 * rows * sum_size * (cols + lam_size), 2 * rows * cols),
        name="pack_density",
    )(basis_count, mask, dens)


def pack_part(pieces, basis_count, first, ncols, size):
    rows, cols = pieces[0].shape
    per = len(pieces)
    depth = per * rows
    atoms = depth // BW

    def body(count_ref, *refs):
        blocks, o_ref, full = refs[:per], refs[per], refs[per + 1]
        row, chip = lax.axis_index("row"), lax.axis_index("col") // CORES
        for i in range(per):
            at = lax.rem(chip ^ (first + i), per) * rows
            full[pl.ds(pl.multiple_of(at, rows), rows), :] = blocks[i][...]
        part = (row * (ncols // CORES) + (chip ^ first)) * rows // depth
        hot = pack_rows(count_ref, part * atoms, atoms, BW, size)
        o_ref[...] = jnp.dot(hot, full[...], preferred_element_type=F32).astype(BF16)

    return pl.pallas_call(
        body,
        out_shape=jax.ShapeDtypeStruct((size, cols), BF16),
        in_specs=[SMEM_SPEC] + [VMEM_SPEC] * per,
        out_specs=VMEM_SPEC,
        scratch_shapes=[pltpu.VMEM((depth, cols), BF16)],
        compiler_params=params(),
        cost_estimate=cost((2 + 10 * first) * size * depth * cols, 2 * cols * (depth + size)),
        name="pack_part",
    )(basis_count, *pieces)


def exchange(x, axis, bit):
    peers = lax.axis_size(axis)
    return lax.ppermute(x, axis, [(i, i ^ bit) for i in range(peers)])


def after(x, *others):
    return lax.optimization_barrier((x, *others))[0]


def double(own, axis, bits):
    have = {0: own}
    for bit in bits:
        for far in sorted(have):
            have[far | bit] = exchange(have[far], axis, bit)
    return have


def add_parts(total, unroll, d_refs, sums, before=None):
    lam, cols = total.shape

    @loop(lam // TILE, unroll)
    def _(j):
        out = span(j, TILE)
        x = None if before is None else before[out, :]
        for chunks, part in zip(d_refs, sums):
            if len(chunks) == 1:
                d = chunks[0][out, :]
            elif isinstance(j, int):
                d = chunks[0][...] if j == 0 else chunks[1][span(j - 1, TILE), :]
            else:
                d = chunks[1][span(jnp.maximum(j - 1, 0), TILE), :].astype(F32)
                d = jnp.where(j == 0, chunks[0][...].astype(F32), d).astype(BF16)
            y = jnp.dot(d, part(), preferred_element_type=F32)
            x = y if x is None else x + y
        total[out, :] = x


def split_refs(dens, refs):
    lists, at = [], 0
    for chunks in dens.values():
        lists.append(refs[at : at + len(chunks)])
        at += len(chunks)
    return lists, refs[at:]


def flat(dens):
    return [chunk for chunks in dens.values() for chunk in chunks]


def ways_back(basis_count, ri_count, nrows, ncols, rows, wide, lam, cols, unroll):
    lam_atoms, blocks = rows // BW, wide // RW

    def body(count_ref, ri_ref, lam_hot, col_hot):
        row, col = lax.axis_index("row"), lax.axis_index("col")
        pack_cols(count_ref, row * lam_atoms, lam_atoms, BW, lam, lam_hot, unroll)
        place = place_row(ri_ref, col * blocks, blocks, RW)

        @loop(cols // RW, unroll)
        def _(i):
            col_hot[span(i, RW), :] = ones_where(iota((RW, wide), 0) + i * RW == place)

    return pl.pallas_call(
        body,
        out_shape=[jax.ShapeDtypeStruct((rows, lam), BF16), jax.ShapeDtypeStruct((cols, wide), BF16)],
        in_specs=[SMEM_SPEC, SMEM_SPEC],
        out_specs=[VMEM_SPEC] * 2,
        compiler_params=params(16 * 1024 * 1024),
        name="ways_back",
    )(basis_count, ri_count)


def contract_near(dens, integrals, ncols, unroll):
    lam, depth = dens[0][0].shape
    groups, nrows = len(integrals), len(integrals[0])
    sums = [integrals[g][far] for far in range(nrows) for g in range(groups)]
    cols = sums[0].shape[1]
    n, parts = len(dens), len(sums)

    def body(*refs):
        d_refs, refs = split_refs(dens, refs)
        s_refs, refs = refs[:parts], refs[parts:]
        total, s_rest, s_all, s_sem, r_sem = refs
        row, col = lax.axis_index("row"), lax.axis_index("col")
        for j, ref in enumerate(s_refs):
            part = (row ^ (j // groups)) * groups + (col // (ncols // groups) ^ (j % groups))
            pltpu.make_async_copy(ref, s_all.at[part], s_sem.at[part]).start()

        @pl.loop(0, parts)
        def _(i):
            pltpu.make_async_copy(s_all.at[i], s_all.at[i], s_sem.at[i]).wait()

        rest = [
            pltpu.make_async_copy(s_all.at[col ^ far], s_rest.at[far - n], r_sem.at[far - n])
            for far in range(n, parts)
        ]
        for copy in rest:
            copy.start()
        add_parts(total, unroll, d_refs, [lambda far=far: s_all[col ^ far] for far in range(n)])
        for copy in rest:
            copy.wait()

    need = 2 * (n * depth * lam + 2 * parts * depth * cols + 4 * lam * cols)
    return pl.pallas_call(
        body,
        out_shape=[
            jax.ShapeDtypeStruct((lam, cols), F32),
            jax.ShapeDtypeStruct((parts - n, depth, cols), BF16),
        ],
        in_specs=[VMEM_SPEC] * n + [ANY_SPEC] * parts,
        out_specs=[VMEM_SPEC] * 2,
        scratch_shapes=[
            pltpu.VMEM((parts, depth, cols), BF16),
            pltpu.SemaphoreType.DMA((parts,)),
            pltpu.SemaphoreType.DMA((parts - n,)),
        ],
        compiler_params=params(need + 4 * 1024 * 1024),
        cost_estimate=cost(2 * n * depth * lam * cols, 2 * n * depth * (lam + cols)),
        name="contract_near",
    )(*flat(dens), *sums)


def contract_far(dens, first, total, sums, unroll):
    (lam, cols), depth = total.shape, sums.shape[1]
    n = len(dens)

    def body(before, s_ref, *refs):
        d_refs, (o_ref,) = split_refs(dens, refs)
        add_parts(o_ref, unroll, d_refs, [lambda i=i: s_ref[first + i] for i in range(n)], before)

    need = 2 * (n * depth * lam + sums.size + 4 * lam * cols)
    return pl.pallas_call(
        body,
        out_shape=jax.ShapeDtypeStruct((lam, cols), F32),
        in_specs=[VMEM_SPEC] * (2 + len(flat(dens))),
        out_specs=VMEM_SPEC,
        compiler_params=params(need + 4 * 1024 * 1024),
        cost_estimate=cost(2 * n * depth * lam * cols, 2 * n * depth * (lam + cols)),
        name="contract_far",
    )(total, sums, *flat(dens))


def contract_last(dens, first, total, sums, lam_hot, col_hot, unroll):
    (rows, lam), (cols, wide) = lam_hot.shape, col_hot.shape
    depth = sums.shape[1]
    n = len(dens)
    half = lam // 2

    def body(before, s_ref, lam_hot, col_hot, *refs):
        d_refs, (o_ref, total, packed) = split_refs(dens, refs)
        add_parts(total, unroll, d_refs, [lambda i=i: s_ref[first + i] for i in range(n)], before)

        @loop(2, unroll)
        def _(j):
            x = total[span(j, half), :].astype(BF16)
            packed[span(j, half), :] = jnp.dot(x, col_hot[...], preferred_element_type=F32).astype(BF16)

        @loop(4, unroll)
        def _(j):
            out = span(j, rows // 4)
            o_ref[out, :] = jnp.dot(lam_hot[out, :], packed[...], preferred_element_type=F32).astype(BF16)

    need = 2 * (n * depth * lam + sums.size + 4 * lam * cols + rows * lam + cols * wide + (lam + rows) * wide)
    return pl.pallas_call(
        body,
        out_shape=jax.ShapeDtypeStruct((rows, wide), BF16),
        in_specs=[VMEM_SPEC] * (4 + len(flat(dens))),
        out_specs=VMEM_SPEC,
        scratch_shapes=[pltpu.VMEM((lam, cols), F32), pltpu.VMEM((lam, wide), BF16)],
        compiler_params=params(need + 4 * 1024 * 1024),
        cost_estimate=cost(2 * n * depth * lam * cols, 2 * n * depth * (lam + cols)),
        name="contract_last",
    )(total, sums, lam_hot, col_hot, *flat(dens))


def program(lam_size, sum_size, col_size, common):
    unroll = common

    def run(three_center, density, block_mask, density_mask, basis_count, ri_count):
        ncols = lax.axis_size("col")
        nrows = lax.axis_size("row")
        chips = ncols // CORES
        rows, depth = density.shape
        wide = three_center.shape[1] // ncols
        row_bits = [1 << b for b in range(nrows.bit_length() - 1)]
        chip_bits = [CORES << b for b in range(chips.bit_length() - 1)][::-1]
        far_bit, near_bits = chip_bits[0], chip_bits[1:]

        counts = (block_mask, basis_count, ri_count, ncols, col_size, unroll)
        other = exchange(pack_integrals(three_center, *counts)[0], "col", 1)
        own, upper, lower = pack_density(density, density_mask, basis_count, lam_size, sum_size, unroll)
        lines = [{0: upper, far_bit: exchange(upper, "col", far_bit)}, {0: lower}]
        near = {0: own, 1: exchange(own, "col", 1)}
        pieces = pack_integrals(three_center, *counts, after(other, own))
        early = lines[0][far_bit]
        got = [pieces[0]] + [exchange(pieces[t], "col", CORES * t) for t in range(1, chips)]
        per = depth // pieces[0].shape[0]
        lam_hot, col_hot = ways_back(
            basis_count, ri_count, nrows, ncols, rows, wide, lam_size, col_size, unroll
        )
        parts, groups, orders = [], [], []
        for g in range(chips // per):
            arrived = got[g * per : (g + 1) * per]
            if g == 0:
                arrived = [after(arrived[0], near[1], early)] + arrived[1:]
            elif g == 1:
                arrived = [after(arrived[0], lam_hot)] + arrived[1:]
            part = pack_part(arrived, basis_count, g * per, ncols, sum_size)
            if g == 0:
                forward = double(after(early, part), "col", near_bits)
                lines[0].update({far_bit | far: block for far, block in forward.items()})
            else:
                part = after(part, *[groups[0][bit] for bit in row_bits], lines[0][ncols - CORES])
            parts.append(part)
            orders.append(row_bits if g % 2 == 0 else row_bits[::-1])
            groups.append({0: part})
            for bit in orders[g]:
                groups[g][bit] = exchange(part, "row", bit)
        step = groups[-1][orders[-1][0]]
        lines[1][far_bit] = exchange(after(lower, parts[-1]), "col", far_bit)
        near.update(double(after(own, parts[-1]), "col", near_bits))
        for g, have in enumerate(groups):
            done = [0, orders[g][0]]
            for bit in orders[g][1:]:
                for far in done[1:]:
                    have[far | bit] = exchange(have[far] if g == len(groups) - 1 else after(have[far], step), "row", bit)
                done += [far | bit for far in done]
        for far in [far for far in near if far > 1]:
            near[far | 1] = exchange(near[far], "col", 1)
        first = {far: [near[far]] for far in sorted(near)}
        total, sums = contract_near(first, groups, ncols, unroll)
        for away, block in double(lines[1][far_bit], "col", near_bits).items():
            lines[1][far_bit | away] = block
        middle = {}
        for far in range(far_bit, ncols - CORES, CORES):
            middle[far] = [line[far] for line in lines]
            middle[far | 1] = [exchange(line[far], "col", 1) for line in lines]
        total = contract_far(middle, 0, total, sums, unroll)
        ends = [line[ncols - CORES] for line in lines]
        last = {ncols - CORES: ends}
        last[ncols - 1] = [exchange(ends[0], "col", 1), exchange(after(ends[1], total), "col", 1)]
        return contract_last(last, len(middle), total, sums, lam_hot, col_hot, unroll)

    return run


def choose(here, yes, no):
    return lambda *args: lax.cond(here, yes, no, *args)


def shards(three_center, density, block_mask, density_mask, basis_count, ri_count):
    ncols = lax.axis_size("col")
    nrows = lax.axis_size("row")
    rows, depth = density.shape
    wide = three_center.shape[1] // ncols
    levels = (
        (rows * 3 // 4, depth * 3 // 4, wide * 5 // 6),
        (rows * 3 // 4, depth, wide * 5 // 6),
        (rows * 3 // 4, depth, wide),
        (rows, depth, wide),
    )
    level = first_fit(basis_count, ri_count, (nrows, ncols, ncols), levels)
    args = (three_center, density, block_mask, density_mask, basis_count, ri_count)
    run = program(*levels[-1], False)
    for n in reversed(range(len(levels) - 1)):
        run = choose(level[0] == n, program(*levels[n], n == 0), run)
    return run(*args)


def solution(mesh):
    in_specs = (
        P(("row", "col"), None),
        P("row", "col"),
        P(("row", "col"), None),
        P("row", "col"),
        P(),
        P(),
    )
    return jax.shard_map(
        shards, mesh=mesh, in_specs=in_specs, out_specs=P("row", "col"), check_vma=False
    )
```

```python
import jax
import jax.numpy as jnp
from jax import lax
from jax.experimental import pallas as pl
from jax.experimental.pallas import tpu as pltpu
from jax.sharding import PartitionSpec as P

BW = 32
RW = 128
CORES = 2
VMEM = 48 * 1024 * 1024
TILE = 256
BF16 = jnp.bfloat16
F32 = jnp.float32
SMEM_SPEC = pl.BlockSpec(memory_space=pltpu.SMEM)
VMEM_SPEC = pl.BlockSpec(memory_space=pltpu.VMEM)
ANY_SPEC = pl.BlockSpec(memory_space=pl.ANY)


def params(limit=VMEM):
    return pltpu.CompilerParams(vmem_limit_bytes=limit)


def cost(flops, bytes_accessed):
    return pl.CostEstimate(flops=flops, bytes_accessed=bytes_accessed, transcendentals=0)


def ones_where(cond):
    return jnp.where(cond, 1.0, 0.0).astype(BF16)


def iota(shape, axis):
    return lax.broadcasted_iota(jnp.int32, shape, axis)


def loop(n, unroll):
    def run(f):
        if unroll:
            for i in range(n):
                f(i)
        else:
            pl.loop(0, n)(f)

    return run


def span(i, size):
    return pl.ds(i * size if isinstance(i, int) else pl.multiple_of(i * size, size), size)


def place_row(count_ref, base, atoms, width):
    lane = iota((1, atoms * width), 1)

    def atom(a, carry):
        place, offset = carry
        count = count_ref[base + a]
        inside = (lane >= a * width) & (lane < a * width + count)
        return jnp.where(inside, lane - a * width + offset, place), offset + count

    return lax.fori_loop(0, atoms, atom, (jnp.full(lane.shape, -1, jnp.int32), jnp.int32(0)))[0]


def pack_rows(count_ref, base, atoms, width, size):
    place = place_row(count_ref, base, atoms, width)
    return ones_where(iota((size, atoms * width), 0) == place)


def pack_cols(count_ref, base, atoms, width, size, out, unroll):
    def atom(a, offset):
        count = count_ref[base + a]
        slot = iota((width, size), 0)
        gap = iota((width, size), 1) - slot
        out[span(a, width), :] = ones_where((gap == offset) & (slot < count))
        return offset + count

    if unroll:
        offset = jnp.int32(0)
        for a in range(atoms):
            offset = atom(a, offset)
    else:
        lax.fori_loop(0, atoms, atom, jnp.int32(0))


def first_fit(basis_count, ri_count, groups, levels):
    def body(count_ref, ri_ref, o_ref):
        level = jnp.int32(0)
        for axis, (ref, parts) in enumerate(zip((count_ref, count_ref, ri_ref), groups)):
            per = ref.shape[0] // parts
            most = jnp.int32(0)
            for g in range(parts):
                total = jnp.int32(0)
                for i in range(per):
                    total = total + ref[g * per + i]
                most = jnp.maximum(most, total)
            for n, sizes in enumerate(levels[:-1]):
                level = jnp.where(most > sizes[axis], jnp.maximum(level, n + 1), level)
        o_ref[0] = level

    return pl.pallas_call(
        body,
        out_shape=jax.ShapeDtypeStruct((1,), jnp.int32),
        in_specs=[SMEM_SPEC, SMEM_SPEC],
        out_specs=SMEM_SPEC,
        name="first_fit",
    )(basis_count, ri_count)


def pack_integrals(tc, block_mask, basis_count, ri_count, ncols, packed, unroll, arrived=None):
    rows, cols = tc.shape
    atoms = rows // BW
    wide = cols // ncols
    blocks = wide // RW
    chips = ncols // CORES
    first = arrived is None

    def body(count_ref, ri_ref, mask_ref, x_ref, *refs):
        outs = refs[:1] if first else refs[1 : 1 + chips]
        held, hot = refs[-2:] if first else refs[-3:-1]
        made = outs[0] if first else refs[-1]
        row, col = lax.axis_index("row"), lax.axis_index("col")
        base = (row * ncols + col) * atoms

        @loop(chips, unroll)
        def _(t):
            dest = col ^ (CORES * t + (1 if first else 0))

            @loop(blocks, unroll)
            def _(b):
                lanes = pl.ds(pl.multiple_of(dest * wide + b * RW, RW), RW)
                slot = iota((BW, RW), 0)
                for a in range(atoms):
                    limit = jnp.where(mask_ref[a, dest * blocks + b] > 0, count_ref[base + a], 0)
                    x = x_ref[pl.ds(a * BW, BW), lanes].astype(F32)
                    held[pl.ds(a * BW, BW), span(b, RW)] = jnp.where(slot < limit, x, 0.0).astype(BF16)

            pack_cols(ri_ref, dest * blocks, blocks, RW, packed, hot, unroll)
            made[t] = jnp.dot(held[...], hot[...], preferred_element_type=F32).astype(BF16)

        if not first:
            core = lax.rem(col, CORES)
            for t in range(chips):
                outs[t][pl.ds(pl.multiple_of(core * rows, rows), rows), :] = made[t]
                outs[t][pl.ds(pl.multiple_of((1 - core) * rows, rows), rows), :] = refs[0][t]

    shape = (chips, rows, packed)
    merged = jax.ShapeDtypeStruct((CORES * rows, packed), BF16)
    out_shape = [jax.ShapeDtypeStruct(shape, BF16)] if first else [merged] * chips
    out_specs = [VMEM_SPEC] * len(out_shape)
    return pl.pallas_call(
        body,
        out_shape=out_shape,
        in_specs=[SMEM_SPEC, SMEM_SPEC, SMEM_SPEC] + [VMEM_SPEC] * (1 if first else 2),
        out_specs=out_specs,
        scratch_shapes=[pltpu.VMEM((rows, wide), BF16), pltpu.VMEM((wide, packed), BF16)]
        + ([] if first else [pltpu.VMEM(shape, BF16)]),
        compiler_params=params(),
        cost_estimate=cost(rows * cols * packed, rows * cols + 3 * chips * rows * packed),
        name="pack_other_core" if first else "pack_own_core",
    )(basis_count, ri_count, block_mask, tc, *([] if first else [arrived]))


def pack_density(dens, mask, basis_count, lam_size, sum_size, unroll):
    rows, cols = dens.shape
    lam_atoms, sum_atoms = mask.shape
    steps = 1 if unroll else 4
    tile = rows // steps
    out_tile = lam_size // steps

    def body(count_ref, mask_ref, x_ref, o_ref, upper_ref, lower_ref, hot, keep, mid):
        row, col = lax.axis_index("row"), lax.axis_index("col")
        first = iota((sum_atoms, cols), 0) * BW
        lane = iota((sum_atoms, cols), 1)
        of_atom = ones_where((lane >= first) & (lane < first + BW))
        keep[...] = jnp.dot(ones_where(mask_ref[...] > 0), of_atom, preferred_element_type=F32).astype(BF16)
        pack_cols(count_ref, col * sum_atoms, sum_atoms, BW, sum_size, hot, unroll)

        @loop(steps, unroll)
        def _(i):
            at = span(i, tile)
            shape = (tile, lam_atoms)
            first = iota(shape, 1) * BW - i * tile
            atom = ones_where((iota(shape, 0) >= first) & (iota(shape, 0) < first + BW))
            kept = jnp.dot(atom, keep[...], preferred_element_type=F32)
            x = jnp.where(kept > 0.5, x_ref[at, :].astype(F32), 0.0).astype(BF16)
            mid[at, :] = jnp.dot(x, hot[...], preferred_element_type=F32).astype(BF16)

        place = place_row(count_ref, row * lam_atoms, lam_atoms, BW)

        @loop(steps, unroll)
        def _(i):
            at = span(i, out_tile)
            left = ones_where(iota((out_tile, rows), 0) + i * out_tile == place)
            o_ref[at, :] = jnp.dot(left, mid[...], preferred_element_type=F32).astype(BF16)

        upper_ref[...] = o_ref[pl.ds(0, TILE), :]
        lower_ref[...] = o_ref[pl.ds(TILE, lam_size - TILE), :]

    return pl.pallas_call(
        body,
        out_shape=[jax.ShapeDtypeStruct((n, sum_size), BF16) for n in (lam_size, TILE, lam_size - TILE)],
        in_specs=[SMEM_SPEC, VMEM_SPEC, VMEM_SPEC],
        out_specs=[VMEM_SPEC] * 3,
        scratch_shapes=[
            pltpu.VMEM((cols, sum_size), BF16),
            pltpu.VMEM((lam_atoms, cols), BF16),
            pltpu.VMEM((rows, sum_size), BF16),
        ],
        compiler_params=params(),
        cost_estimate=cost(2 * rows * sum_size * (cols + lam_size), 2 * rows * cols),
        name="pack_density",
    )(basis_count, mask, dens)


def pack_part(pieces, basis_count, first, ncols, size):
    rows, cols = pieces[0].shape
    per = len(pieces)
    depth = per * rows
    atoms = depth // BW

    def body(count_ref, *refs):
        blocks, o_ref, full = refs[:per], refs[per], refs[per + 1]
        row, chip = lax.axis_index("row"), lax.axis_index("col") // CORES
        for i in range(per):
            at = lax.rem(chip ^ (first + i), per) * rows
            full[pl.ds(pl.multiple_of(at, rows), rows), :] = blocks[i][...]
        part = (row * (ncols // CORES) + (chip ^ first)) * rows // depth
        hot = pack_rows(count_ref, part * atoms, atoms, BW, size)
        o_ref[...] = jnp.dot(hot, full[...], preferred_element_type=F32).astype(BF16)

    return pl.pallas_call(
        body,
        out_shape=jax.ShapeDtypeStruct((size, cols), BF16),
        in_specs=[SMEM_SPEC] + [VMEM_SPEC] * per,
        out_specs=VMEM_SPEC,
        scratch_shapes=[pltpu.VMEM((depth, cols), BF16)],
        compiler_params=params(),
        cost_estimate=cost((2 + 10 * first) * size * depth * cols, 2 * cols * (depth + size)),
        name="pack_part",
    )(basis_count, *pieces)


def exchange(x, axis, bit):
    peers = lax.axis_size(axis)
    return lax.ppermute(x, axis, [(i, i ^ bit) for i in range(peers)])


def after(x, *others):
    return lax.optimization_barrier((x, *others))[0]


def double(own, axis, bits):
    have = {0: own}
    for bit in bits:
        for far in sorted(have):
            have[far | bit] = exchange(have[far], axis, bit)
    return have


def add_parts(total, unroll, d_refs, sums, before=None):
    lam, cols = total.shape

    @loop(lam // TILE, unroll)
    def _(j):
        out = span(j, TILE)
        x = None if before is None else before[out, :]
        for chunks, part in zip(d_refs, sums):
            if len(chunks) == 1:
                d = chunks[0][out, :]
            elif isinstance(j, int):
                d = chunks[0][...] if j == 0 else chunks[1][span(j - 1, TILE), :]
            else:
                d = chunks[1][span(jnp.maximum(j - 1, 0), TILE), :].astype(F32)
                d = jnp.where(j == 0, chunks[0][...].astype(F32), d).astype(BF16)
            y = jnp.dot(d, part(), preferred_element_type=F32)
            x = y if x is None else x + y
        total[out, :] = x


def split_refs(dens, refs):
    lists, at = [], 0
    for chunks in dens.values():
        lists.append(refs[at : at + len(chunks)])
        at += len(chunks)
    return lists, refs[at:]


def flat(dens):
    return [chunk for chunks in dens.values() for chunk in chunks]


def ways_back(basis_count, ri_count, nrows, ncols, rows, wide, lam, cols, unroll):
    lam_atoms, blocks = rows // BW, wide // RW

    def body(count_ref, ri_ref, lam_hot, col_hot):
        row, col = lax.axis_index("row"), lax.axis_index("col")
        pack_cols(count_ref, row * lam_atoms, lam_atoms, BW, lam, lam_hot, unroll)
        place = place_row(ri_ref, col * blocks, blocks, RW)

        @loop(cols // RW, unroll)
        def _(i):
            col_hot[span(i, RW), :] = ones_where(iota((RW, wide), 0) + i * RW == place)

    return pl.pallas_call(
        body,
        out_shape=[jax.ShapeDtypeStruct((rows, lam), BF16), jax.ShapeDtypeStruct((cols, wide), BF16)],
        in_specs=[SMEM_SPEC, SMEM_SPEC],
        out_specs=[VMEM_SPEC] * 2,
        compiler_params=params(16 * 1024 * 1024),
        name="ways_back",
    )(basis_count, ri_count)


def contract_near(dens, integrals, ncols, unroll):
    lam, depth = dens[0][0].shape
    groups, nrows = len(integrals), len(integrals[0])
    sums = [integrals[g][far] for far in range(nrows) for g in range(groups)]
    cols = sums[0].shape[1]
    n, parts = len(dens), len(sums)

    def body(*refs):
        d_refs, refs = split_refs(dens, refs)
        s_refs, refs = refs[:parts], refs[parts:]
        total, s_rest, s_all, s_sem, r_sem = refs
        row, col = lax.axis_index("row"), lax.axis_index("col")
        for j, ref in enumerate(s_refs):
            part = (row ^ (j // groups)) * groups + (col // (ncols // groups) ^ (j % groups))
            pltpu.make_async_copy(ref, s_all.at[part], s_sem.at[part]).start()

        @pl.loop(0, parts)
        def _(i):
            pltpu.make_async_copy(s_all.at[i], s_all.at[i], s_sem.at[i]).wait()

        rest = [
            pltpu.make_async_copy(s_all.at[col ^ far], s_rest.at[far - n], r_sem.at[far - n])
            for far in range(n, parts)
        ]
        for copy in rest:
            copy.start()
        add_parts(total, unroll, d_refs, [lambda far=far: s_all[col ^ far] for far in range(n)])
        for copy in rest:
            copy.wait()

    need = 2 * (n * depth * lam + 2 * parts * depth * cols + 4 * lam * cols)
    return pl.pallas_call(
        body,
        out_shape=[
            jax.ShapeDtypeStruct((lam, cols), F32),
            jax.ShapeDtypeStruct((parts - n, depth, cols), BF16),
        ],
        in_specs=[VMEM_SPEC] * n + [ANY_SPEC] * parts,
        out_specs=[VMEM_SPEC] * 2,
        scratch_shapes=[
            pltpu.VMEM((parts, depth, cols), BF16),
            pltpu.SemaphoreType.DMA((parts,)),
            pltpu.SemaphoreType.DMA((parts - n,)),
        ],
        compiler_params=params(need + 4 * 1024 * 1024),
        cost_estimate=cost(2 * n * depth * lam * cols, 2 * n * depth * (lam + cols)),
        name="contract_near",
    )(*flat(dens), *sums)


def contract_far(dens, first, total, sums, unroll):
    (lam, cols), depth = total.shape, sums.shape[1]
    n = len(dens)

    def body(before, s_ref, *refs):
        d_refs, (o_ref,) = split_refs(dens, refs)
        add_parts(o_ref, unroll, d_refs, [lambda i=i: s_ref[first + i] for i in range(n)], before)

    need = 2 * (n * depth * lam + sums.size + 4 * lam * cols)
    return pl.pallas_call(
        body,
        out_shape=jax.ShapeDtypeStruct((lam, cols), F32),
        in_specs=[VMEM_SPEC] * (2 + len(flat(dens))),
        out_specs=VMEM_SPEC,
        compiler_params=params(need + 4 * 1024 * 1024),
        cost_estimate=cost(2 * n * depth * lam * cols, 2 * n * depth * (lam + cols)),
        name="contract_far",
    )(total, sums, *flat(dens))


def contract_last(dens, first, total, sums, lam_hot, col_hot, unroll):
    (rows, lam), (cols, wide) = lam_hot.shape, col_hot.shape
    depth = sums.shape[1]
    n = len(dens)
    half = lam // 2

    def body(before, s_ref, lam_hot, col_hot, *refs):
        d_refs, (o_ref, total, packed) = split_refs(dens, refs)
        add_parts(total, unroll, d_refs, [lambda i=i: s_ref[first + i] for i in range(n)], before)

        @loop(2, unroll)
        def _(j):
            x = total[span(j, half), :].astype(BF16)
            packed[span(j, half), :] = jnp.dot(x, col_hot[...], preferred_element_type=F32).astype(BF16)

        @loop(4, unroll)
        def _(j):
            out = span(j, rows // 4)
            o_ref[out, :] = jnp.dot(lam_hot[out, :], packed[...], preferred_element_type=F32).astype(BF16)

    need = 2 * (n * depth * lam + sums.size + 4 * lam * cols + rows * lam + cols * wide + (lam + rows) * wide)
    return pl.pallas_call(
        body,
        out_shape=jax.ShapeDtypeStruct((rows, wide), BF16),
        in_specs=[VMEM_SPEC] * (4 + len(flat(dens))),
        out_specs=VMEM_SPEC,
        scratch_shapes=[pltpu.VMEM((lam, cols), F32), pltpu.VMEM((lam, wide), BF16)],
        compiler_params=params(need + 4 * 1024 * 1024),
        cost_estimate=cost(2 * n * depth * lam * cols, 2 * n * depth * (lam + cols)),
        name="contract_last",
    )(total, sums, lam_hot, col_hot, *flat(dens))


def program(lam_size, sum_size, col_size, common):
    unroll = common

    def run(three_center, density, block_mask, density_mask, basis_count, ri_count):
        ncols = lax.axis_size("col")
        nrows = lax.axis_size("row")
        chips = ncols // CORES
        rows, depth = density.shape
        wide = three_center.shape[1] // ncols
        row_bits = [1 << b for b in range(nrows.bit_length() - 1)]
        chip_bits = [CORES << b for b in range(chips.bit_length() - 1)][::-1]
        far_bit, near_bits = chip_bits[0], chip_bits[1:]

        counts = (block_mask, basis_count, ri_count, ncols, col_size, unroll)
        other = exchange(pack_integrals(three_center, *counts)[0], "col", 1)
        own, upper, lower = pack_density(density, density_mask, basis_count, lam_size, sum_size, unroll)
        lines = [{0: upper, far_bit: exchange(upper, "col", far_bit)}, {0: lower}]
        near = {0: own, 1: exchange(own, "col", 1)}
        pieces = pack_integrals(three_center, *counts, after(other, own))
        early = lines[0][far_bit]
        got = [pieces[0]] + [exchange(pieces[t], "col", CORES * t) for t in range(1, chips)]
        per = depth // pieces[0].shape[0]
        lam_hot, col_hot = ways_back(
            basis_count, ri_count, nrows, ncols, rows, wide, lam_size, col_size, unroll
        )
        parts, groups, orders = [], [], []
        for g in range(chips // per):
            arrived = got[g * per : (g + 1) * per]
            if g == 0:
                arrived = [after(arrived[0], near[1], early)] + arrived[1:]
            elif g == 1:
                arrived = [after(arrived[0], lam_hot)] + arrived[1:]
            part = pack_part(arrived, basis_count, g * per, ncols, sum_size)
            if g == 0:
                near.update(double(after(own, part), "col", near_bits))
                steps = [near[far] for far in near if far > 1]
            else:
                part = after(part, *[groups[0][bit] for bit in row_bits])
            parts.append(part)
            orders.append(row_bits if g % 2 == 0 else row_bits[::-1])
            groups.append({0: part})
            for bit in orders[g]:
                groups[g][bit] = exchange(part, "row", bit)
        step = groups[-1][orders[-1][0]]
        across = exchange(after(early, parts[-1]), "col", 1)
        forward = double(after(early, across, *steps), "col", near_bits)
        lines[0].update({far_bit | far: block for far, block in forward.items() if far > 0})
        lines[1][far_bit] = exchange(after(lower, parts[-1]), "col", far_bit)
        for far in [far for far in near if far > 1]:
            near[far | 1] = exchange(near[far], "col", 1)
        for g, have in enumerate(groups):
            done = [0, orders[g][0]]
            for bit in orders[g][1:]:
                for far in done[1:]:
                    block = have[far] if g == len(groups) - 1 else after(have[far], step, *near.values())
                    have[far | bit] = exchange(block, "row", bit)
                done += [far | bit for far in done]
        first = {far: [near[far]] for far in sorted(near)}
        total, sums = contract_near(first, groups, ncols, unroll)
        block = after(lines[1][far_bit], lines[0][ncols - CORES])
        for away, block in double(block, "col", near_bits).items():
            lines[1][far_bit | away] = block
        middle = {}
        for far in range(far_bit, ncols - CORES, CORES):
            middle[far] = [line[far] for line in lines]
            middle[far | 1] = [across if line[far] is early else exchange(line[far], "col", 1) for line in lines]
        total = contract_far(middle, 0, total, sums, unroll)
        ends = [line[ncols - CORES] for line in lines]
        last = {ncols - CORES: ends}
        last[ncols - 1] = [exchange(ends[0], "col", 1), exchange(after(ends[1], total), "col", 1)]
        return contract_last(last, len(middle), total, sums, lam_hot, col_hot, unroll)

    return run


def choose(here, yes, no):
    return lambda *args: lax.cond(here, yes, no, *args)


def shards(three_center, density, block_mask, density_mask, basis_count, ri_count):
    ncols = lax.axis_size("col")
    nrows = lax.axis_size("row")
    rows, depth = density.shape
    wide = three_center.shape[1] // ncols
    levels = (
        (rows * 3 // 4, depth * 3 // 4, wide * 5 // 6),
        (rows * 3 // 4, depth, wide * 5 // 6),
        (rows * 3 // 4, depth, wide),
        (rows, depth, wide),
    )
    level = first_fit(basis_count, ri_count, (nrows, ncols, ncols), levels)
    args = (three_center, density, block_mask, density_mask, basis_count, ri_count)
    run = program(*levels[-1], False)
    for n in reversed(range(len(levels) - 1)):
        run = choose(level[0] == n, program(*levels[n], n == 0), run)
    return run(*args)


def solution(mesh):
    in_specs = (
        P(("row", "col"), None),
        P("row", "col"),
        P(("row", "col"), None),
        P("row", "col"),
        P(),
        P(),
    )
    return jax.shard_map(
        shards, mesh=mesh, in_specs=in_specs, out_specs=P("row", "col"), check_vma=False
    )
```

```python
import jax
import jax.numpy as jnp
from jax import lax
from jax.experimental import pallas as pl
from jax.experimental.pallas import tpu as pltpu
from jax.sharding import PartitionSpec as P

BW = 32
RW = 128
CORES = 2
VMEM = 48 * 1024 * 1024
TILE = 256
BF16 = jnp.bfloat16
F32 = jnp.float32
SMEM_SPEC = pl.BlockSpec(memory_space=pltpu.SMEM)
VMEM_SPEC = pl.BlockSpec(memory_space=pltpu.VMEM)
ANY_SPEC = pl.BlockSpec(memory_space=pl.ANY)


def params(limit=VMEM):
    return pltpu.CompilerParams(vmem_limit_bytes=limit)


def cost(flops, bytes_accessed):
    return pl.CostEstimate(flops=flops, bytes_accessed=bytes_accessed, transcendentals=0)


def ones_where(cond):
    return jnp.where(cond, 1.0, 0.0).astype(BF16)


def iota(shape, axis):
    return lax.broadcasted_iota(jnp.int32, shape, axis)


def loop(n, unroll):
    def run(f):
        if unroll:
            for i in range(n):
                f(i)
        else:
            pl.loop(0, n)(f)

    return run


def span(i, size):
    return pl.ds(i * size if isinstance(i, int) else pl.multiple_of(i * size, size), size)


def place_row(count_ref, base, atoms, width):
    lane = iota((1, atoms * width), 1)

    def atom(a, carry):
        place, offset = carry
        count = count_ref[base + a]
        inside = (lane >= a * width) & (lane < a * width + count)
        return jnp.where(inside, lane - a * width + offset, place), offset + count

    return lax.fori_loop(0, atoms, atom, (jnp.full(lane.shape, -1, jnp.int32), jnp.int32(0)))[0]


def pack_rows(count_ref, base, atoms, width, size):
    place = place_row(count_ref, base, atoms, width)
    return ones_where(iota((size, atoms * width), 0) == place)


def pack_cols(count_ref, base, atoms, width, size, out, unroll):
    def atom(a, offset):
        count = count_ref[base + a]
        slot = iota((width, size), 0)
        gap = iota((width, size), 1) - slot
        out[span(a, width), :] = ones_where((gap == offset) & (slot < count))
        return offset + count

    if unroll:
        offset = jnp.int32(0)
        for a in range(atoms):
            offset = atom(a, offset)
    else:
        lax.fori_loop(0, atoms, atom, jnp.int32(0))


def first_fit(basis_count, ri_count, groups, levels):
    def body(count_ref, ri_ref, o_ref):
        level = jnp.int32(0)
        for axis, (ref, parts) in enumerate(zip((count_ref, count_ref, ri_ref), groups)):
            per = ref.shape[0] // parts
            most = jnp.int32(0)
            for g in range(parts):
                total = jnp.int32(0)
                for i in range(per):
                    total = total + ref[g * per + i]
                most = jnp.maximum(most, total)
            for n, sizes in enumerate(levels[:-1]):
                level = jnp.where(most > sizes[axis], jnp.maximum(level, n + 1), level)
        o_ref[0] = level

    return pl.pallas_call(
        body,
        out_shape=jax.ShapeDtypeStruct((1,), jnp.int32),
        in_specs=[SMEM_SPEC, SMEM_SPEC],
        out_specs=SMEM_SPEC,
        name="first_fit",
    )(basis_count, ri_count)


def pack_integrals(tc, block_mask, basis_count, ri_count, ncols, packed, unroll, arrived=None):
    rows, cols = tc.shape
    atoms = rows // BW
    wide = cols // ncols
    blocks = wide // RW
    chips = ncols // CORES
    first = arrived is None

    def body(count_ref, ri_ref, mask_ref, x_ref, *refs):
        outs = refs[:1] if first else refs[1 : 1 + chips]
        held, hot = refs[-2:] if first else refs[-3:-1]
        made = outs[0] if first else refs[-1]
        row, col = lax.axis_index("row"), lax.axis_index("col")
        base = (row * ncols + col) * atoms

        @loop(chips, unroll)
        def _(t):
            dest = col ^ (CORES * t + (1 if first else 0))

            @loop(blocks, unroll)
            def _(b):
                lanes = pl.ds(pl.multiple_of(dest * wide + b * RW, RW), RW)
                slot = iota((BW, RW), 0)
                for a in range(atoms):
                    limit = jnp.where(mask_ref[a, dest * blocks + b] > 0, count_ref[base + a], 0)
                    x = x_ref[pl.ds(a * BW, BW), lanes].astype(F32)
                    held[pl.ds(a * BW, BW), span(b, RW)] = jnp.where(slot < limit, x, 0.0).astype(BF16)

            pack_cols(ri_ref, dest * blocks, blocks, RW, packed, hot, unroll)
            made[t] = jnp.dot(held[...], hot[...], preferred_element_type=F32).astype(BF16)

        if not first:
            core = lax.rem(col, CORES)
            for t in range(chips):
                outs[t][pl.ds(pl.multiple_of(core * rows, rows), rows), :] = made[t]
                outs[t][pl.ds(pl.multiple_of((1 - core) * rows, rows), rows), :] = refs[0][t]

    shape = (chips, rows, packed)
    merged = jax.ShapeDtypeStruct((CORES * rows, packed), BF16)
    out_shape = [jax.ShapeDtypeStruct(shape, BF16)] if first else [merged] * chips
    out_specs = [VMEM_SPEC] * len(out_shape)
    return pl.pallas_call(
        body,
        out_shape=out_shape,
        in_specs=[SMEM_SPEC, SMEM_SPEC, SMEM_SPEC] + [VMEM_SPEC] * (1 if first else 2),
        out_specs=out_specs,
        scratch_shapes=[pltpu.VMEM((rows, wide), BF16), pltpu.VMEM((wide, packed), BF16)]
        + ([] if first else [pltpu.VMEM(shape, BF16)]),
        compiler_params=params(),
        cost_estimate=cost(rows * cols * packed, rows * cols + 3 * chips * rows * packed),
        name="pack_other_core" if first else "pack_own_core",
    )(basis_count, ri_count, block_mask, tc, *([] if first else [arrived]))


def pack_density(dens, mask, basis_count, lam_size, sum_size, unroll):
    rows, cols = dens.shape
    lam_atoms, sum_atoms = mask.shape
    steps = 1 if unroll else 4
    tile = rows // steps
    out_tile = lam_size // steps

    def body(count_ref, mask_ref, x_ref, o_ref, upper_ref, lower_ref, hot, keep, mid):
        row, col = lax.axis_index("row"), lax.axis_index("col")
        first = iota((sum_atoms, cols), 0) * BW
        lane = iota((sum_atoms, cols), 1)
        of_atom = ones_where((lane >= first) & (lane < first + BW))
        keep[...] = jnp.dot(ones_where(mask_ref[...] > 0), of_atom, preferred_element_type=F32).astype(BF16)
        pack_cols(count_ref, col * sum_atoms, sum_atoms, BW, sum_size, hot, unroll)

        @loop(steps, unroll)
        def _(i):
            at = span(i, tile)
            shape = (tile, lam_atoms)
            first = iota(shape, 1) * BW - i * tile
            atom = ones_where((iota(shape, 0) >= first) & (iota(shape, 0) < first + BW))
            kept = jnp.dot(atom, keep[...], preferred_element_type=F32)
            x = jnp.where(kept > 0.5, x_ref[at, :].astype(F32), 0.0).astype(BF16)
            mid[at, :] = jnp.dot(x, hot[...], preferred_element_type=F32).astype(BF16)

        place = place_row(count_ref, row * lam_atoms, lam_atoms, BW)

        @loop(steps, unroll)
        def _(i):
            at = span(i, out_tile)
            left = ones_where(iota((out_tile, rows), 0) + i * out_tile == place)
            o_ref[at, :] = jnp.dot(left, mid[...], preferred_element_type=F32).astype(BF16)

        upper_ref[...] = o_ref[pl.ds(0, TILE), :]
        lower_ref[...] = o_ref[pl.ds(TILE, lam_size - TILE), :]

    return pl.pallas_call(
        body,
        out_shape=[jax.ShapeDtypeStruct((n, sum_size), BF16) for n in (lam_size, TILE, lam_size - TILE)],
        in_specs=[SMEM_SPEC, VMEM_SPEC, VMEM_SPEC],
        out_specs=[VMEM_SPEC] * 3,
        scratch_shapes=[
            pltpu.VMEM((cols, sum_size), BF16),
            pltpu.VMEM((lam_atoms, cols), BF16),
            pltpu.VMEM((rows, sum_size), BF16),
        ],
        compiler_params=params(),
        cost_estimate=cost(2 * rows * sum_size * (cols + lam_size), 2 * rows * cols),
        name="pack_density",
    )(basis_count, mask, dens)


def pack_part(pieces, basis_count, first, ncols, size):
    rows, cols = pieces[0].shape
    per = len(pieces)
    depth = per * rows
    atoms = depth // BW

    def body(count_ref, *refs):
        blocks, o_ref, full = refs[:per], refs[per], refs[per + 1]
        row, chip = lax.axis_index("row"), lax.axis_index("col") // CORES
        for i in range(per):
            at = lax.rem(chip ^ (first + i), per) * rows
            full[pl.ds(pl.multiple_of(at, rows), rows), :] = blocks[i][...]
        part = (row * (ncols // CORES) + (chip ^ first)) * rows // depth
        hot = pack_rows(count_ref, part * atoms, atoms, BW, size)
        o_ref[...] = jnp.dot(hot, full[...], preferred_element_type=F32).astype(BF16)

    return pl.pallas_call(
        body,
        out_shape=jax.ShapeDtypeStruct((size, cols), BF16),
        in_specs=[SMEM_SPEC] + [VMEM_SPEC] * per,
        out_specs=VMEM_SPEC,
        scratch_shapes=[pltpu.VMEM((depth, cols), BF16)],
        compiler_params=params(),
        cost_estimate=cost((2 + 40 * first) * size * depth * cols, 2 * cols * (depth + size)),
        name="pack_part",
    )(basis_count, *pieces)


def exchange(x, axis, bit):
    peers = lax.axis_size(axis)
    return lax.ppermute(x, axis, [(i, i ^ bit) for i in range(peers)])


def after(x, *others):
    return lax.optimization_barrier((x, *others))[0]


def double(own, axis, bits):
    have = {0: own}
    for bit in bits:
        for far in sorted(have):
            have[far | bit] = exchange(have[far], axis, bit)
    return have


def add_parts(total, unroll, d_refs, sums, before=None):
    lam, cols = total.shape

    @loop(lam // TILE, unroll)
    def _(j):
        out = span(j, TILE)
        x = None if before is None else before[out, :]
        for chunks, part in zip(d_refs, sums):
            if len(chunks) == 1:
                d = chunks[0][out, :]
            elif isinstance(j, int):
                d = chunks[0][...] if j == 0 else chunks[1][span(j - 1, TILE), :]
            else:
                d = chunks[1][span(jnp.maximum(j - 1, 0), TILE), :].astype(F32)
                d = jnp.where(j == 0, chunks[0][...].astype(F32), d).astype(BF16)
            y = jnp.dot(d, part(), preferred_element_type=F32)
            x = y if x is None else x + y
        total[out, :] = x


def split_refs(dens, refs):
    lists, at = [], 0
    for chunks in dens.values():
        lists.append(refs[at : at + len(chunks)])
        at += len(chunks)
    return lists, refs[at:]


def flat(dens):
    return [chunk for chunks in dens.values() for chunk in chunks]


def ways_back(basis_count, ri_count, nrows, ncols, rows, wide, lam, cols, unroll):
    lam_atoms, blocks = rows // BW, wide // RW

    def body(count_ref, ri_ref, lam_hot, col_hot):
        row, col = lax.axis_index("row"), lax.axis_index("col")
        pack_cols(count_ref, row * lam_atoms, lam_atoms, BW, lam, lam_hot, unroll)
        place = place_row(ri_ref, col * blocks, blocks, RW)

        @loop(cols // RW, unroll)
        def _(i):
            col_hot[span(i, RW), :] = ones_where(iota((RW, wide), 0) + i * RW == place)

    return pl.pallas_call(
        body,
        out_shape=[jax.ShapeDtypeStruct((rows, lam), BF16), jax.ShapeDtypeStruct((cols, wide), BF16)],
        in_specs=[SMEM_SPEC, SMEM_SPEC],
        out_specs=[VMEM_SPEC] * 2,
        compiler_params=params(16 * 1024 * 1024),
        name="ways_back",
    )(basis_count, ri_count)


def contract_near(dens, integrals, ncols, unroll):
    lam, depth = dens[0][0].shape
    groups, nrows = len(integrals), len(integrals[0])
    sums = [integrals[g][far] for far in range(nrows) for g in range(groups)]
    cols = sums[0].shape[1]
    n, parts = len(dens), len(sums)

    def body(*refs):
        d_refs, refs = split_refs(dens, refs)
        s_refs, refs = refs[:parts], refs[parts:]
        total, s_rest, s_all, s_sem, r_sem = refs
        row, col = lax.axis_index("row"), lax.axis_index("col")
        for j, ref in enumerate(s_refs):
            part = (row ^ (j // groups)) * groups + (col // (ncols // groups) ^ (j % groups))
            pltpu.make_async_copy(ref, s_all.at[part], s_sem.at[part]).start()

        @pl.loop(0, parts)
        def _(i):
            pltpu.make_async_copy(s_all.at[i], s_all.at[i], s_sem.at[i]).wait()

        rest = [
            pltpu.make_async_copy(s_all.at[col ^ far], s_rest.at[far - n], r_sem.at[far - n])
            for far in range(n, parts)
        ]
        for copy in rest:
            copy.start()
        add_parts(total, unroll, d_refs, [lambda far=far: s_all[col ^ far] for far in range(n)])
        for copy in rest:
            copy.wait()

    need = 2 * (n * depth * lam + 2 * parts * depth * cols + 4 * lam * cols)
    return pl.pallas_call(
        body,
        out_shape=[
            jax.ShapeDtypeStruct((lam, cols), F32),
            jax.ShapeDtypeStruct((parts - n, depth, cols), BF16),
        ],
        in_specs=[VMEM_SPEC] * n + [ANY_SPEC] * parts,
        out_specs=[VMEM_SPEC] * 2,
        scratch_shapes=[
            pltpu.VMEM((parts, depth, cols), BF16),
            pltpu.SemaphoreType.DMA((parts,)),
            pltpu.SemaphoreType.DMA((parts - n,)),
        ],
        compiler_params=params(need + 4 * 1024 * 1024),
        cost_estimate=cost(2 * n * depth * lam * cols, 2 * n * depth * (lam + cols)),
        name="contract_near",
    )(*flat(dens), *sums)


def contract_far(dens, first, total, sums, unroll):
    (lam, cols), depth = total.shape, sums.shape[1]
    n = len(dens)

    def body(before, s_ref, *refs):
        d_refs, (o_ref,) = split_refs(dens, refs)
        add_parts(o_ref, unroll, d_refs, [lambda i=i: s_ref[first + i] for i in range(n)], before)

    need = 2 * (n * depth * lam + sums.size + 4 * lam * cols)
    return pl.pallas_call(
        body,
        out_shape=jax.ShapeDtypeStruct((lam, cols), F32),
        in_specs=[VMEM_SPEC] * (2 + len(flat(dens))),
        out_specs=VMEM_SPEC,
        compiler_params=params(need + 4 * 1024 * 1024),
        cost_estimate=cost(2 * n * depth * lam * cols, 2 * n * depth * (lam + cols)),
        name="contract_far",
    )(total, sums, *flat(dens))


def contract_last(dens, first, total, sums, lam_hot, col_hot, unroll):
    (rows, lam), (cols, wide) = lam_hot.shape, col_hot.shape
    depth = sums.shape[1]
    n = len(dens)
    half = lam // 2

    def body(before, s_ref, lam_hot, col_hot, *refs):
        d_refs, (o_ref, total, packed) = split_refs(dens, refs)
        add_parts(total, unroll, d_refs, [lambda i=i: s_ref[first + i] for i in range(n)], before)

        @loop(2, unroll)
        def _(j):
            x = total[span(j, half), :].astype(BF16)
            packed[span(j, half), :] = jnp.dot(x, col_hot[...], preferred_element_type=F32).astype(BF16)

        @loop(4, unroll)
        def _(j):
            out = span(j, rows // 4)
            o_ref[out, :] = jnp.dot(lam_hot[out, :], packed[...], preferred_element_type=F32).astype(BF16)

    need = 2 * (n * depth * lam + sums.size + 4 * lam * cols + rows * lam + cols * wide + (lam + rows) * wide)
    return pl.pallas_call(
        body,
        out_shape=jax.ShapeDtypeStruct((rows, wide), BF16),
        in_specs=[VMEM_SPEC] * (4 + len(flat(dens))),
        out_specs=VMEM_SPEC,
        scratch_shapes=[pltpu.VMEM((lam, cols), F32), pltpu.VMEM((lam, wide), BF16)],
        compiler_params=params(need + 4 * 1024 * 1024),
        cost_estimate=cost(2 * n * depth * lam * cols, 2 * n * depth * (lam + cols)),
        name="contract_last",
    )(total, sums, lam_hot, col_hot, *flat(dens))


def program(lam_size, sum_size, col_size, common):
    unroll = common

    def run(three_center, density, block_mask, density_mask, basis_count, ri_count):
        ncols = lax.axis_size("col")
        nrows = lax.axis_size("row")
        chips = ncols // CORES
        rows, depth = density.shape
        wide = three_center.shape[1] // ncols
        row_bits = [1 << b for b in range(nrows.bit_length() - 1)]
        chip_bits = [CORES << b for b in range(chips.bit_length() - 1)][::-1]
        far_bit, near_bits = chip_bits[0], chip_bits[1:]

        counts = (block_mask, basis_count, ri_count, ncols, col_size, unroll)
        other = exchange(pack_integrals(three_center, *counts)[0], "col", 1)
        own, upper, lower = pack_density(density, density_mask, basis_count, lam_size, sum_size, unroll)
        lines = [{0: upper, far_bit: exchange(upper, "col", far_bit)}, {0: lower}]
        near = {0: own, 1: exchange(own, "col", 1)}
        pieces = pack_integrals(three_center, *counts, after(other, own))
        early = lines[0][far_bit]
        got = [pieces[0]] + [exchange(pieces[t], "col", CORES * t) for t in range(1, chips)]
        per = depth // pieces[0].shape[0]
        lam_hot, col_hot = ways_back(
            basis_count, ri_count, nrows, ncols, rows, wide, lam_size, col_size, unroll
        )
        parts, groups, orders = [], [], []
        for g in range(chips // per):
            arrived = got[g * per : (g + 1) * per]
            if g == 0:
                arrived = [after(arrived[0], near[1], early)] + arrived[1:]
            elif g == 1:
                arrived = [after(arrived[0], lam_hot)] + arrived[1:]
            part = pack_part(arrived, basis_count, g * per, ncols, sum_size)
            if g == 0:
                near.update(double(after(own, part), "col", near_bits))
                steps = [near[far] for far in near if far > 1]
            else:
                part = after(part, *[groups[0][bit] for bit in row_bits])
            parts.append(part)
            orders.append(row_bits if g % 2 == 0 else row_bits[::-1])
            groups.append({0: part})
            for bit in orders[g]:
                groups[g][bit] = exchange(part, "row", bit)
        step = groups[-1][orders[-1][0]]
        across = exchange(after(early, parts[-1]), "col", 1)
        forward = double(after(early, across, *steps), "col", near_bits)
        lines[0].update({far_bit | far: block for far, block in forward.items() if far > 0})
        lines[1][far_bit] = exchange(after(lower, parts[-1]), "col", far_bit)
        for far in [far for far in near if far > 1]:
            near[far | 1] = exchange(after(near[far], across), "col", 1)
        for g, have in enumerate(groups):
            done = [0, orders[g][0]]
            for bit in orders[g][1:]:
                for far in done[1:]:
                    block = have[far] if g == len(groups) - 1 else after(have[far], *[groups[-1][bit] for bit in row_bits])
                    have[far | bit] = exchange(block, "row", bit)
                done += [far | bit for far in done]
        first = {far: [near[far]] for far in sorted(near)}
        total, sums = contract_near(first, groups, ncols, unroll)
        block = after(lines[1][far_bit], lines[0][ncols - CORES])
        for away, block in double(block, "col", near_bits).items():
            lines[1][far_bit | away] = block
        middle = {}
        for far in range(far_bit, ncols - CORES, CORES):
            middle[far] = [line[far] for line in lines]
            middle[far | 1] = [across if line[far] is early else exchange(line[far], "col", 1) for line in lines]
        total = contract_far(middle, 0, total, sums, unroll)
        ends = [line[ncols - CORES] for line in lines]
        last = {ncols - CORES: ends}
        last[ncols - 1] = [exchange(ends[0], "col", 1), exchange(after(ends[1], total), "col", 1)]
        return contract_last(last, len(middle), total, sums, lam_hot, col_hot, unroll)

    return run


def choose(here, yes, no):
    return lambda *args: lax.cond(here, yes, no, *args)


def shards(three_center, density, block_mask, density_mask, basis_count, ri_count):
    ncols = lax.axis_size("col")
    nrows = lax.axis_size("row")
    rows, depth = density.shape
    wide = three_center.shape[1] // ncols
    levels = (
        (rows * 3 // 4, depth * 3 // 4, wide * 5 // 6),
        (rows * 3 // 4, depth, wide * 5 // 6),
        (rows * 3 // 4, depth, wide),
        (rows, depth, wide),
    )
    level = first_fit(basis_count, ri_count, (nrows, ncols, ncols), levels)
    args = (three_center, density, block_mask, density_mask, basis_count, ri_count)
    run = program(*levels[-1], False)
    for n in reversed(range(len(levels) - 1)):
        run = choose(level[0] == n, program(*levels[n], n == 0), run)
    return run(*args)


def solution(mesh):
    in_specs = (
        P(("row", "col"), None),
        P("row", "col"),
        P(("row", "col"), None),
        P("row", "col"),
        P(),
        P(),
    )
    return jax.shard_map(
        shards, mesh=mesh, in_specs=in_specs, out_specs=P("row", "col"), check_vma=False
    )
```

```python
import jax
import jax.numpy as jnp
from jax import lax
from jax.experimental import pallas as pl
from jax.experimental.pallas import tpu as pltpu
from jax.sharding import PartitionSpec as P

BW = 32
RW = 128
CORES = 2
VMEM = 48 * 1024 * 1024
TILE = 256
BF16 = jnp.bfloat16
F32 = jnp.float32
SMEM_SPEC = pl.BlockSpec(memory_space=pltpu.SMEM)
VMEM_SPEC = pl.BlockSpec(memory_space=pltpu.VMEM)
ANY_SPEC = pl.BlockSpec(memory_space=pl.ANY)


def params(limit=VMEM):
    return pltpu.CompilerParams(vmem_limit_bytes=limit)


def cost(flops, bytes_accessed):
    return pl.CostEstimate(flops=flops, bytes_accessed=bytes_accessed, transcendentals=0)


def ones_where(cond):
    return jnp.where(cond, 1.0, 0.0).astype(BF16)


def iota(shape, axis):
    return lax.broadcasted_iota(jnp.int32, shape, axis)


def loop(n, unroll):
    def run(f):
        if unroll:
            for i in range(n):
                f(i)
        else:
            pl.loop(0, n)(f)

    return run


def span(i, size):
    return pl.ds(i * size if isinstance(i, int) else pl.multiple_of(i * size, size), size)


def place_row(count_ref, base, atoms, width):
    lane = iota((1, atoms * width), 1)

    def atom(a, carry):
        place, offset = carry
        count = count_ref[base + a]
        inside = (lane >= a * width) & (lane < a * width + count)
        return jnp.where(inside, lane - a * width + offset, place), offset + count

    return lax.fori_loop(0, atoms, atom, (jnp.full(lane.shape, -1, jnp.int32), jnp.int32(0)))[0]


def pack_rows(count_ref, base, atoms, width, size):
    place = place_row(count_ref, base, atoms, width)
    return ones_where(iota((size, atoms * width), 0) == place)


def pack_cols(count_ref, base, atoms, width, size, out, unroll):
    def atom(a, offset):
        count = count_ref[base + a]
        slot = iota((width, size), 0)
        gap = iota((width, size), 1) - slot
        out[span(a, width), :] = ones_where((gap == offset) & (slot < count))
        return offset + count

    if unroll:
        offset = jnp.int32(0)
        for a in range(atoms):
            offset = atom(a, offset)
    else:
        lax.fori_loop(0, atoms, atom, jnp.int32(0))


def first_fit(basis_count, ri_count, groups, levels):
    def body(count_ref, ri_ref, o_ref):
        level = jnp.int32(0)
        for axis, (ref, parts) in enumerate(zip((count_ref, count_ref, ri_ref), groups)):
            per = ref.shape[0] // parts
            most = jnp.int32(0)
            for g in range(parts):
                total = jnp.int32(0)
                for i in range(per):
                    total = total + ref[g * per + i]
                most = jnp.maximum(most, total)
            for n, sizes in enumerate(levels[:-1]):
                level = jnp.where(most > sizes[axis], jnp.maximum(level, n + 1), level)
        o_ref[0] = level

    return pl.pallas_call(
        body,
        out_shape=jax.ShapeDtypeStruct((1,), jnp.int32),
        in_specs=[SMEM_SPEC, SMEM_SPEC],
        out_specs=SMEM_SPEC,
        name="first_fit",
    )(basis_count, ri_count)


def pack_integrals(tc, block_mask, basis_count, ri_count, ncols, packed, unroll, arrived=None):
    rows, cols = tc.shape
    atoms = rows // BW
    wide = cols // ncols
    blocks = wide // RW
    chips = ncols // CORES
    first = arrived is None

    def body(count_ref, ri_ref, mask_ref, x_ref, *refs):
        outs = refs[:1] if first else refs[1 : 1 + chips]
        held, hot = refs[-2:] if first else refs[-3:-1]
        made = outs[0] if first else refs[-1]
        row, col = lax.axis_index("row"), lax.axis_index("col")
        base = (row * ncols + col) * atoms

        @loop(chips, unroll)
        def _(t):
            dest = col ^ (CORES * t + (1 if first else 0))

            @loop(blocks, unroll)
            def _(b):
                lanes = pl.ds(pl.multiple_of(dest * wide + b * RW, RW), RW)
                slot = iota((BW, RW), 0)
                for a in range(atoms):
                    limit = jnp.where(mask_ref[a, dest * blocks + b] > 0, count_ref[base + a], 0)
                    x = x_ref[pl.ds(a * BW, BW), lanes].astype(F32)
                    held[pl.ds(a * BW, BW), span(b, RW)] = jnp.where(slot < limit, x, 0.0).astype(BF16)

            pack_cols(ri_ref, dest * blocks, blocks, RW, packed, hot, unroll)
            made[t] = jnp.dot(held[...], hot[...], preferred_element_type=F32).astype(BF16)

        if not first:
            core = lax.rem(col, CORES)
            for t in range(chips):
                outs[t][pl.ds(pl.multiple_of(core * rows, rows), rows), :] = made[t]
                outs[t][pl.ds(pl.multiple_of((1 - core) * rows, rows), rows), :] = refs[0][t]

    shape = (chips, rows, packed)
    merged = jax.ShapeDtypeStruct((CORES * rows, packed), BF16)
    out_shape = [jax.ShapeDtypeStruct(shape, BF16)] if first else [merged] * chips
    out_specs = [VMEM_SPEC] * len(out_shape)
    return pl.pallas_call(
        body,
        out_shape=out_shape,
        in_specs=[SMEM_SPEC, SMEM_SPEC, SMEM_SPEC] + [VMEM_SPEC] * (1 if first else 2),
        out_specs=out_specs,
        scratch_shapes=[pltpu.VMEM((rows, wide), BF16), pltpu.VMEM((wide, packed), BF16)]
        + ([] if first else [pltpu.VMEM(shape, BF16)]),
        compiler_params=params(),
        cost_estimate=cost(rows * cols * packed, rows * cols + 3 * chips * rows * packed),
        name="pack_other_core" if first else "pack_own_core",
    )(basis_count, ri_count, block_mask, tc, *([] if first else [arrived]))


def pack_density(dens, mask, basis_count, lam_size, sum_size, unroll):
    rows, cols = dens.shape
    lam_atoms, sum_atoms = mask.shape
    steps = 1 if unroll else 4
    tile = rows // steps
    out_tile = lam_size // steps

    def body(count_ref, mask_ref, x_ref, o_ref, upper_ref, lower_ref, hot, keep, mid):
        row, col = lax.axis_index("row"), lax.axis_index("col")
        first = iota((sum_atoms, cols), 0) * BW
        lane = iota((sum_atoms, cols), 1)
        of_atom = ones_where((lane >= first) & (lane < first + BW))
        keep[...] = jnp.dot(ones_where(mask_ref[...] > 0), of_atom, preferred_element_type=F32).astype(BF16)
        pack_cols(count_ref, col * sum_atoms, sum_atoms, BW, sum_size, hot, unroll)

        @loop(steps, unroll)
        def _(i):
            at = span(i, tile)
            shape = (tile, lam_atoms)
            first = iota(shape, 1) * BW - i * tile
            atom = ones_where((iota(shape, 0) >= first) & (iota(shape, 0) < first + BW))
            kept = jnp.dot(atom, keep[...], preferred_element_type=F32)
            x = jnp.where(kept > 0.5, x_ref[at, :].astype(F32), 0.0).astype(BF16)
            mid[at, :] = jnp.dot(x, hot[...], preferred_element_type=F32).astype(BF16)

        place = place_row(count_ref, row * lam_atoms, lam_atoms, BW)

        @loop(steps, unroll)
        def _(i):
            at = span(i, out_tile)
            left = ones_where(iota((out_tile, rows), 0) + i * out_tile == place)
            o_ref[at, :] = jnp.dot(left, mid[...], preferred_element_type=F32).astype(BF16)

        upper_ref[...] = o_ref[pl.ds(0, TILE), :]
        lower_ref[...] = o_ref[pl.ds(TILE, lam_size - TILE), :]

    return pl.pallas_call(
        body,
        out_shape=[jax.ShapeDtypeStruct((n, sum_size), BF16) for n in (lam_size, TILE, lam_size - TILE)],
        in_specs=[SMEM_SPEC, VMEM_SPEC, VMEM_SPEC],
        out_specs=[VMEM_SPEC] * 3,
        scratch_shapes=[
            pltpu.VMEM((cols, sum_size), BF16),
            pltpu.VMEM((lam_atoms, cols), BF16),
            pltpu.VMEM((rows, sum_size), BF16),
        ],
        compiler_params=params(),
        cost_estimate=cost(2 * rows * sum_size * (cols + lam_size), 2 * rows * cols),
        name="pack_density",
    )(basis_count, mask, dens)


def pack_part(pieces, basis_count, first, ncols, size):
    rows, cols = pieces[0].shape
    per = len(pieces)
    depth = per * rows
    atoms = depth // BW

    def body(count_ref, *refs):
        blocks, o_ref, full = refs[:per], refs[per], refs[per + 1]
        row, chip = lax.axis_index("row"), lax.axis_index("col") // CORES
        for i in range(per):
            at = lax.rem(chip ^ (first + i), per) * rows
            full[pl.ds(pl.multiple_of(at, rows), rows), :] = blocks[i][...]
        part = (row * (ncols // CORES) + (chip ^ first)) * rows // depth
        hot = pack_rows(count_ref, part * atoms, atoms, BW, size)
        o_ref[...] = jnp.dot(hot, full[...], preferred_element_type=F32).astype(BF16)

    return pl.pallas_call(
        body,
        out_shape=jax.ShapeDtypeStruct((size, cols), BF16),
        in_specs=[SMEM_SPEC] + [VMEM_SPEC] * per,
        out_specs=VMEM_SPEC,
        scratch_shapes=[pltpu.VMEM((depth, cols), BF16)],
        compiler_params=params(),
        cost_estimate=cost((2 + 40 * first) * size * depth * cols, 2 * cols * (depth + size)),
        name="pack_part",
    )(basis_count, *pieces)


def exchange(x, axis, bit):
    peers = lax.axis_size(axis)
    return lax.ppermute(x, axis, [(i, i ^ bit) for i in range(peers)])


def after(x, *others):
    return lax.optimization_barrier((x, *others))[0]


def double(own, axis, bits):
    have = {0: own}
    for bit in bits:
        for far in sorted(have):
            have[far | bit] = exchange(have[far], axis, bit)
    return have


def add_parts(total, unroll, d_refs, sums, before=None):
    lam, cols = total.shape

    @loop(lam // TILE, unroll)
    def _(j):
        out = span(j, TILE)
        x = None if before is None else before[out, :]
        for chunks, part in zip(d_refs, sums):
            if len(chunks) == 1:
                d = chunks[0][out, :]
            elif isinstance(j, int):
                d = chunks[0][...] if j == 0 else chunks[1][span(j - 1, TILE), :]
            else:
                d = chunks[1][span(jnp.maximum(j - 1, 0), TILE), :].astype(F32)
                d = jnp.where(j == 0, chunks[0][...].astype(F32), d).astype(BF16)
            y = jnp.dot(d, part(), preferred_element_type=F32)
            x = y if x is None else x + y
        total[out, :] = x


def split_refs(dens, refs):
    lists, at = [], 0
    for chunks in dens.values():
        lists.append(refs[at : at + len(chunks)])
        at += len(chunks)
    return lists, refs[at:]


def flat(dens):
    return [chunk for chunks in dens.values() for chunk in chunks]


def ways_back(basis_count, ri_count, nrows, ncols, rows, wide, lam, cols, unroll):
    lam_atoms, blocks = rows // BW, wide // RW

    def body(count_ref, ri_ref, lam_hot, col_hot):
        row, col = lax.axis_index("row"), lax.axis_index("col")
        pack_cols(count_ref, row * lam_atoms, lam_atoms, BW, lam, lam_hot, unroll)
        place = place_row(ri_ref, col * blocks, blocks, RW)

        @loop(cols // RW, unroll)
        def _(i):
            col_hot[span(i, RW), :] = ones_where(iota((RW, wide), 0) + i * RW == place)

    return pl.pallas_call(
        body,
        out_shape=[jax.ShapeDtypeStruct((rows, lam), BF16), jax.ShapeDtypeStruct((cols, wide), BF16)],
        in_specs=[SMEM_SPEC, SMEM_SPEC],
        out_specs=[VMEM_SPEC] * 2,
        compiler_params=params(16 * 1024 * 1024),
        name="ways_back",
    )(basis_count, ri_count)


def contract_near(dens, integrals, ncols, unroll):
    lam, depth = dens[0][0].shape
    groups, nrows = len(integrals), len(integrals[0])
    sums = [integrals[g][far] for far in range(nrows) for g in range(groups)]
    cols = sums[0].shape[1]
    n, parts = len(dens), len(sums)

    def body(*refs):
        d_refs, refs = split_refs(dens, refs)
        s_refs, refs = refs[:parts], refs[parts:]
        total, s_rest, s_all, s_sem, r_sem = refs
        row, col = lax.axis_index("row"), lax.axis_index("col")
        for j, ref in enumerate(s_refs):
            part = (row ^ (j // groups)) * groups + (col // (ncols // groups) ^ (j % groups))
            pltpu.make_async_copy(ref, s_all.at[part], s_sem.at[part]).start()

        @pl.loop(0, parts)
        def _(i):
            pltpu.make_async_copy(s_all.at[i], s_all.at[i], s_sem.at[i]).wait()

        rest = [
            pltpu.make_async_copy(s_all.at[col ^ far], s_rest.at[far - n], r_sem.at[far - n])
            for far in range(n, parts)
        ]
        for copy in rest:
            copy.start()
        add_parts(total, unroll, d_refs, [lambda far=far: s_all[col ^ far] for far in range(n)])
        for copy in rest:
            copy.wait()

    need = 2 * (n * depth * lam + 2 * parts * depth * cols + 4 * lam * cols)
    return pl.pallas_call(
        body,
        out_shape=[
            jax.ShapeDtypeStruct((lam, cols), F32),
            jax.ShapeDtypeStruct((parts - n, depth, cols), BF16),
        ],
        in_specs=[VMEM_SPEC] * n + [ANY_SPEC] * parts,
        out_specs=[VMEM_SPEC] * 2,
        scratch_shapes=[
            pltpu.VMEM((parts, depth, cols), BF16),
            pltpu.SemaphoreType.DMA((parts,)),
            pltpu.SemaphoreType.DMA((parts - n,)),
        ],
        compiler_params=params(need + 4 * 1024 * 1024),
        cost_estimate=cost(2 * n * depth * lam * cols, 2 * n * depth * (lam + cols)),
        name="contract_near",
    )(*flat(dens), *sums)


def contract_far(dens, first, total, sums, unroll):
    (lam, cols), depth = total.shape, sums.shape[1]
    n = len(dens)

    def body(before, s_ref, *refs):
        d_refs, (o_ref,) = split_refs(dens, refs)
        add_parts(o_ref, unroll, d_refs, [lambda i=i: s_ref[first + i] for i in range(n)], before)

    need = 2 * (n * depth * lam + sums.size + 4 * lam * cols)
    return pl.pallas_call(
        body,
        out_shape=jax.ShapeDtypeStruct((lam, cols), F32),
        in_specs=[VMEM_SPEC] * (2 + len(flat(dens))),
        out_specs=VMEM_SPEC,
        compiler_params=params(need + 4 * 1024 * 1024),
        cost_estimate=cost(2 * n * depth * lam * cols, 2 * n * depth * (lam + cols)),
        name="contract_far",
    )(total, sums, *flat(dens))


def contract_last(dens, first, total, sums, lam_hot, col_hot, unroll):
    (rows, lam), (cols, wide) = lam_hot.shape, col_hot.shape
    depth = sums.shape[1]
    n = len(dens)
    half = lam // 2

    def body(before, s_ref, lam_hot, col_hot, *refs):
        d_refs, (o_ref, total, packed) = split_refs(dens, refs)
        add_parts(total, unroll, d_refs, [lambda i=i: s_ref[first + i] for i in range(n)], before)

        @loop(2, unroll)
        def _(j):
            x = total[span(j, half), :].astype(BF16)
            packed[span(j, half), :] = jnp.dot(x, col_hot[...], preferred_element_type=F32).astype(BF16)

        @loop(4, unroll)
        def _(j):
            out = span(j, rows // 4)
            o_ref[out, :] = jnp.dot(lam_hot[out, :], packed[...], preferred_element_type=F32).astype(BF16)

    need = 2 * (n * depth * lam + sums.size + 4 * lam * cols + rows * lam + cols * wide + (lam + rows) * wide)
    return pl.pallas_call(
        body,
        out_shape=jax.ShapeDtypeStruct((rows, wide), BF16),
        in_specs=[VMEM_SPEC] * (4 + len(flat(dens))),
        out_specs=VMEM_SPEC,
        scratch_shapes=[pltpu.VMEM((lam, cols), F32), pltpu.VMEM((lam, wide), BF16)],
        compiler_params=params(need + 4 * 1024 * 1024),
        cost_estimate=cost(2 * n * depth * lam * cols, 2 * n * depth * (lam + cols)),
        name="contract_last",
    )(total, sums, lam_hot, col_hot, *flat(dens))


def program(lam_size, sum_size, col_size, common):
    unroll = common

    def run(three_center, density, block_mask, density_mask, basis_count, ri_count):
        ncols = lax.axis_size("col")
        nrows = lax.axis_size("row")
        chips = ncols // CORES
        rows, depth = density.shape
        wide = three_center.shape[1] // ncols
        row_bits = [1 << b for b in range(nrows.bit_length() - 1)]
        chip_bits = [CORES << b for b in range(chips.bit_length() - 1)][::-1]
        far_bit, near_bits = chip_bits[0], chip_bits[1:]

        counts = (block_mask, basis_count, ri_count, ncols, col_size, unroll)
        other = exchange(pack_integrals(three_center, *counts)[0], "col", 1)
        own, upper, lower = pack_density(density, density_mask, basis_count, lam_size, sum_size, unroll)
        lines = [{0: upper, far_bit: exchange(upper, "col", far_bit)}, {0: lower}]
        near = {0: own, 1: exchange(own, "col", 1)}
        pieces = pack_integrals(three_center, *counts, after(other, own))
        early = lines[0][far_bit]
        got = [pieces[0]] + [exchange(pieces[t], "col", CORES * t) for t in range(1, chips)]
        per = depth // pieces[0].shape[0]
        lam_hot, col_hot = ways_back(
            basis_count, ri_count, nrows, ncols, rows, wide, lam_size, col_size, unroll
        )
        parts, groups, orders = [], [], []
        for g in range(chips // per):
            arrived = got[g * per : (g + 1) * per]
            if g == 0:
                arrived = [after(arrived[0], near[1])] + arrived[1:]
            elif g == 1:
                arrived = [after(arrived[0], lam_hot)] + arrived[1:]
            part = pack_part(arrived, basis_count, g * per, ncols, sum_size)
            if g == 0:
                near.update(double(after(own, part), "col", near_bits))
                steps = [near[far] for far in near if far > 1]
            else:
                part = after(part, *[groups[0][bit] for bit in row_bits])
            parts.append(part)
            orders.append(row_bits if g % 2 == 0 else row_bits[::-1])
            groups.append({0: part})
            for bit in orders[g]:
                groups[g][bit] = exchange(part, "row", bit)
        step = groups[-1][orders[-1][0]]
        across = exchange(after(early, parts[-1]), "col", 1)
        forward = double(after(early, across, *steps), "col", near_bits)
        lines[0].update({far_bit | far: block for far, block in forward.items() if far > 0})
        lines[1][far_bit] = exchange(after(lower, parts[-1]), "col", far_bit)
        for far in [far for far in near if far > 1]:
            near[far | 1] = exchange(after(near[far], across), "col", 1)
        for g, have in enumerate(groups):
            done = [0, orders[g][0]]
            for bit in orders[g][1:]:
                for far in done[1:]:
                    block = have[far] if g == len(groups) - 1 else after(have[far], *[groups[-1][bit] for bit in row_bits])
                    have[far | bit] = exchange(block, "row", bit)
                done += [far | bit for far in done]
        first = {far: [near[far]] for far in sorted(near)}
        total, sums = contract_near(first, groups, ncols, unroll)
        block = after(lines[1][far_bit], lines[0][ncols - CORES])
        for away, block in double(block, "col", near_bits).items():
            lines[1][far_bit | away] = block
        middle = {}
        for far in range(far_bit, ncols - CORES, CORES):
            middle[far] = [line[far] for line in lines]
            middle[far | 1] = [across if line[far] is early else exchange(line[far], "col", 1) for line in lines]
        total = contract_far(middle, 0, total, sums, unroll)
        ends = [line[ncols - CORES] for line in lines]
        last = {ncols - CORES: ends}
        last[ncols - 1] = [exchange(ends[0], "col", 1), exchange(after(ends[1], total), "col", 1)]
        return contract_last(last, len(middle), total, sums, lam_hot, col_hot, unroll)

    return run


def choose(here, yes, no):
    return lambda *args: lax.cond(here, yes, no, *args)


def shards(three_center, density, block_mask, density_mask, basis_count, ri_count):
    ncols = lax.axis_size("col")
    nrows = lax.axis_size("row")
    rows, depth = density.shape
    wide = three_center.shape[1] // ncols
    levels = (
        (rows * 3 // 4, depth * 3 // 4, wide * 5 // 6),
        (rows * 3 // 4, depth, wide * 5 // 6),
        (rows * 3 // 4, depth, wide),
        (rows, depth, wide),
    )
    level = first_fit(basis_count, ri_count, (nrows, ncols, ncols), levels)
    args = (three_center, density, block_mask, density_mask, basis_count, ri_count)
    run = program(*levels[-1], False)
    for n in reversed(range(len(levels) - 1)):
        run = choose(level[0] == n, program(*levels[n], n == 0), run)
    return run(*args)


def solution(mesh):
    in_specs = (
        P(("row", "col"), None),
        P("row", "col"),
        P(("row", "col"), None),
        P("row", "col"),
        P(),
        P(),
    )
    return jax.shard_map(
        shards, mesh=mesh, in_specs=in_specs, out_specs=P("row", "col"), check_vma=False
    )
```

```python
import jax
import jax.numpy as jnp
from jax import lax
from jax.experimental import pallas as pl
from jax.experimental.pallas import tpu as pltpu
from jax.sharding import PartitionSpec as P

BW = 32
RW = 128
CORES = 2
VMEM = 48 * 1024 * 1024
TILE = 256
BF16 = jnp.bfloat16
F32 = jnp.float32
SMEM_SPEC = pl.BlockSpec(memory_space=pltpu.SMEM)
VMEM_SPEC = pl.BlockSpec(memory_space=pltpu.VMEM)
ANY_SPEC = pl.BlockSpec(memory_space=pl.ANY)


def params(limit=VMEM):
    return pltpu.CompilerParams(vmem_limit_bytes=limit)


def cost(flops, bytes_accessed):
    return pl.CostEstimate(flops=flops, bytes_accessed=bytes_accessed, transcendentals=0)


def ones_where(cond):
    return jnp.where(cond, 1.0, 0.0).astype(BF16)


def iota(shape, axis):
    return lax.broadcasted_iota(jnp.int32, shape, axis)


def loop(n, unroll):
    def run(f):
        if unroll:
            for i in range(n):
                f(i)
        else:
            pl.loop(0, n)(f)

    return run


def span(i, size):
    return pl.ds(i * size if isinstance(i, int) else pl.multiple_of(i * size, size), size)


def place_row(count_ref, base, atoms, width, unroll):
    lane = iota((1, atoms * width), 1)

    def atom(a, carry):
        place, offset = carry
        count = count_ref[base + a]
        inside = (lane >= a * width) & (lane < a * width + count)
        return jnp.where(inside, lane - a * width + offset, place), offset + count

    carry = (jnp.full(lane.shape, -1, jnp.int32), jnp.int32(0))
    if not unroll:
        return lax.fori_loop(0, atoms, atom, carry)[0]
    for a in range(atoms):
        carry = atom(a, carry)
    return carry[0]


def pack_rows(count_ref, base, atoms, width, size, unroll):
    place = place_row(count_ref, base, atoms, width, unroll)
    return ones_where(iota((size, atoms * width), 0) == place)


def pack_cols(count_ref, base, atoms, width, size, out, unroll):
    def atom(a, offset):
        count = count_ref[base + a]
        lanes = min(size, (a + 1) * width) if unroll and width % 128 == 0 else size
        slot = iota((width, lanes), 0)
        gap = iota((width, lanes), 1) - slot
        out[span(a, width), pl.ds(0, lanes)] = ones_where((gap == offset) & (slot < count))
        return offset + count

    if unroll:
        offset = jnp.int32(0)
        for a in range(atoms):
            offset = atom(a, offset)
    else:
        lax.fori_loop(0, atoms, atom, jnp.int32(0))


def first_fit(basis_count, ri_count, groups, levels):
    def body(count_ref, ri_ref, o_ref):
        level = jnp.int32(0)
        for axis, (ref, parts) in enumerate(zip((count_ref, count_ref, ri_ref), groups)):
            per = ref.shape[0] // parts
            most = jnp.int32(0)
            for g in range(parts):
                total = jnp.int32(0)
                for i in range(per):
                    total = total + ref[g * per + i]
                most = jnp.maximum(most, total)
            for n, sizes in enumerate(levels[:-1]):
                level = jnp.where(most > sizes[axis], jnp.maximum(level, n + 1), level)
        o_ref[0] = level

    return pl.pallas_call(
        body,
        out_shape=jax.ShapeDtypeStruct((1,), jnp.int32),
        in_specs=[SMEM_SPEC, SMEM_SPEC],
        out_specs=SMEM_SPEC,
        name="first_fit",
    )(basis_count, ri_count)


def pack_integrals(tc, block_mask, basis_count, ri_count, ncols, packed, unroll, arrived=None):
    rows, cols = tc.shape
    atoms = rows // BW
    wide = cols // ncols
    blocks = wide // RW
    chips = ncols // CORES
    first = arrived is None

    def body(count_ref, ri_ref, mask_ref, x_ref, *refs):
        outs = refs[:1] if first else refs[1 : 1 + chips]
        held, hot = refs[-2:] if first else refs[-3:-1]
        made = outs[0] if first else refs[-1]
        row, col = lax.axis_index("row"), lax.axis_index("col")
        base = (row * ncols + col) * atoms
        hot[...] = jnp.zeros_like(hot)

        @loop(chips, unroll)
        def _(t):
            dest = col ^ (CORES * t + (1 if first else 0))

            @loop(blocks, unroll)
            def _(b):
                lanes = pl.ds(pl.multiple_of(dest * wide + b * RW, RW), RW)
                slot = iota((BW, RW), 0)
                for a in range(atoms):
                    limit = jnp.where(mask_ref[a, dest * blocks + b] > 0, count_ref[base + a], 0)
                    x = x_ref[pl.ds(a * BW, BW), lanes].astype(F32)
                    held[pl.ds(a * BW, BW), span(b, RW)] = jnp.where(slot < limit, x, 0.0).astype(BF16)

            pack_cols(ri_ref, dest * blocks, blocks, RW, packed, hot, unroll)
            made[t] = jnp.dot(held[...], hot[...], preferred_element_type=F32).astype(BF16)

        if not first:
            core = lax.rem(col, CORES)
            for t in range(chips):
                outs[t][pl.ds(pl.multiple_of(core * rows, rows), rows), :] = made[t]
                outs[t][pl.ds(pl.multiple_of((1 - core) * rows, rows), rows), :] = refs[0][t]

    shape = (chips, rows, packed)
    merged = jax.ShapeDtypeStruct((CORES * rows, packed), BF16)
    out_shape = [jax.ShapeDtypeStruct(shape, BF16)] if first else [merged] * chips
    out_specs = [VMEM_SPEC] * len(out_shape)
    return pl.pallas_call(
        body,
        out_shape=out_shape,
        in_specs=[SMEM_SPEC, SMEM_SPEC, SMEM_SPEC] + [VMEM_SPEC] * (1 if first else 2),
        out_specs=out_specs,
        scratch_shapes=[pltpu.VMEM((rows, wide), BF16), pltpu.VMEM((wide, packed), BF16)]
        + ([] if first else [pltpu.VMEM(shape, BF16)]),
        compiler_params=params(),
        cost_estimate=cost(rows * cols * packed, rows * cols + 3 * chips * rows * packed),
        name="pack_other_core" if first else "pack_own_core",
    )(basis_count, ri_count, block_mask, tc, *([] if first else [arrived]))


def pack_density(dens, mask, basis_count, lam_size, sum_size, unroll):
    rows, cols = dens.shape
    lam_atoms, sum_atoms = mask.shape
    steps = 1 if unroll else 4
    tile = rows // steps
    out_tile = lam_size // steps

    def body(count_ref, mask_ref, x_ref, o_ref, upper_ref, lower_ref, hot, keep, mid):
        row, col = lax.axis_index("row"), lax.axis_index("col")
        first = iota((sum_atoms, cols), 0) * BW
        lane = iota((sum_atoms, cols), 1)
        of_atom = ones_where((lane >= first) & (lane < first + BW))
        keep[...] = jnp.dot(ones_where(mask_ref[...] > 0), of_atom, preferred_element_type=F32).astype(BF16)
        pack_cols(count_ref, col * sum_atoms, sum_atoms, BW, sum_size, hot, unroll)

        @loop(steps, unroll)
        def _(i):
            at = span(i, tile)
            shape = (tile, lam_atoms)
            first = iota(shape, 1) * BW - i * tile
            atom = ones_where((iota(shape, 0) >= first) & (iota(shape, 0) < first + BW))
            kept = jnp.dot(atom, keep[...], preferred_element_type=F32)
            x = jnp.where(kept > 0.5, x_ref[at, :].astype(F32), 0.0).astype(BF16)
            mid[at, :] = jnp.dot(x, hot[...], preferred_element_type=F32).astype(BF16)

        place = place_row(count_ref, row * lam_atoms, lam_atoms, BW, unroll)

        @loop(steps, unroll)
        def _(i):
            at = span(i, out_tile)
            left = ones_where(iota((out_tile, rows), 0) + i * out_tile == place)
            o_ref[at, :] = jnp.dot(left, mid[...], preferred_element_type=F32).astype(BF16)

        upper_ref[...] = o_ref[pl.ds(0, TILE), :]
        lower_ref[...] = o_ref[pl.ds(TILE, lam_size - TILE), :]

    return pl.pallas_call(
        body,
        out_shape=[jax.ShapeDtypeStruct((n, sum_size), BF16) for n in (lam_size, TILE, lam_size - TILE)],
        in_specs=[SMEM_SPEC, VMEM_SPEC, VMEM_SPEC],
        out_specs=[VMEM_SPEC] * 3,
        scratch_shapes=[
            pltpu.VMEM((cols, sum_size), BF16),
            pltpu.VMEM((lam_atoms, cols), BF16),
            pltpu.VMEM((rows, sum_size), BF16),
        ],
        compiler_params=params(),
        cost_estimate=cost(2 * rows * sum_size * (cols + lam_size), 2 * rows * cols),
        name="pack_density",
    )(basis_count, mask, dens)


def pack_part(pieces, basis_count, first, ncols, size, unroll):
    rows, cols = pieces[0].shape
    per = len(pieces)
    depth = per * rows
    atoms = depth // BW

    def body(count_ref, *refs):
        blocks, o_ref, full = refs[:per], refs[per], refs[per + 1]
        row, chip = lax.axis_index("row"), lax.axis_index("col") // CORES
        for i in range(per):
            at = lax.rem(chip ^ (first + i), per) * rows
            full[pl.ds(pl.multiple_of(at, rows), rows), :] = blocks[i][...]
        part = (row * (ncols // CORES) + (chip ^ first)) * rows // depth
        hot = pack_rows(count_ref, part * atoms, atoms, BW, size, unroll)
        o_ref[...] = jnp.dot(hot, full[...], preferred_element_type=F32).astype(BF16)

    return pl.pallas_call(
        body,
        out_shape=jax.ShapeDtypeStruct((size, cols), BF16),
        in_specs=[SMEM_SPEC] + [VMEM_SPEC] * per,
        out_specs=VMEM_SPEC,
        scratch_shapes=[pltpu.VMEM((depth, cols), BF16)],
        compiler_params=params(),
        cost_estimate=cost((2 + 40 * first) * size * depth * cols, 2 * cols * (depth + size)),
        name="pack_part",
    )(basis_count, *pieces)


def exchange(x, axis, bit):
    peers = lax.axis_size(axis)
    return lax.ppermute(x, axis, [(i, i ^ bit) for i in range(peers)])


def after(x, *others):
    return lax.optimization_barrier((x, *others))[0]


def double(own, axis, bits):
    have = {0: own}
    for bit in bits:
        for far in sorted(have):
            have[far | bit] = exchange(have[far], axis, bit)
    return have


def add_parts(total, unroll, d_refs, sums, before=None):
    lam, cols = total.shape

    @loop(lam // TILE, unroll)
    def _(j):
        out = span(j, TILE)
        x = None if before is None else before[out, :]
        for chunks, part in zip(d_refs, sums):
            if len(chunks) == 1:
                d = chunks[0][out, :]
            elif isinstance(j, int):
                d = chunks[0][...] if j == 0 else chunks[1][span(j - 1, TILE), :]
            else:
                d = chunks[1][span(jnp.maximum(j - 1, 0), TILE), :].astype(F32)
                d = jnp.where(j == 0, chunks[0][...].astype(F32), d).astype(BF16)
            y = jnp.dot(d, part(), preferred_element_type=F32)
            x = y if x is None else x + y
        total[out, :] = x


def split_refs(dens, refs):
    lists, at = [], 0
    for chunks in dens.values():
        lists.append(refs[at : at + len(chunks)])
        at += len(chunks)
    return lists, refs[at:]


def flat(dens):
    return [chunk for chunks in dens.values() for chunk in chunks]


def ways_back(basis_count, ri_count, nrows, ncols, rows, wide, lam, cols, unroll):
    lam_atoms, blocks = rows // BW, wide // RW

    def body(count_ref, ri_ref, lam_hot, col_hot):
        row, col = lax.axis_index("row"), lax.axis_index("col")
        pack_cols(count_ref, row * lam_atoms, lam_atoms, BW, lam, lam_hot, unroll)
        place = place_row(ri_ref, col * blocks, blocks, RW, unroll)

        @loop(cols // RW, unroll)
        def _(i):
            col_hot[span(i, RW), :] = ones_where(iota((RW, wide), 0) + i * RW == place)

    return pl.pallas_call(
        body,
        out_shape=[jax.ShapeDtypeStruct((rows, lam), BF16), jax.ShapeDtypeStruct((cols, wide), BF16)],
        in_specs=[SMEM_SPEC, SMEM_SPEC],
        out_specs=[VMEM_SPEC] * 2,
        compiler_params=params(16 * 1024 * 1024),
        name="ways_back",
    )(basis_count, ri_count)


def contract_near(dens, integrals, ncols, unroll):
    lam, depth = dens[0][0].shape
    groups, nrows = len(integrals), len(integrals[0])
    sums = [integrals[g][far] for far in range(nrows) for g in range(groups)]
    cols = sums[0].shape[1]
    n, parts = len(dens), len(sums)

    def body(*refs):
        d_refs, refs = split_refs(dens, refs)
        s_refs, refs = refs[:parts], refs[parts:]
        total, s_rest, s_all, s_sem, r_sem = refs
        row, col = lax.axis_index("row"), lax.axis_index("col")
        for j, ref in enumerate(s_refs):
            part = (row ^ (j // groups)) * groups + (col // (ncols // groups) ^ (j % groups))
            pltpu.make_async_copy(ref, s_all.at[part], s_sem.at[part]).start()

        @pl.loop(0, parts)
        def _(i):
            pltpu.make_async_copy(s_all.at[i], s_all.at[i], s_sem.at[i]).wait()

        rest = [
            pltpu.make_async_copy(s_all.at[col ^ far], s_rest.at[far - n], r_sem.at[far - n])
            for far in range(n, parts)
        ]
        for copy in rest:
            copy.start()
        add_parts(total, unroll, d_refs, [lambda far=far: s_all[col ^ far] for far in range(n)])
        for copy in rest:
            copy.wait()

    need = 2 * (n * depth * lam + 2 * parts * depth * cols + 4 * lam * cols)
    return pl.pallas_call(
        body,
        out_shape=[
            jax.ShapeDtypeStruct((lam, cols), F32),
            jax.ShapeDtypeStruct((parts - n, depth, cols), BF16),
        ],
        in_specs=[VMEM_SPEC] * n + [ANY_SPEC] * parts,
        out_specs=[VMEM_SPEC] * 2,
        scratch_shapes=[
            pltpu.VMEM((parts, depth, cols), BF16),
            pltpu.SemaphoreType.DMA((parts,)),
            pltpu.SemaphoreType.DMA((parts - n,)),
        ],
        compiler_params=params(need + 4 * 1024 * 1024),
        cost_estimate=cost(2 * n * depth * lam * cols, 2 * n * depth * (lam + cols)),
        name="contract_near",
    )(*flat(dens), *sums)


def contract_far(dens, first, total, sums, unroll):
    (lam, cols), depth = total.shape, sums.shape[1]
    n = len(dens)

    def body(before, s_ref, *refs):
        d_refs, (o_ref,) = split_refs(dens, refs)
        add_parts(o_ref, unroll, d_refs, [lambda i=i: s_ref[first + i] for i in range(n)], before)

    need = 2 * (n * depth * lam + sums.size + 4 * lam * cols)
    return pl.pallas_call(
        body,
        out_shape=jax.ShapeDtypeStruct((lam, cols), F32),
        in_specs=[VMEM_SPEC] * (2 + len(flat(dens))),
        out_specs=VMEM_SPEC,
        compiler_params=params(need + 4 * 1024 * 1024),
        cost_estimate=cost(2 * n * depth * lam * cols, 2 * n * depth * (lam + cols)),
        name="contract_far",
    )(total, sums, *flat(dens))


def contract_last(dens, first, total, sums, lam_hot, col_hot, unroll):
    (rows, lam), (cols, wide) = lam_hot.shape, col_hot.shape
    depth = sums.shape[1]
    n = len(dens)
    half = lam // 2

    def body(before, s_ref, lam_hot, col_hot, *refs):
        d_refs, (o_ref, total, packed) = split_refs(dens, refs)
        add_parts(total, unroll, d_refs, [lambda i=i: s_ref[first + i] for i in range(n)], before)

        @loop(2, unroll)
        def _(j):
            x = total[span(j, half), :].astype(BF16)
            packed[span(j, half), :] = jnp.dot(x, col_hot[...], preferred_element_type=F32).astype(BF16)

        @loop(4, unroll)
        def _(j):
            out = span(j, rows // 4)
            o_ref[out, :] = jnp.dot(lam_hot[out, :], packed[...], preferred_element_type=F32).astype(BF16)

    need = 2 * (n * depth * lam + sums.size + 4 * lam * cols + rows * lam + cols * wide + (lam + rows) * wide)
    return pl.pallas_call(
        body,
        out_shape=jax.ShapeDtypeStruct((rows, wide), BF16),
        in_specs=[VMEM_SPEC] * (4 + len(flat(dens))),
        out_specs=VMEM_SPEC,
        scratch_shapes=[pltpu.VMEM((lam, cols), F32), pltpu.VMEM((lam, wide), BF16)],
        compiler_params=params(need + 4 * 1024 * 1024),
        cost_estimate=cost(2 * n * depth * lam * cols, 2 * n * depth * (lam + cols)),
        name="contract_last",
    )(total, sums, lam_hot, col_hot, *flat(dens))


def program(lam_size, sum_size, col_size, common):
    unroll = common

    def run(three_center, density, block_mask, density_mask, basis_count, ri_count):
        ncols = lax.axis_size("col")
        nrows = lax.axis_size("row")
        chips = ncols // CORES
        rows, depth = density.shape
        wide = three_center.shape[1] // ncols
        row_bits = [1 << b for b in range(nrows.bit_length() - 1)]
        chip_bits = [CORES << b for b in range(chips.bit_length() - 1)][::-1]
        far_bit, near_bits = chip_bits[0], chip_bits[1:]

        counts = (block_mask, basis_count, ri_count, ncols, col_size, unroll)
        other = exchange(pack_integrals(three_center, *counts)[0], "col", 1)
        own, upper, lower = pack_density(density, density_mask, basis_count, lam_size, sum_size, unroll)
        lines = [{0: upper, far_bit: exchange(upper, "col", far_bit)}, {0: lower}]
        near = {0: own, 1: exchange(own, "col", 1)}
        pieces = pack_integrals(three_center, *counts, after(other, own))
        early = lines[0][far_bit]
        got = [pieces[0]] + [exchange(pieces[t], "col", CORES * t) for t in range(1, chips)]
        per = depth // pieces[0].shape[0]
        lam_hot, col_hot = ways_back(
            basis_count, ri_count, nrows, ncols, rows, wide, lam_size, col_size, unroll
        )
        parts, groups, orders = [], [], []
        for g in range(chips // per):
            arrived = got[g * per : (g + 1) * per]
            if g == 0:
                arrived = [after(arrived[0], near[1])] + arrived[1:]
            elif g == 1:
                arrived = [after(arrived[0], lam_hot)] + arrived[1:]
            part = pack_part(arrived, basis_count, g * per, ncols, sum_size, unroll)
            if g == 0:
                near.update(double(after(own, part), "col", near_bits))
                steps = [near[far] for far in near if far > 1]
            else:
                part = after(part, *[groups[0][bit] for bit in row_bits])
            parts.append(part)
            orders.append(row_bits if g % 2 == 0 else row_bits[::-1])
            groups.append({0: part})
            for bit in orders[g]:
                groups[g][bit] = exchange(part, "row", bit)
        step = groups[-1][orders[-1][0]]
        across = exchange(after(early, parts[-1]), "col", 1)
        forward = double(after(early, across, *steps), "col", near_bits)
        lines[0].update({far_bit | far: block for far, block in forward.items() if far > 0})
        lines[1][far_bit] = exchange(after(lower, parts[-1]), "col", far_bit)
        for far in [far for far in near if far > 1]:
            near[far | 1] = exchange(after(near[far], across), "col", 1)
        for g, have in enumerate(groups):
            done = [0, orders[g][0]]
            for bit in orders[g][1:]:
                for far in done[1:]:
                    block = have[far] if g == len(groups) - 1 else after(have[far], *[groups[-1][bit] for bit in row_bits])
                    have[far | bit] = exchange(block, "row", bit)
                done += [far | bit for far in done]
        first = {far: [near[far]] for far in sorted(near)}
        total, sums = contract_near(first, groups, ncols, unroll)
        block = after(lines[1][far_bit], lines[0][ncols - CORES])
        for away, block in double(block, "col", near_bits).items():
            lines[1][far_bit | away] = block
        middle = {}
        for far in range(far_bit, ncols - CORES, CORES):
            middle[far] = [line[far] for line in lines]
            middle[far | 1] = [across if line[far] is early else exchange(line[far], "col", 1) for line in lines]
        total = contract_far(middle, 0, total, sums, unroll)
        ends = [line[ncols - CORES] for line in lines]
        last = {ncols - CORES: ends}
        last[ncols - 1] = [exchange(ends[0], "col", 1), exchange(after(ends[1], total), "col", 1)]
        return contract_last(last, len(middle), total, sums, lam_hot, col_hot, unroll)

    return run


def choose(here, yes, no):
    return lambda *args: lax.cond(here, yes, no, *args)


def shards(three_center, density, block_mask, density_mask, basis_count, ri_count):
    ncols = lax.axis_size("col")
    nrows = lax.axis_size("row")
    rows, depth = density.shape
    wide = three_center.shape[1] // ncols
    levels = (
        (rows * 3 // 4, depth * 3 // 4, wide * 5 // 6),
        (rows * 3 // 4, depth, wide * 5 // 6),
        (rows * 3 // 4, depth, wide),
        (rows, depth, wide),
    )
    level = first_fit(basis_count, ri_count, (nrows, ncols, ncols), levels)
    args = (three_center, density, block_mask, density_mask, basis_count, ri_count)
    run = program(*levels[-1], False)
    for n in reversed(range(len(levels) - 1)):
        run = choose(level[0] == n, program(*levels[n], n == 0), run)
    return run(*args)


def solution(mesh):
    in_specs = (
        P(("row", "col"), None),
        P("row", "col"),
        P(("row", "col"), None),
        P("row", "col"),
        P(),
        P(),
    )
    return jax.shard_map(
        shards, mesh=mesh, in_specs=in_specs, out_specs=P("row", "col"), check_vma=False
    )
```

```python
import jax
import jax.numpy as jnp
from jax import lax
from jax.experimental import pallas as pl
from jax.experimental.pallas import tpu as pltpu
from jax.sharding import PartitionSpec as P

BW = 32
RW = 128
CORES = 2
VMEM = 48 * 1024 * 1024
TILE = 256
BF16 = jnp.bfloat16
F32 = jnp.float32
SMEM_SPEC = pl.BlockSpec(memory_space=pltpu.SMEM)
VMEM_SPEC = pl.BlockSpec(memory_space=pltpu.VMEM)
ANY_SPEC = pl.BlockSpec(memory_space=pl.ANY)


def params(limit=VMEM):
    return pltpu.CompilerParams(vmem_limit_bytes=limit)


def cost(flops, bytes_accessed):
    return pl.CostEstimate(flops=flops, bytes_accessed=bytes_accessed, transcendentals=0)


def ones_where(cond):
    return jnp.where(cond, 1.0, 0.0).astype(BF16)


def iota(shape, axis):
    return lax.broadcasted_iota(jnp.int32, shape, axis)


def loop(n, unroll):
    def run(f):
        if unroll:
            for i in range(n):
                f(i)
        else:
            pl.loop(0, n)(f)

    return run


def span(i, size):
    return pl.ds(i * size if isinstance(i, int) else pl.multiple_of(i * size, size), size)


def place_row(count_ref, base, atoms, width, unroll):
    lane = iota((1, atoms * width), 1)

    def atom(a, carry):
        place, offset = carry
        count = count_ref[base + a]
        inside = (lane >= a * width) & (lane < a * width + count)
        return jnp.where(inside, lane - a * width + offset, place), offset + count

    carry = (jnp.full(lane.shape, -1, jnp.int32), jnp.int32(0))
    if not unroll:
        return lax.fori_loop(0, atoms, atom, carry)[0]
    for a in range(atoms):
        carry = atom(a, carry)
    return carry[0]


def pack_rows(count_ref, base, atoms, width, size, unroll):
    place = place_row(count_ref, base, atoms, width, unroll)
    return ones_where(iota((size, atoms * width), 0) == place)


def pack_cols(count_ref, base, atoms, width, size, out, unroll):
    def atom(a, offset):
        count = count_ref[base + a]
        lanes = min(size, (a + 1) * width) if unroll and width % 128 == 0 else size
        slot = iota((width, lanes), 0)
        gap = iota((width, lanes), 1) - slot
        out[span(a, width), pl.ds(0, lanes)] = ones_where((gap == offset) & (slot < count))
        return offset + count

    if unroll:
        offset = jnp.int32(0)
        for a in range(atoms):
            offset = atom(a, offset)
    else:
        lax.fori_loop(0, atoms, atom, jnp.int32(0))


class Sums:
    def __init__(self, ref, atoms):
        self.ref, self.atoms = ref, atoms

    def __getitem__(self, i):
        total = self.ref[i * self.atoms]
        for a in range(1, self.atoms):
            total = total + self.ref[i * self.atoms + a]
        return total


def first_fit(basis_count, ri_count, groups, levels):
    def body(count_ref, ri_ref, o_ref):
        level = jnp.int32(0)
        for axis, (ref, parts) in enumerate(zip((count_ref, count_ref, ri_ref, count_ref), groups)):
            per = ref.shape[0] // parts
            most = jnp.int32(0)
            for g in range(parts):
                total = jnp.int32(0)
                for i in range(per):
                    total = total + ref[g * per + i]
                most = jnp.maximum(most, total)
            for n, sizes in enumerate(levels[:-1]):
                level = jnp.where(most > sizes[axis], jnp.maximum(level, n + 1), level)
        o_ref[0] = level

    return pl.pallas_call(
        body,
        out_shape=jax.ShapeDtypeStruct((1,), jnp.int32),
        in_specs=[SMEM_SPEC, SMEM_SPEC],
        out_specs=SMEM_SPEC,
        name="first_fit",
    )(basis_count, ri_count)


def pack_integrals(tc, block_mask, basis_count, ri_count, ncols, packed, unroll, chip_rows, arrived=None):
    rows, cols = tc.shape
    atoms = rows // BW
    wide = cols // ncols
    blocks = wide // RW
    chips = ncols // CORES
    first = arrived is None

    def body(count_ref, ri_ref, mask_ref, x_ref, *refs):
        outs = refs[:1] if first else refs[1 : 1 + chips]
        held, hot = refs[-2:] if first else refs[-4:-2]
        made, both = (outs[0], None) if first else refs[-2:]
        row, col = lax.axis_index("row"), lax.axis_index("col")
        base = (row * ncols + col) * atoms
        hot[...] = jnp.zeros_like(hot)

        @loop(chips, unroll)
        def _(t):
            dest = col ^ (CORES * t + (1 if first else 0))

            @loop(blocks, unroll)
            def _(b):
                lanes = pl.ds(pl.multiple_of(dest * wide + b * RW, RW), RW)
                slot = iota((BW, RW), 0)
                for a in range(atoms):
                    limit = jnp.where(mask_ref[a, dest * blocks + b] > 0, count_ref[base + a], 0)
                    x = x_ref[pl.ds(a * BW, BW), lanes].astype(F32)
                    held[pl.ds(a * BW, BW), span(b, RW)] = jnp.where(slot < limit, x, 0.0).astype(BF16)

            pack_cols(ri_ref, dest * blocks, blocks, RW, packed, hot, unroll)
            made[t] = jnp.dot(held[...], hot[...], preferred_element_type=F32).astype(BF16)

        if not first:
            core = lax.rem(col, CORES)
            chip = (row * ncols + col - core) * atoms
            for t in range(chips):
                into = outs[t] if chip_rows == CORES * rows else both.at[t]
                into[pl.ds(pl.multiple_of(core * rows, rows), rows), :] = made[t]
                into[pl.ds(pl.multiple_of((1 - core) * rows, rows), rows), :] = refs[0][t]
            if chip_rows < CORES * rows:
                left = pack_rows(count_ref, chip, CORES * atoms, BW, chip_rows, unroll)
                for t in range(chips):
                    outs[t][...] = jnp.dot(left, both[t], preferred_element_type=F32).astype(BF16)

    shape = (chips, rows, packed)
    merged = jax.ShapeDtypeStruct((chip_rows, packed), BF16)
    out_shape = [jax.ShapeDtypeStruct(shape, BF16)] if first else [merged] * chips
    out_specs = [VMEM_SPEC] * len(out_shape)
    return pl.pallas_call(
        body,
        out_shape=out_shape,
        in_specs=[SMEM_SPEC, SMEM_SPEC, SMEM_SPEC] + [VMEM_SPEC] * (1 if first else 2),
        out_specs=out_specs,
        scratch_shapes=[pltpu.VMEM((rows, wide), BF16), pltpu.VMEM((wide, packed), BF16)]
        + ([] if first else [pltpu.VMEM(shape, BF16), pltpu.VMEM((chips, CORES * rows, packed), BF16)]),
        compiler_params=params(),
        cost_estimate=cost(rows * cols * packed, rows * cols + 3 * chips * rows * packed),
        name="pack_other_core" if first else "pack_own_core",
    )(basis_count, ri_count, block_mask, tc, *([] if first else [arrived]))


def pack_density(dens, mask, basis_count, lam_size, sum_size, unroll):
    rows, cols = dens.shape
    lam_atoms, sum_atoms = mask.shape
    steps = 1 if unroll else 4
    tile = rows // steps
    out_tile = lam_size // steps

    def body(count_ref, mask_ref, x_ref, o_ref, upper_ref, lower_ref, hot, keep, mid):
        row, col = lax.axis_index("row"), lax.axis_index("col")
        first = iota((sum_atoms, cols), 0) * BW
        lane = iota((sum_atoms, cols), 1)
        of_atom = ones_where((lane >= first) & (lane < first + BW))
        keep[...] = jnp.dot(ones_where(mask_ref[...] > 0), of_atom, preferred_element_type=F32).astype(BF16)
        pack_cols(count_ref, col * sum_atoms, sum_atoms, BW, sum_size, hot, unroll)

        @loop(steps, unroll)
        def _(i):
            at = span(i, tile)
            shape = (tile, lam_atoms)
            first = iota(shape, 1) * BW - i * tile
            atom = ones_where((iota(shape, 0) >= first) & (iota(shape, 0) < first + BW))
            kept = jnp.dot(atom, keep[...], preferred_element_type=F32)
            x = jnp.where(kept > 0.5, x_ref[at, :].astype(F32), 0.0).astype(BF16)
            mid[at, :] = jnp.dot(x, hot[...], preferred_element_type=F32).astype(BF16)

        place = place_row(count_ref, row * lam_atoms, lam_atoms, BW, unroll)

        @loop(steps, unroll)
        def _(i):
            at = span(i, out_tile)
            left = ones_where(iota((out_tile, rows), 0) + i * out_tile == place)
            o_ref[at, :] = jnp.dot(left, mid[...], preferred_element_type=F32).astype(BF16)

        upper_ref[...] = o_ref[pl.ds(0, TILE), :]
        lower_ref[...] = o_ref[pl.ds(TILE, lam_size - TILE), :]

    return pl.pallas_call(
        body,
        out_shape=[jax.ShapeDtypeStruct((n, sum_size), BF16) for n in (lam_size, TILE, lam_size - TILE)],
        in_specs=[SMEM_SPEC, VMEM_SPEC, VMEM_SPEC],
        out_specs=[VMEM_SPEC] * 3,
        scratch_shapes=[
            pltpu.VMEM((cols, sum_size), BF16),
            pltpu.VMEM((lam_atoms, cols), BF16),
            pltpu.VMEM((rows, sum_size), BF16),
        ],
        compiler_params=params(),
        cost_estimate=cost(2 * rows * sum_size * (cols + lam_size), 2 * rows * cols),
        name="pack_density",
    )(basis_count, mask, dens)


def pack_part(pieces, basis_count, first, ncols, chip_atoms, size, unroll):
    rows, cols = pieces[0].shape
    per = len(pieces)

    def body(count_ref, *refs):
        blocks, o_ref, full = refs[:per], refs[per], refs[per + 1]
        row, chip = lax.axis_index("row"), lax.axis_index("col") // CORES
        for i in range(per):
            at = lax.rem(chip ^ (first + i), per) * rows
            full[pl.ds(pl.multiple_of(at, rows), rows), :] = blocks[i][...]
        chips = (row * (ncols // CORES) + (chip ^ first)) // per * per
        if rows == chip_atoms * BW:
            hot = pack_rows(count_ref, chips * chip_atoms, per * chip_atoms, BW, size, unroll)
        else:
            hot = pack_rows(Sums(count_ref, chip_atoms), chips, per, rows, size, unroll)
        o_ref[...] = jnp.dot(hot, full[...], preferred_element_type=F32).astype(BF16)

    return pl.pallas_call(
        body,
        out_shape=jax.ShapeDtypeStruct((size, cols), BF16),
        in_specs=[SMEM_SPEC] + [VMEM_SPEC] * per,
        out_specs=VMEM_SPEC,
        scratch_shapes=[pltpu.VMEM((per * rows, cols), BF16)],
        compiler_params=params(),
        cost_estimate=cost((2 + 40 * first) * size * per * rows * cols, 2 * cols * (per * rows + size)),
        name="pack_part",
    )(basis_count, *pieces)


def exchange(x, axis, bit):
    peers = lax.axis_size(axis)
    return lax.ppermute(x, axis, [(i, i ^ bit) for i in range(peers)])


def after(x, *others):
    return lax.optimization_barrier((x, *others))[0]


def double(own, axis, bits):
    have = {0: own}
    for bit in bits:
        for far in sorted(have):
            have[far | bit] = exchange(have[far], axis, bit)
    return have


def add_parts(total, unroll, d_refs, sums, before=None):
    lam, cols = total.shape

    @loop(lam // TILE, unroll)
    def _(j):
        out = span(j, TILE)
        x = None if before is None else before[out, :]
        for chunks, part in zip(d_refs, sums):
            if len(chunks) == 1:
                d = chunks[0][out, :]
            elif isinstance(j, int):
                d = chunks[0][...] if j == 0 else chunks[1][span(j - 1, TILE), :]
            else:
                d = chunks[1][span(jnp.maximum(j - 1, 0), TILE), :].astype(F32)
                d = jnp.where(j == 0, chunks[0][...].astype(F32), d).astype(BF16)
            y = jnp.dot(d, part(), preferred_element_type=F32)
            x = y if x is None else x + y
        total[out, :] = x


def split_refs(dens, refs):
    lists, at = [], 0
    for chunks in dens.values():
        lists.append(refs[at : at + len(chunks)])
        at += len(chunks)
    return lists, refs[at:]


def flat(dens):
    return [chunk for chunks in dens.values() for chunk in chunks]


def ways_back(basis_count, ri_count, nrows, ncols, rows, wide, lam, cols, unroll):
    lam_atoms, blocks = rows // BW, wide // RW

    def body(count_ref, ri_ref, lam_hot, col_hot):
        row, col = lax.axis_index("row"), lax.axis_index("col")
        pack_cols(count_ref, row * lam_atoms, lam_atoms, BW, lam, lam_hot, unroll)
        place = place_row(ri_ref, col * blocks, blocks, RW, unroll)

        @loop(cols // RW, unroll)
        def _(i):
            col_hot[span(i, RW), :] = ones_where(iota((RW, wide), 0) + i * RW == place)

    return pl.pallas_call(
        body,
        out_shape=[jax.ShapeDtypeStruct((rows, lam), BF16), jax.ShapeDtypeStruct((cols, wide), BF16)],
        in_specs=[SMEM_SPEC, SMEM_SPEC],
        out_specs=[VMEM_SPEC] * 2,
        compiler_params=params(16 * 1024 * 1024),
        name="ways_back",
    )(basis_count, ri_count)


def contract_near(dens, integrals, ncols, unroll):
    lam, depth = dens[0][0].shape
    groups, nrows = len(integrals), len(integrals[0])
    sums = [integrals[g][far] for far in range(nrows) for g in range(groups)]
    cols = sums[0].shape[1]
    n, parts = len(dens), len(sums)

    def body(*refs):
        d_refs, refs = split_refs(dens, refs)
        s_refs, refs = refs[:parts], refs[parts:]
        total, s_rest, s_all, s_sem, r_sem = refs
        row, col = lax.axis_index("row"), lax.axis_index("col")
        for j, ref in enumerate(s_refs):
            part = (row ^ (j // groups)) * groups + (col // (ncols // groups) ^ (j % groups))
            pltpu.make_async_copy(ref, s_all.at[part], s_sem.at[part]).start()

        @pl.loop(0, parts)
        def _(i):
            pltpu.make_async_copy(s_all.at[i], s_all.at[i], s_sem.at[i]).wait()

        rest = [
            pltpu.make_async_copy(s_all.at[col ^ far], s_rest.at[far - n], r_sem.at[far - n])
            for far in range(n, parts)
        ]
        for copy in rest:
            copy.start()
        add_parts(total, unroll, d_refs, [lambda far=far: s_all[col ^ far] for far in range(n)])
        for copy in rest:
            copy.wait()

    need = 2 * (n * depth * lam + 2 * parts * depth * cols + 4 * lam * cols)
    return pl.pallas_call(
        body,
        out_shape=[
            jax.ShapeDtypeStruct((lam, cols), F32),
            jax.ShapeDtypeStruct((parts - n, depth, cols), BF16),
        ],
        in_specs=[VMEM_SPEC] * n + [ANY_SPEC] * parts,
        out_specs=[VMEM_SPEC] * 2,
        scratch_shapes=[
            pltpu.VMEM((parts, depth, cols), BF16),
            pltpu.SemaphoreType.DMA((parts,)),
            pltpu.SemaphoreType.DMA((parts - n,)),
        ],
        compiler_params=params(need + 4 * 1024 * 1024),
        cost_estimate=cost(2 * n * depth * lam * cols, 2 * n * depth * (lam + cols)),
        name="contract_near",
    )(*flat(dens), *sums)


def contract_far(dens, first, total, sums, unroll):
    (lam, cols), depth = total.shape, sums.shape[1]
    n = len(dens)

    def body(before, s_ref, *refs):
        d_refs, (o_ref,) = split_refs(dens, refs)
        add_parts(o_ref, unroll, d_refs, [lambda i=i: s_ref[first + i] for i in range(n)], before)

    need = 2 * (n * depth * lam + sums.size + 4 * lam * cols)
    return pl.pallas_call(
        body,
        out_shape=jax.ShapeDtypeStruct((lam, cols), F32),
        in_specs=[VMEM_SPEC] * (2 + len(flat(dens))),
        out_specs=VMEM_SPEC,
        compiler_params=params(need + 4 * 1024 * 1024),
        cost_estimate=cost(2 * n * depth * lam * cols, 2 * n * depth * (lam + cols)),
        name="contract_far",
    )(total, sums, *flat(dens))


def contract_last(dens, first, total, sums, lam_hot, col_hot, unroll):
    (rows, lam), (cols, wide) = lam_hot.shape, col_hot.shape
    depth = sums.shape[1]
    n = len(dens)
    half = lam // 2

    def body(before, s_ref, lam_hot, col_hot, *refs):
        d_refs, (o_ref, total, packed) = split_refs(dens, refs)
        add_parts(total, unroll, d_refs, [lambda i=i: s_ref[first + i] for i in range(n)], before)

        @loop(2, unroll)
        def _(j):
            x = total[span(j, half), :].astype(BF16)
            packed[span(j, half), :] = jnp.dot(x, col_hot[...], preferred_element_type=F32).astype(BF16)

        @loop(4, unroll)
        def _(j):
            out = span(j, rows // 4)
            o_ref[out, :] = jnp.dot(lam_hot[out, :], packed[...], preferred_element_type=F32).astype(BF16)

    need = 2 * (n * depth * lam + sums.size + 4 * lam * cols + rows * lam + cols * wide + (lam + rows) * wide)
    return pl.pallas_call(
        body,
        out_shape=jax.ShapeDtypeStruct((rows, wide), BF16),
        in_specs=[VMEM_SPEC] * (4 + len(flat(dens))),
        out_specs=VMEM_SPEC,
        scratch_shapes=[pltpu.VMEM((lam, cols), F32), pltpu.VMEM((lam, wide), BF16)],
        compiler_params=params(need + 4 * 1024 * 1024),
        cost_estimate=cost(2 * n * depth * lam * cols, 2 * n * depth * (lam + cols)),
        name="contract_last",
    )(total, sums, lam_hot, col_hot, *flat(dens))


def program(lam_size, sum_size, col_size, chip_size, common):
    unroll = common

    def run(three_center, density, block_mask, density_mask, basis_count, ri_count):
        ncols = lax.axis_size("col")
        nrows = lax.axis_size("row")
        chips = ncols // CORES
        rows, depth = density.shape
        wide = three_center.shape[1] // ncols
        row_bits = [1 << b for b in range(nrows.bit_length() - 1)]
        chip_bits = [CORES << b for b in range(chips.bit_length() - 1)][::-1]
        far_bit, near_bits = chip_bits[0], chip_bits[1:]

        counts = (block_mask, basis_count, ri_count, ncols, col_size, unroll, chip_size)
        other = exchange(pack_integrals(three_center, *counts)[0], "col", 1)
        own, upper, lower = pack_density(density, density_mask, basis_count, lam_size, sum_size, unroll)
        lines = [{0: upper, far_bit: exchange(upper, "col", far_bit)}, {0: lower}]
        near = {0: own, 1: exchange(own, "col", 1)}
        pieces = pack_integrals(three_center, *counts, after(other, own))
        early = lines[0][far_bit]
        got = [pieces[0]] + [exchange(pieces[t], "col", CORES * t) for t in range(1, chips)]
        chip_rows = CORES * three_center.shape[0]
        per = depth // chip_rows
        lam_hot, col_hot = ways_back(
            basis_count, ri_count, nrows, ncols, rows, wide, lam_size, col_size, unroll
        )
        parts, groups, orders = [], [], []
        for g in range(chips // per):
            arrived = got[g * per : (g + 1) * per]
            if g == 0:
                arrived = [after(arrived[0], near[1])] + arrived[1:]
            elif g == 1:
                arrived = [after(arrived[0], lam_hot)] + arrived[1:]
            part = pack_part(arrived, basis_count, g * per, ncols, chip_rows // BW, sum_size, unroll)
            if g == 0:
                near.update(double(after(own, part), "col", near_bits))
                steps = [near[far] for far in near if far > 1]
            else:
                part = after(part, *[groups[0][bit] for bit in row_bits])
            parts.append(part)
            orders.append(row_bits if g % 2 == 0 else row_bits[::-1])
            groups.append({0: part})
            for bit in orders[g]:
                groups[g][bit] = exchange(part, "row", bit)
        step = groups[-1][orders[-1][0]]
        across = exchange(after(early, parts[-1]), "col", 1)
        forward = double(after(early, across, *steps), "col", near_bits)
        lines[0].update({far_bit | far: block for far, block in forward.items() if far > 0})
        lines[1][far_bit] = exchange(after(lower, parts[-1]), "col", far_bit)
        for far in [far for far in near if far > 1]:
            near[far | 1] = exchange(after(near[far], across), "col", 1)
        for g, have in enumerate(groups):
            done = [0, orders[g][0]]
            for bit in orders[g][1:]:
                for far in done[1:]:
                    block = have[far] if g == len(groups) - 1 else after(have[far], *[groups[-1][bit] for bit in row_bits])
                    have[far | bit] = exchange(block, "row", bit)
                done += [far | bit for far in done]
        first = {far: [near[far]] for far in sorted(near)}
        total, sums = contract_near(first, groups, ncols, unroll)
        block = after(lines[1][far_bit], lines[0][ncols - CORES])
        for away, block in double(block, "col", near_bits).items():
            lines[1][far_bit | away] = block
        middle = {}
        for far in range(far_bit, ncols - CORES, CORES):
            middle[far] = [line[far] for line in lines]
            middle[far | 1] = [across if line[far] is early else exchange(line[far], "col", 1) for line in lines]
        total = contract_far(middle, 0, total, sums, unroll)
        ends = [line[ncols - CORES] for line in lines]
        last = {ncols - CORES: ends}
        last[ncols - 1] = [exchange(ends[0], "col", 1), exchange(after(ends[1], total), "col", 1)]
        return contract_last(last, len(middle), total, sums, lam_hot, col_hot, unroll)

    return run


def choose(here, yes, no):
    return lambda *args: lax.cond(here, yes, no, *args)


def shards(three_center, density, block_mask, density_mask, basis_count, ri_count):
    ncols = lax.axis_size("col")
    nrows = lax.axis_size("row")
    rows, depth = density.shape
    wide = three_center.shape[1] // ncols
    chip = CORES * three_center.shape[0]
    levels = (
        (rows * 3 // 4, depth * 3 // 4, wide * 5 // 6, chip * 7 // 8),
        (rows * 3 // 4, depth, wide * 5 // 6, chip),
        (rows * 3 // 4, depth, wide, chip),
        (rows, depth, wide, chip),
    )
    level = first_fit(basis_count, ri_count, (nrows, ncols, ncols, nrows * ncols // CORES), levels)
    args = (three_center, density, block_mask, density_mask, basis_count, ri_count)
    run = program(*levels[-1], False)
    for n in reversed(range(len(levels) - 1)):
        run = choose(level[0] == n, program(*levels[n], n == 0), run)
    return run(*args)


def solution(mesh):
    in_specs = (
        P(("row", "col"), None),
        P("row", "col"),
        P(("row", "col"), None),
        P("row", "col"),
        P(),
        P(),
    )
    return jax.shard_map(
        shards, mesh=mesh, in_specs=in_specs, out_specs=P("row", "col"), check_vma=False
    )
```

```python
import jax
import jax.numpy as jnp
from jax import lax
from jax.experimental import pallas as pl
from jax.experimental.pallas import tpu as pltpu
from jax.sharding import PartitionSpec as P

BW = 32
RW = 128
CORES = 2
VMEM = 48 * 1024 * 1024
TILE = 256
BF16 = jnp.bfloat16
F32 = jnp.float32
SMEM_SPEC = pl.BlockSpec(memory_space=pltpu.SMEM)
VMEM_SPEC = pl.BlockSpec(memory_space=pltpu.VMEM)
ANY_SPEC = pl.BlockSpec(memory_space=pl.ANY)


def params(limit=VMEM):
    return pltpu.CompilerParams(vmem_limit_bytes=limit)


def cost(flops, bytes_accessed):
    return pl.CostEstimate(flops=flops, bytes_accessed=bytes_accessed, transcendentals=0)


def ones_where(cond):
    return jnp.where(cond, 1.0, 0.0).astype(BF16)


def iota(shape, axis):
    return lax.broadcasted_iota(jnp.int32, shape, axis)


def loop(n, unroll):
    def run(f):
        if unroll:
            for i in range(n):
                f(i)
        else:
            pl.loop(0, n)(f)

    return run


def span(i, size):
    return pl.ds(i * size if isinstance(i, int) else pl.multiple_of(i * size, size), size)


def place_row(count_ref, base, atoms, width, unroll):
    lane = iota((1, atoms * width), 1)

    def atom(a, carry):
        place, offset = carry
        count = count_ref[base + a]
        inside = (lane >= a * width) & (lane < a * width + count)
        return jnp.where(inside, lane - a * width + offset, place), offset + count

    carry = (jnp.full(lane.shape, -1, jnp.int32), jnp.int32(0))
    if not unroll:
        return lax.fori_loop(0, atoms, atom, carry)[0]
    for a in range(atoms):
        carry = atom(a, carry)
    return carry[0]


def pack_rows(count_ref, base, atoms, width, size, unroll):
    place = place_row(count_ref, base, atoms, width, unroll)
    return ones_where(iota((size, atoms * width), 0) == place)


def pack_cols(count_ref, base, atoms, width, size, out, unroll):
    def atom(a, offset):
        count = count_ref[base + a]
        lanes = min(size, (a + 1) * width) if unroll and width % 128 == 0 else size
        slot = iota((width, lanes), 0)
        gap = iota((width, lanes), 1) - slot
        out[span(a, width), pl.ds(0, lanes)] = ones_where((gap == offset) & (slot < count))
        return offset + count

    if unroll:
        offset = jnp.int32(0)
        for a in range(atoms):
            offset = atom(a, offset)
    else:
        lax.fori_loop(0, atoms, atom, jnp.int32(0))


class Sums:
    def __init__(self, ref, atoms):
        self.ref, self.atoms = ref, atoms

    def __getitem__(self, i):
        total = self.ref[i * self.atoms]
        for a in range(1, self.atoms):
            total = total + self.ref[i * self.atoms + a]
        return total


def first_fit(basis_count, ri_count, groups, levels):
    def body(count_ref, ri_ref, o_ref):
        level = jnp.int32(0)
        for axis, (ref, parts) in enumerate(zip((count_ref, count_ref, ri_ref, count_ref), groups)):
            per = ref.shape[0] // parts
            most = jnp.int32(0)
            for g in range(parts):
                total = jnp.int32(0)
                for i in range(per):
                    total = total + ref[g * per + i]
                most = jnp.maximum(most, total)
            for n, sizes in enumerate(levels[:-1]):
                level = jnp.where(most > sizes[axis], jnp.maximum(level, n + 1), level)
        o_ref[0] = level

    return pl.pallas_call(
        body,
        out_shape=jax.ShapeDtypeStruct((1,), jnp.int32),
        in_specs=[SMEM_SPEC, SMEM_SPEC],
        out_specs=SMEM_SPEC,
        name="first_fit",
    )(basis_count, ri_count)


def pack_integrals(tc, block_mask, basis_count, ri_count, ncols, packed, unroll, chip_rows, arrived=None):
    rows, cols = tc.shape
    atoms = rows // BW
    wide = cols // ncols
    blocks = wide // RW
    chips = ncols // CORES
    first = arrived is None

    def body(count_ref, ri_ref, mask_ref, x_ref, *refs):
        outs = refs[:1] if first else refs[1 : 1 + chips]
        held, hot = refs[-2:] if first else refs[-4:-2]
        made, both = (outs[0], None) if first else refs[-2:]
        row, col = lax.axis_index("row"), lax.axis_index("col")
        base = (row * ncols + col) * atoms
        hot[...] = jnp.zeros_like(hot)

        @loop(chips, unroll)
        def _(t):
            dest = col ^ (CORES * t + (1 if first else 0))

            @loop(blocks, unroll)
            def _(b):
                lanes = pl.ds(pl.multiple_of(dest * wide + b * RW, RW), RW)
                slot = iota((BW, RW), 0)
                for a in range(atoms):
                    limit = jnp.where(mask_ref[a, dest * blocks + b] > 0, count_ref[base + a], 0)
                    x = x_ref[pl.ds(a * BW, BW), lanes].astype(F32)
                    held[pl.ds(a * BW, BW), span(b, RW)] = jnp.where(slot < limit, x, 0.0).astype(BF16)

            pack_cols(ri_ref, dest * blocks, blocks, RW, packed, hot, unroll)
            made[t] = jnp.dot(held[...], hot[...], preferred_element_type=F32).astype(BF16)

        if not first:
            core = lax.rem(col, CORES)
            chip = (row * ncols + col - core) * atoms
            for t in range(chips):
                into = outs[t] if chip_rows == CORES * rows else both.at[t]
                into[pl.ds(pl.multiple_of(core * rows, rows), rows), :] = made[t]
                into[pl.ds(pl.multiple_of((1 - core) * rows, rows), rows), :] = refs[0][t]
            if chip_rows < CORES * rows:
                left = pack_rows(count_ref, chip, CORES * atoms, BW, chip_rows, unroll)
                for t in range(chips):
                    outs[t][...] = jnp.dot(left, both[t], preferred_element_type=F32).astype(BF16)

    shape = (chips, rows, packed)
    merged = jax.ShapeDtypeStruct((chip_rows, packed), BF16)
    out_shape = [jax.ShapeDtypeStruct(shape, BF16)] if first else [merged] * chips
    out_specs = [VMEM_SPEC] * len(out_shape)
    return pl.pallas_call(
        body,
        out_shape=out_shape,
        in_specs=[SMEM_SPEC, SMEM_SPEC, SMEM_SPEC] + [VMEM_SPEC] * (1 if first else 2),
        out_specs=out_specs,
        scratch_shapes=[pltpu.VMEM((rows, wide), BF16), pltpu.VMEM((wide, packed), BF16)]
        + ([] if first else [pltpu.VMEM(shape, BF16), pltpu.VMEM((chips, CORES * rows, packed), BF16)]),
        compiler_params=params(),
        cost_estimate=cost(rows * cols * packed, rows * cols + 3 * chips * rows * packed),
        name="pack_other_core" if first else "pack_own_core",
    )(basis_count, ri_count, block_mask, tc, *([] if first else [arrived]))


def pack_density(dens, mask, basis_count, lam_size, sum_size, unroll):
    rows, cols = dens.shape
    lam_atoms, sum_atoms = mask.shape
    steps = 1 if unroll else 4
    tile = rows // steps
    out_tile = lam_size // steps

    def body(count_ref, mask_ref, x_ref, o_ref, upper_ref, lower_ref, hot, keep, mid):
        row, col = lax.axis_index("row"), lax.axis_index("col")
        first = iota((sum_atoms, cols), 0) * BW
        lane = iota((sum_atoms, cols), 1)
        of_atom = ones_where((lane >= first) & (lane < first + BW))
        keep[...] = jnp.dot(ones_where(mask_ref[...] > 0), of_atom, preferred_element_type=F32).astype(BF16)
        pack_cols(count_ref, col * sum_atoms, sum_atoms, BW, sum_size, hot, unroll)

        @loop(steps, unroll)
        def _(i):
            at = span(i, tile)
            shape = (tile, lam_atoms)
            first = iota(shape, 1) * BW - i * tile
            atom = ones_where((iota(shape, 0) >= first) & (iota(shape, 0) < first + BW))
            kept = jnp.dot(atom, keep[...], preferred_element_type=F32)
            x = jnp.where(kept > 0.5, x_ref[at, :].astype(F32), 0.0).astype(BF16)
            mid[at, :] = jnp.dot(x, hot[...], preferred_element_type=F32).astype(BF16)

        place = place_row(count_ref, row * lam_atoms, lam_atoms, BW, unroll)

        @loop(steps, unroll)
        def _(i):
            at = span(i, out_tile)
            left = ones_where(iota((out_tile, rows), 0) + i * out_tile == place)
            o_ref[at, :] = jnp.dot(left, mid[...], preferred_element_type=F32).astype(BF16)

        upper_ref[...] = o_ref[pl.ds(0, TILE), :]
        lower_ref[...] = o_ref[pl.ds(TILE, lam_size - TILE), :]

    return pl.pallas_call(
        body,
        out_shape=[jax.ShapeDtypeStruct((n, sum_size), BF16) for n in (lam_size, TILE, lam_size - TILE)],
        in_specs=[SMEM_SPEC, VMEM_SPEC, VMEM_SPEC],
        out_specs=[VMEM_SPEC] * 3,
        scratch_shapes=[
            pltpu.VMEM((cols, sum_size), BF16),
            pltpu.VMEM((lam_atoms, cols), BF16),
            pltpu.VMEM((rows, sum_size), BF16),
        ],
        compiler_params=params(),
        cost_estimate=cost(2 * rows * sum_size * (cols + lam_size), 2 * rows * cols),
        name="pack_density",
    )(basis_count, mask, dens)


def pack_part(pieces, basis_count, first, ncols, chip_atoms, size, unroll):
    rows, cols = pieces[0].shape
    per = len(pieces)

    def body(count_ref, *refs):
        blocks, o_ref, full = refs[:per], refs[per], refs[per + 1]
        row, chip = lax.axis_index("row"), lax.axis_index("col") // CORES
        for i in range(per):
            at = lax.rem(chip ^ (first + i), per) * rows
            full[pl.ds(pl.multiple_of(at, rows), rows), :] = blocks[i][...]
        chips = (row * (ncols // CORES) + (chip ^ first)) // per * per
        if rows == chip_atoms * BW:
            hot = pack_rows(count_ref, chips * chip_atoms, per * chip_atoms, BW, size, unroll)
        else:
            hot = pack_rows(Sums(count_ref, chip_atoms), chips, per, rows, size, unroll)
        o_ref[...] = jnp.dot(hot, full[...], preferred_element_type=F32).astype(BF16)

    return pl.pallas_call(
        body,
        out_shape=jax.ShapeDtypeStruct((size, cols), BF16),
        in_specs=[SMEM_SPEC] + [VMEM_SPEC] * per,
        out_specs=VMEM_SPEC,
        scratch_shapes=[pltpu.VMEM((per * rows, cols), BF16)],
        compiler_params=params(),
        cost_estimate=cost((2 + 40 * first) * size * per * rows * cols, 2 * cols * (per * rows + size)),
        name="pack_part",
    )(basis_count, *pieces)


def exchange(x, axis, bit):
    peers = lax.axis_size(axis)
    return lax.ppermute(x, axis, [(i, i ^ bit) for i in range(peers)])


def after(x, *others):
    return lax.optimization_barrier((x, *others))[0]


def double(own, axis, bits):
    have = {0: own}
    for bit in bits:
        for far in sorted(have):
            have[far | bit] = exchange(have[far], axis, bit)
    return have


def add_parts(total, unroll, d_refs, sums, before=None):
    lam, cols = total.shape

    @loop(lam // TILE, unroll)
    def _(j):
        out = span(j, TILE)
        x = None if before is None else before[out, :]
        for chunks, part in zip(d_refs, sums):
            if len(chunks) == 1:
                d = chunks[0][out, :]
            elif isinstance(j, int):
                d = chunks[0][...] if j == 0 else chunks[1][span(j - 1, TILE), :]
            else:
                d = chunks[1][span(jnp.maximum(j - 1, 0), TILE), :].astype(F32)
                d = jnp.where(j == 0, chunks[0][...].astype(F32), d).astype(BF16)
            y = jnp.dot(d, part(), preferred_element_type=F32)
            x = y if x is None else x + y
        total[out, :] = x


def split_refs(dens, refs):
    lists, at = [], 0
    for chunks in dens.values():
        lists.append(refs[at : at + len(chunks)])
        at += len(chunks)
    return lists, refs[at:]


def flat(dens):
    return [chunk for chunks in dens.values() for chunk in chunks]


def ways_back(basis_count, ri_count, nrows, ncols, rows, wide, lam, cols, unroll):
    lam_atoms, blocks = rows // BW, wide // RW

    def body(count_ref, ri_ref, lam_hot, col_hot):
        row, col = lax.axis_index("row"), lax.axis_index("col")
        pack_cols(count_ref, row * lam_atoms, lam_atoms, BW, lam, lam_hot, unroll)
        place = place_row(ri_ref, col * blocks, blocks, RW, unroll)

        @loop(cols // RW, unroll)
        def _(i):
            col_hot[span(i, RW), :] = ones_where(iota((RW, wide), 0) + i * RW == place)

    return pl.pallas_call(
        body,
        out_shape=[jax.ShapeDtypeStruct((rows, lam), BF16), jax.ShapeDtypeStruct((cols, wide), BF16)],
        in_specs=[SMEM_SPEC, SMEM_SPEC],
        out_specs=[VMEM_SPEC] * 2,
        compiler_params=params(16 * 1024 * 1024),
        name="ways_back",
    )(basis_count, ri_count)


def contract_near(dens, integrals, ncols, unroll):
    lam, depth = dens[0][0].shape
    groups, nrows = len(integrals), len(integrals[0])
    sums = [integrals[g][far] for far in range(nrows) for g in range(groups)]
    cols = sums[0].shape[1]
    n, parts = len(dens), len(sums)

    def body(*refs):
        d_refs, refs = split_refs(dens, refs)
        s_refs, refs = refs[:parts], refs[parts:]
        total, s_rest, s_all, s_sem, r_sem = refs
        row, col = lax.axis_index("row"), lax.axis_index("col")
        for j, ref in enumerate(s_refs):
            part = (row ^ (j // groups)) * groups + (col // (ncols // groups) ^ (j % groups))
            pltpu.make_async_copy(ref, s_all.at[part], s_sem.at[part]).start()

        @pl.loop(0, parts)
        def _(i):
            pltpu.make_async_copy(s_all.at[i], s_all.at[i], s_sem.at[i]).wait()

        rest = [
            pltpu.make_async_copy(s_all.at[col ^ far], s_rest.at[far - n], r_sem.at[far - n])
            for far in range(n, parts)
        ]
        for copy in rest:
            copy.start()
        add_parts(total, unroll, d_refs, [lambda far=far: s_all[col ^ far] for far in range(n)])
        for copy in rest:
            copy.wait()

    need = 2 * (n * depth * lam + 2 * parts * depth * cols + 4 * lam * cols)
    return pl.pallas_call(
        body,
        out_shape=[
            jax.ShapeDtypeStruct((lam, cols), F32),
            jax.ShapeDtypeStruct((parts - n, depth, cols), BF16),
        ],
        in_specs=[VMEM_SPEC] * n + [ANY_SPEC] * parts,
        out_specs=[VMEM_SPEC] * 2,
        scratch_shapes=[
            pltpu.VMEM((parts, depth, cols), BF16),
            pltpu.SemaphoreType.DMA((parts,)),
            pltpu.SemaphoreType.DMA((parts - n,)),
        ],
        compiler_params=params(need + 4 * 1024 * 1024),
        cost_estimate=cost(2 * n * depth * lam * cols, 2 * n * depth * (lam + cols)),
        name="contract_near",
    )(*flat(dens), *sums)


def contract_far(dens, first, total, sums, unroll):
    (lam, cols), depth = total.shape, sums.shape[1]
    n = len(dens)

    def body(before, s_ref, *refs):
        d_refs, (o_ref,) = split_refs(dens, refs)
        add_parts(o_ref, unroll, d_refs, [lambda i=i: s_ref[first + i] for i in range(n)], before)

    need = 2 * (n * depth * lam + sums.size + 4 * lam * cols)
    return pl.pallas_call(
        body,
        out_shape=jax.ShapeDtypeStruct((lam, cols), F32),
        in_specs=[VMEM_SPEC] * (2 + len(flat(dens))),
        out_specs=VMEM_SPEC,
        compiler_params=params(need + 4 * 1024 * 1024),
        cost_estimate=cost(2 * n * depth * lam * cols, 2 * n * depth * (lam + cols)),
        name="contract_far",
    )(total, sums, *flat(dens))


def contract_last(dens, first, total, sums, lam_hot, col_hot, unroll):
    (rows, lam), (cols, wide) = lam_hot.shape, col_hot.shape
    depth = sums.shape[1]
    n = len(dens)
    half = lam // 2

    def body(before, s_ref, lam_hot, col_hot, *refs):
        d_refs, (o_ref, total, packed) = split_refs(dens, refs)
        add_parts(total, unroll, d_refs, [lambda i=i: s_ref[first + i] for i in range(n)], before)

        @loop(2, unroll)
        def _(j):
            x = total[span(j, half), :].astype(BF16)
            packed[span(j, half), :] = jnp.dot(x, col_hot[...], preferred_element_type=F32).astype(BF16)

        @loop(4, unroll)
        def _(j):
            out = span(j, rows // 4)
            o_ref[out, :] = jnp.dot(lam_hot[out, :], packed[...], preferred_element_type=F32).astype(BF16)

    need = 2 * (n * depth * lam + sums.size + 4 * lam * cols + rows * lam + cols * wide + (lam + rows) * wide)
    return pl.pallas_call(
        body,
        out_shape=jax.ShapeDtypeStruct((rows, wide), BF16),
        in_specs=[VMEM_SPEC] * (4 + len(flat(dens))),
        out_specs=VMEM_SPEC,
        scratch_shapes=[pltpu.VMEM((lam, cols), F32), pltpu.VMEM((lam, wide), BF16)],
        compiler_params=params(need + 4 * 1024 * 1024),
        cost_estimate=cost(2 * n * depth * lam * cols, 2 * n * depth * (lam + cols)),
        name="contract_last",
    )(total, sums, lam_hot, col_hot, *flat(dens))


def program(lam_size, sum_size, col_size, chip_size, common):
    unroll = common

    def run(three_center, density, block_mask, density_mask, basis_count, ri_count):
        ncols = lax.axis_size("col")
        nrows = lax.axis_size("row")
        chips = ncols // CORES
        rows, depth = density.shape
        wide = three_center.shape[1] // ncols
        row_bits = [1 << b for b in range(nrows.bit_length() - 1)]
        chip_bits = [CORES << b for b in range(chips.bit_length() - 1)][::-1]
        far_bit, near_bits = chip_bits[0], chip_bits[1:]

        counts = (block_mask, basis_count, ri_count, ncols, col_size, unroll, chip_size)
        other = exchange(pack_integrals(three_center, *counts)[0], "col", 1)
        own, upper, lower = pack_density(density, density_mask, basis_count, lam_size, sum_size, unroll)
        lines = [{0: upper, far_bit: exchange(upper, "col", far_bit)}, {0: lower}]
        near = {0: own, 1: exchange(own, "col", 1)}
        pieces = pack_integrals(three_center, *counts, after(other, own))
        early = lines[0][far_bit]
        got = [pieces[0]] + [exchange(pieces[t], "col", CORES * t) for t in range(1, chips)]
        chip_rows = CORES * three_center.shape[0]
        per = depth // chip_rows
        lam_hot, col_hot = ways_back(
            basis_count, ri_count, nrows, ncols, rows, wide, lam_size, col_size, unroll
        )
        parts, groups, orders = [], [], []
        for g in range(chips // per):
            arrived = got[g * per : (g + 1) * per]
            if g == 0:
                arrived = [after(arrived[0], near[1])] + arrived[1:]
            elif g == 1:
                arrived = [after(arrived[0], lam_hot)] + arrived[1:]
            part = pack_part(arrived, basis_count, g * per, ncols, chip_rows // BW, sum_size, unroll)
            if g == 0:
                near.update(double(after(own, part), "col", near_bits))
                steps = [near[far] for far in near if far > 1]
            else:
                part = after(part, *[groups[0][bit] for bit in row_bits])
            parts.append(part)
            orders.append(row_bits if g % 2 == 0 else row_bits[::-1])
            groups.append({0: part})
            for bit in orders[g]:
                groups[g][bit] = exchange(part, "row", bit)
        step = groups[-1][orders[-1][0]]
        across = exchange(after(early, step), "col", 1)
        forward = double(after(early, step, *steps), "col", near_bits)
        lines[0].update({far_bit | far: block for far, block in forward.items() if far > 0})
        lines[1][far_bit] = exchange(after(lower, parts[-1]), "col", far_bit)
        for far in [far for far in near if far > 1]:
            near[far | 1] = exchange(after(near[far], parts[-1]), "col", 1)
        for g, have in enumerate(groups):
            done = [0, orders[g][0]]
            for bit in orders[g][1:]:
                for far in done[1:]:
                    block = have[far] if g == len(groups) - 1 else after(have[far], *[groups[-1][bit] for bit in row_bits])
                    have[far | bit] = exchange(block, "row", bit)
                done += [far | bit for far in done]
        first = {far: [near[far]] for far in sorted(near)}
        total, sums = contract_near(first, groups, ncols, unroll)
        block = after(lines[1][far_bit], lines[0][ncols - CORES])
        for away, block in double(block, "col", near_bits).items():
            lines[1][far_bit | away] = block
        middle = {}
        for far in range(far_bit, ncols - CORES, CORES):
            middle[far] = [line[far] for line in lines]
            middle[far | 1] = [across if line[far] is early else exchange(line[far], "col", 1) for line in lines]
        total = contract_far(middle, 0, total, sums, unroll)
        ends = [line[ncols - CORES] for line in lines]
        last = {ncols - CORES: ends}
        last[ncols - 1] = [exchange(ends[0], "col", 1), exchange(after(ends[1], total), "col", 1)]
        return contract_last(last, len(middle), total, sums, lam_hot, col_hot, unroll)

    return run


def choose(here, yes, no):
    return lambda *args: lax.cond(here, yes, no, *args)


def shards(three_center, density, block_mask, density_mask, basis_count, ri_count):
    ncols = lax.axis_size("col")
    nrows = lax.axis_size("row")
    rows, depth = density.shape
    wide = three_center.shape[1] // ncols
    chip = CORES * three_center.shape[0]
    levels = (
        (rows * 3 // 4, depth * 3 // 4, wide * 5 // 6, chip * 7 // 8),
        (rows * 3 // 4, depth, wide * 5 // 6, chip),
        (rows * 3 // 4, depth, wide, chip),
        (rows, depth, wide, chip),
    )
    level = first_fit(basis_count, ri_count, (nrows, ncols, ncols, nrows * ncols // CORES), levels)
    args = (three_center, density, block_mask, density_mask, basis_count, ri_count)
    run = program(*levels[-1], False)
    for n in reversed(range(len(levels) - 1)):
        run = choose(level[0] == n, program(*levels[n], n == 0), run)
    return run(*args)


def solution(mesh):
    in_specs = (
        P(("row", "col"), None),
        P("row", "col"),
        P(("row", "col"), None),
        P("row", "col"),
        P(),
        P(),
    )
    return jax.shard_map(
        shards, mesh=mesh, in_specs=in_specs, out_specs=P("row", "col"), check_vma=False
    )
```

```python
import jax
import jax.numpy as jnp
from jax import lax
from jax.experimental import pallas as pl
from jax.experimental.pallas import tpu as pltpu
from jax.sharding import PartitionSpec as P

BW = 32
RW = 128
CORES = 2
VMEM = 48 * 1024 * 1024
TILE = 256
BF16 = jnp.bfloat16
F32 = jnp.float32
SMEM_SPEC = pl.BlockSpec(memory_space=pltpu.SMEM)
VMEM_SPEC = pl.BlockSpec(memory_space=pltpu.VMEM)
ANY_SPEC = pl.BlockSpec(memory_space=pl.ANY)


def params(limit=VMEM):
    return pltpu.CompilerParams(vmem_limit_bytes=limit)


def cost(flops, bytes_accessed):
    return pl.CostEstimate(flops=flops, bytes_accessed=bytes_accessed, transcendentals=0)


def ones_where(cond):
    return jnp.where(cond, 1.0, 0.0).astype(BF16)


def iota(shape, axis):
    return lax.broadcasted_iota(jnp.int32, shape, axis)


def loop(n, unroll):
    def run(f):
        if unroll:
            for i in range(n):
                f(i)
        else:
            pl.loop(0, n)(f)

    return run


def span(i, size):
    return pl.ds(i * size if isinstance(i, int) else pl.multiple_of(i * size, size), size)


def place_row(count_ref, base, atoms, width, unroll):
    lane = iota((1, atoms * width), 1)

    def atom(a, carry):
        place, offset = carry
        count = count_ref[base + a]
        inside = (lane >= a * width) & (lane < a * width + count)
        return jnp.where(inside, lane - a * width + offset, place), offset + count

    carry = (jnp.full(lane.shape, -1, jnp.int32), jnp.int32(0))
    if not unroll:
        return lax.fori_loop(0, atoms, atom, carry)[0]
    for a in range(atoms):
        carry = atom(a, carry)
    return carry[0]


def pack_rows(count_ref, base, atoms, width, size, unroll):
    place = place_row(count_ref, base, atoms, width, unroll)
    return ones_where(iota((size, atoms * width), 0) == place)


def pack_cols(count_ref, base, atoms, width, size, out, unroll):
    def atom(a, offset):
        count = count_ref[base + a]
        lanes = min(size, (a + 1) * width) if unroll and width % 128 == 0 else size
        slot = iota((width, lanes), 0)
        gap = iota((width, lanes), 1) - slot
        out[span(a, width), pl.ds(0, lanes)] = ones_where((gap == offset) & (slot < count))
        return offset + count

    if unroll:
        offset = jnp.int32(0)
        for a in range(atoms):
            offset = atom(a, offset)
    else:
        lax.fori_loop(0, atoms, atom, jnp.int32(0))


class Sums:
    def __init__(self, ref, atoms):
        self.ref, self.atoms = ref, atoms

    def __getitem__(self, i):
        total = self.ref[i * self.atoms]
        for a in range(1, self.atoms):
            total = total + self.ref[i * self.atoms + a]
        return total


def first_fit(basis_count, ri_count, groups, levels):
    def body(count_ref, ri_ref, o_ref):
        level = jnp.int32(0)
        for axis, (ref, parts) in enumerate(zip((count_ref, count_ref, ri_ref, count_ref), groups)):
            per = ref.shape[0] // parts
            most = jnp.int32(0)
            for g in range(parts):
                total = jnp.int32(0)
                for i in range(per):
                    total = total + ref[g * per + i]
                most = jnp.maximum(most, total)
            for n, sizes in enumerate(levels[:-1]):
                level = jnp.where(most > sizes[axis], jnp.maximum(level, n + 1), level)
        o_ref[0] = level

    return pl.pallas_call(
        body,
        out_shape=jax.ShapeDtypeStruct((1,), jnp.int32),
        in_specs=[SMEM_SPEC, SMEM_SPEC],
        out_specs=SMEM_SPEC,
        name="first_fit",
    )(basis_count, ri_count)


def pack_integrals(tc, block_mask, basis_count, ri_count, ncols, packed, unroll, chip_rows, arrived=None):
    rows, cols = tc.shape
    atoms = rows // BW
    wide = cols // ncols
    blocks = wide // RW
    chips = ncols // CORES
    first = arrived is None

    def body(count_ref, ri_ref, mask_ref, x_ref, *refs):
        outs = refs[:1] if first else refs[1 : 1 + chips]
        held, hot = refs[-2:] if first else refs[-4:-2]
        made, both = (outs[0], None) if first else refs[-2:]
        row, col = lax.axis_index("row"), lax.axis_index("col")
        base = (row * ncols + col) * atoms
        hot[...] = jnp.zeros_like(hot)

        @loop(chips, unroll)
        def _(t):
            dest = col ^ (CORES * t + (1 if first else 0))

            @loop(blocks, unroll)
            def _(b):
                lanes = pl.ds(pl.multiple_of(dest * wide + b * RW, RW), RW)
                slot = iota((BW, RW), 0)
                for a in range(atoms):
                    limit = jnp.where(mask_ref[a, dest * blocks + b] > 0, count_ref[base + a], 0)
                    x = x_ref[pl.ds(a * BW, BW), lanes].astype(F32)
                    held[pl.ds(a * BW, BW), span(b, RW)] = jnp.where(slot < limit, x, 0.0).astype(BF16)

            pack_cols(ri_ref, dest * blocks, blocks, RW, packed, hot, unroll)
            made[t] = jnp.dot(held[...], hot[...], preferred_element_type=F32).astype(BF16)

        if not first:
            core = lax.rem(col, CORES)
            chip = (row * ncols + col - core) * atoms
            for t in range(chips):
                into = outs[t] if chip_rows == CORES * rows else both.at[t]
                into[pl.ds(pl.multiple_of(core * rows, rows), rows), :] = made[t]
                into[pl.ds(pl.multiple_of((1 - core) * rows, rows), rows), :] = refs[0][t]
            if chip_rows < CORES * rows:
                left = pack_rows(count_ref, chip, CORES * atoms, BW, chip_rows, unroll)
                for t in range(chips):
                    outs[t][...] = jnp.dot(left, both[t], preferred_element_type=F32).astype(BF16)

    shape = (chips, rows, packed)
    merged = jax.ShapeDtypeStruct((chip_rows, packed), BF16)
    out_shape = [jax.ShapeDtypeStruct(shape, BF16)] if first else [merged] * chips
    out_specs = [VMEM_SPEC] * len(out_shape)
    return pl.pallas_call(
        body,
        out_shape=out_shape,
        in_specs=[SMEM_SPEC, SMEM_SPEC, SMEM_SPEC] + [VMEM_SPEC] * (1 if first else 2),
        out_specs=out_specs,
        scratch_shapes=[pltpu.VMEM((rows, wide), BF16), pltpu.VMEM((wide, packed), BF16)]
        + ([] if first else [pltpu.VMEM(shape, BF16), pltpu.VMEM((chips, CORES * rows, packed), BF16)]),
        compiler_params=params(),
        cost_estimate=cost(rows * cols * packed, rows * cols + 3 * chips * rows * packed),
        name="pack_other_core" if first else "pack_own_core",
    )(basis_count, ri_count, block_mask, tc, *([] if first else [arrived]))


def pack_density(dens, mask, basis_count, lam_size, sum_size, unroll):
    rows, cols = dens.shape
    lam_atoms, sum_atoms = mask.shape
    steps = 1 if unroll else 4
    tile = rows // steps
    out_tile = lam_size // steps

    def body(count_ref, mask_ref, x_ref, o_ref, upper_ref, lower_ref, hot, keep, mid):
        row, col = lax.axis_index("row"), lax.axis_index("col")
        first = iota((sum_atoms, cols), 0) * BW
        lane = iota((sum_atoms, cols), 1)
        of_atom = ones_where((lane >= first) & (lane < first + BW))
        keep[...] = lax.dot_general(
            ones_where(mask_ref[...] > 0), of_atom, (((0,), (0,)), ((), ())), preferred_element_type=F32
        ).astype(BF16)
        pack_cols(count_ref, col * sum_atoms, sum_atoms, BW, sum_size, hot, unroll)

        @loop(steps, unroll)
        def _(i):
            at = span(i, tile)
            shape = (tile, lam_atoms)
            first = iota(shape, 1) * BW - i * tile
            atom = ones_where((iota(shape, 0) >= first) & (iota(shape, 0) < first + BW))
            kept = jnp.dot(atom, keep[...], preferred_element_type=F32)
            x = jnp.where(kept > 0.5, x_ref[at, :].astype(F32), 0.0).astype(BF16)
            mid[at, :] = jnp.dot(x, hot[...], preferred_element_type=F32).astype(BF16)

        place = place_row(count_ref, row * lam_atoms, lam_atoms, BW, unroll)

        @loop(steps, unroll)
        def _(i):
            at = span(i, out_tile)
            left = ones_where(iota((out_tile, rows), 0) + i * out_tile == place)
            o_ref[at, :] = jnp.dot(left, mid[...], preferred_element_type=F32).astype(BF16)

        upper_ref[...] = o_ref[pl.ds(0, TILE), :]
        lower_ref[...] = o_ref[pl.ds(TILE, lam_size - TILE), :]

    return pl.pallas_call(
        body,
        out_shape=[jax.ShapeDtypeStruct((n, sum_size), BF16) for n in (lam_size, TILE, lam_size - TILE)],
        in_specs=[SMEM_SPEC, VMEM_SPEC, VMEM_SPEC],
        out_specs=[VMEM_SPEC] * 3,
        scratch_shapes=[
            pltpu.VMEM((cols, sum_size), BF16),
            pltpu.VMEM((lam_atoms, cols), BF16),
            pltpu.VMEM((rows, sum_size), BF16),
        ],
        compiler_params=params(),
        cost_estimate=cost(2 * rows * sum_size * (cols + lam_size), 2 * rows * cols),
        name="pack_density",
    )(basis_count, mask.T, dens)


def pack_part(pieces, basis_count, first, ncols, chip_atoms, size, unroll):
    rows, cols = pieces[0].shape
    per = len(pieces)

    def body(count_ref, *refs):
        blocks, o_ref, full = refs[:per], refs[per], refs[per + 1]
        row, chip = lax.axis_index("row"), lax.axis_index("col") // CORES
        for i in range(per):
            at = lax.rem(chip ^ (first + i), per) * rows
            full[pl.ds(pl.multiple_of(at, rows), rows), :] = blocks[i][...]
        chips = (row * (ncols // CORES) + (chip ^ first)) // per * per
        if rows == chip_atoms * BW:
            hot = pack_rows(count_ref, chips * chip_atoms, per * chip_atoms, BW, size, unroll)
        else:
            hot = pack_rows(Sums(count_ref, chip_atoms), chips, per, rows, size, unroll)
        o_ref[...] = jnp.dot(hot, full[...], preferred_element_type=F32).astype(BF16)

    return pl.pallas_call(
        body,
        out_shape=jax.ShapeDtypeStruct((size, cols), BF16),
        in_specs=[SMEM_SPEC] + [VMEM_SPEC] * per,
        out_specs=VMEM_SPEC,
        scratch_shapes=[pltpu.VMEM((per * rows, cols), BF16)],
        compiler_params=params(),
        cost_estimate=cost((2 + 40 * first) * size * per * rows * cols, 2 * cols * (per * rows + size)),
        name="pack_part",
    )(basis_count, *pieces)


def exchange(x, axis, bit):
    peers = lax.axis_size(axis)
    return lax.ppermute(x, axis, [(i, i ^ bit) for i in range(peers)])


def after(x, *others):
    return lax.optimization_barrier((x, *others))[0]


def double(own, axis, bits):
    have = {0: own}
    for bit in bits:
        for far in sorted(have):
            have[far | bit] = exchange(have[far], axis, bit)
    return have


def add_parts(total, unroll, d_refs, sums, before=None):
    lam, cols = total.shape

    @loop(lam // TILE, unroll)
    def _(j):
        out = span(j, TILE)
        x = None if before is None else before[out, :]
        for chunks, part in zip(d_refs, sums):
            if len(chunks) == 1:
                d = chunks[0][out, :]
            elif isinstance(j, int):
                d = chunks[0][...] if j == 0 else chunks[1][span(j - 1, TILE), :]
            else:
                d = chunks[1][span(jnp.maximum(j - 1, 0), TILE), :].astype(F32)
                d = jnp.where(j == 0, chunks[0][...].astype(F32), d).astype(BF16)
            y = jnp.dot(d, part(), preferred_element_type=F32)
            x = y if x is None else x + y
        total[out, :] = x


def split_refs(dens, refs):
    lists, at = [], 0
    for chunks in dens.values():
        lists.append(refs[at : at + len(chunks)])
        at += len(chunks)
    return lists, refs[at:]


def flat(dens):
    return [chunk for chunks in dens.values() for chunk in chunks]


def ways_back(basis_count, ri_count, nrows, ncols, rows, wide, lam, cols, unroll):
    lam_atoms, blocks = rows // BW, wide // RW

    def body(count_ref, ri_ref, lam_hot, col_hot):
        row, col = lax.axis_index("row"), lax.axis_index("col")
        pack_cols(count_ref, row * lam_atoms, lam_atoms, BW, lam, lam_hot, unroll)
        place = place_row(ri_ref, col * blocks, blocks, RW, unroll)

        @loop(cols // RW, unroll)
        def _(i):
            col_hot[span(i, RW), :] = ones_where(iota((RW, wide), 0) + i * RW == place)

    return pl.pallas_call(
        body,
        out_shape=[jax.ShapeDtypeStruct((rows, lam), BF16), jax.ShapeDtypeStruct((cols, wide), BF16)],
        in_specs=[SMEM_SPEC, SMEM_SPEC],
        out_specs=[VMEM_SPEC] * 2,
        compiler_params=params(16 * 1024 * 1024),
        name="ways_back",
    )(basis_count, ri_count)


def contract_near(dens, integrals, ncols, unroll):
    lam, depth = dens[0][0].shape
    groups, nrows = len(integrals), len(integrals[0])
    sums = [integrals[g][far] for far in range(nrows) for g in range(groups)]
    cols = sums[0].shape[1]
    n, parts = len(dens), len(sums)

    def body(*refs):
        d_refs, refs = split_refs(dens, refs)
        s_refs, refs = refs[:parts], refs[parts:]
        total, s_rest, s_all, s_sem, r_sem = refs
        row, col = lax.axis_index("row"), lax.axis_index("col")
        for j, ref in enumerate(s_refs):
            part = (row ^ (j // groups)) * groups + (col // (ncols // groups) ^ (j % groups))
            pltpu.make_async_copy(ref, s_all.at[part], s_sem.at[part]).start()

        @pl.loop(0, parts)
        def _(i):
            pltpu.make_async_copy(s_all.at[i], s_all.at[i], s_sem.at[i]).wait()

        rest = [
            pltpu.make_async_copy(s_all.at[col ^ far], s_rest.at[far - n], r_sem.at[far - n])
            for far in range(n, parts)
        ]
        for copy in rest:
            copy.start()
        add_parts(total, unroll, d_refs, [lambda far=far: s_all[col ^ far] for far in range(n)])
        for copy in rest:
            copy.wait()

    need = 2 * (n * depth * lam + 2 * parts * depth * cols + 4 * lam * cols)
    return pl.pallas_call(
        body,
        out_shape=[
            jax.ShapeDtypeStruct((lam, cols), F32),
            jax.ShapeDtypeStruct((parts - n, depth, cols), BF16),
        ],
        in_specs=[VMEM_SPEC] * n + [ANY_SPEC] * parts,
        out_specs=[VMEM_SPEC] * 2,
        scratch_shapes=[
            pltpu.VMEM((parts, depth, cols), BF16),
            pltpu.SemaphoreType.DMA((parts,)),
            pltpu.SemaphoreType.DMA((parts - n,)),
        ],
        compiler_params=params(need + 4 * 1024 * 1024),
        cost_estimate=cost(2 * n * depth * lam * cols, 2 * n * depth * (lam + cols)),
        name="contract_near",
    )(*flat(dens), *sums)


def contract_far(dens, first, total, sums, unroll):
    (lam, cols), depth = total.shape, sums.shape[1]
    n = len(dens)

    def body(before, s_ref, *refs):
        d_refs, (o_ref,) = split_refs(dens, refs)
        add_parts(o_ref, unroll, d_refs, [lambda i=i: s_ref[first + i] for i in range(n)], before)

    need = 2 * (n * depth * lam + sums.size + 4 * lam * cols)
    return pl.pallas_call(
        body,
        out_shape=jax.ShapeDtypeStruct((lam, cols), F32),
        in_specs=[VMEM_SPEC] * (2 + len(flat(dens))),
        out_specs=VMEM_SPEC,
        compiler_params=params(need + 4 * 1024 * 1024),
        cost_estimate=cost(2 * n * depth * lam * cols, 2 * n * depth * (lam + cols)),
        name="contract_far",
    )(total, sums, *flat(dens))


def contract_last(dens, first, total, sums, lam_hot, col_hot, unroll):
    (rows, lam), (cols, wide) = lam_hot.shape, col_hot.shape
    depth = sums.shape[1]
    n = len(dens)
    half = lam // 2

    def body(before, s_ref, lam_hot, col_hot, *refs):
        d_refs, (o_ref, total, packed) = split_refs(dens, refs)
        add_parts(total, unroll, d_refs, [lambda i=i: s_ref[first + i] for i in range(n)], before)

        @loop(2, unroll)
        def _(j):
            x = total[span(j, half), :].astype(BF16)
            packed[span(j, half), :] = jnp.dot(x, col_hot[...], preferred_element_type=F32).astype(BF16)

        @loop(4, unroll)
        def _(j):
            out = span(j, rows // 4)
            o_ref[out, :] = jnp.dot(lam_hot[out, :], packed[...], preferred_element_type=F32).astype(BF16)

    need = 2 * (n * depth * lam + sums.size + 4 * lam * cols + rows * lam + cols * wide + (lam + rows) * wide)
    return pl.pallas_call(
        body,
        out_shape=jax.ShapeDtypeStruct((rows, wide), BF16),
        in_specs=[VMEM_SPEC] * (4 + len(flat(dens))),
        out_specs=VMEM_SPEC,
        scratch_shapes=[pltpu.VMEM((lam, cols), F32), pltpu.VMEM((lam, wide), BF16)],
        compiler_params=params(need + 4 * 1024 * 1024),
        cost_estimate=cost(2 * n * depth * lam * cols, 2 * n * depth * (lam + cols)),
        name="contract_last",
    )(total, sums, lam_hot, col_hot, *flat(dens))


def program(lam_size, sum_size, col_size, chip_size, common):
    unroll = common

    def run(three_center, density, block_mask, density_mask, basis_count, ri_count):
        ncols = lax.axis_size("col")
        nrows = lax.axis_size("row")
        chips = ncols // CORES
        rows, depth = density.shape
        wide = three_center.shape[1] // ncols
        row_bits = [1 << b for b in range(nrows.bit_length() - 1)]
        chip_bits = [CORES << b for b in range(chips.bit_length() - 1)][::-1]
        far_bit, near_bits = chip_bits[0], chip_bits[1:]

        counts = (block_mask, basis_count, ri_count, ncols, col_size, unroll, chip_size)
        other = exchange(pack_integrals(three_center, *counts)[0], "col", 1)
        own, upper, lower = pack_density(density, density_mask, basis_count, lam_size, sum_size, unroll)
        lines = [{0: upper, far_bit: exchange(upper, "col", far_bit)}, {0: lower}]
        near = {0: own, 1: exchange(own, "col", 1)}
        pieces = pack_integrals(three_center, *counts, after(other, own))
        early = lines[0][far_bit]
        got = [pieces[0]] + [exchange(pieces[t], "col", CORES * t) for t in range(1, chips)]
        chip_rows = CORES * three_center.shape[0]
        per = depth // chip_rows
        lam_hot, col_hot = ways_back(
            basis_count, ri_count, nrows, ncols, rows, wide, lam_size, col_size, unroll
        )
        parts, groups, orders = [], [], []
        for g in range(chips // per):
            arrived = got[g * per : (g + 1) * per]
            if g == 0:
                arrived = [after(arrived[0], near[1])] + arrived[1:]
            elif g == 1:
                arrived = [after(arrived[0], lam_hot)] + arrived[1:]
            part = pack_part(arrived, basis_count, g * per, ncols, chip_rows // BW, sum_size, unroll)
            if g == 0:
                near.update(double(after(own, part), "col", near_bits))
                steps = [near[far] for far in near if far > 1]
            else:
                part = after(part, *[groups[0][bit] for bit in row_bits])
            parts.append(part)
            orders.append(row_bits if g % 2 == 0 else row_bits[::-1])
            groups.append({0: part})
            for bit in orders[g]:
                groups[g][bit] = exchange(part, "row", bit)
        step = groups[-1][orders[-1][0]]
        across = exchange(after(early, parts[-1]), "col", 1)
        forward = double(after(early, across, *steps), "col", near_bits)
        lines[0].update({far_bit | far: block for far, block in forward.items() if far > 0})
        lines[1][far_bit] = exchange(after(lower, parts[-1]), "col", far_bit)
        for far in [far for far in near if far > 1]:
            near[far | 1] = exchange(after(near[far], across), "col", 1)
        for g, have in enumerate(groups):
            done = [0, orders[g][0]]
            for bit in orders[g][1:]:
                for far in done[1:]:
                    block = have[far] if g == len(groups) - 1 else after(have[far], *[groups[-1][bit] for bit in row_bits])
                    have[far | bit] = exchange(block, "row", bit)
                done += [far | bit for far in done]
        first = {far: [near[far]] for far in sorted(near)}
        total, sums = contract_near(first, groups, ncols, unroll)
        block = after(lines[1][far_bit], lines[0][ncols - CORES])
        for away, block in double(block, "col", near_bits).items():
            lines[1][far_bit | away] = block
        middle = {}
        for far in range(far_bit, ncols - CORES, CORES):
            middle[far] = [line[far] for line in lines]
            middle[far | 1] = [across if line[far] is early else exchange(line[far], "col", 1) for line in lines]
        total = contract_far(middle, 0, total, sums, unroll)
        ends = [line[ncols - CORES] for line in lines]
        last = {ncols - CORES: ends}
        last[ncols - 1] = [exchange(ends[0], "col", 1), exchange(after(ends[1], total), "col", 1)]
        return contract_last(last, len(middle), total, sums, lam_hot, col_hot, unroll)

    return run


def choose(here, yes, no):
    return lambda *args: lax.cond(here, yes, no, *args)


def shards(three_center, density, block_mask, density_mask, basis_count, ri_count):
    ncols = lax.axis_size("col")
    nrows = lax.axis_size("row")
    rows, depth = density.shape
    wide = three_center.shape[1] // ncols
    chip = CORES * three_center.shape[0]
    levels = (
        (rows * 3 // 4, depth * 3 // 4, wide * 5 // 6, chip * 7 // 8),
        (rows * 3 // 4, depth, wide * 5 // 6, chip),
        (rows * 3 // 4, depth, wide, chip),
        (rows, depth, wide, chip),
    )
    level = first_fit(basis_count, ri_count, (nrows, ncols, ncols, nrows * ncols // CORES), levels)
    args = (three_center, density, block_mask, density_mask, basis_count, ri_count)
    run = program(*levels[-1], False)
    for n in reversed(range(len(levels) - 1)):
        run = choose(level[0] == n, program(*levels[n], n == 0), run)
    return run(*args)


def solution(mesh):
    in_specs = (
        P(("row", "col"), None),
        P("row", "col"),
        P(("row", "col"), None),
        P("row", "col"),
        P(),
        P(),
    )
    return jax.shard_map(
        shards, mesh=mesh, in_specs=in_specs, out_specs=P("row", "col"), check_vma=False
    )
```
